512 devices in a mesh: views: 8 (over y), tiles: 64 (over x, z, core).
Axes of the slice: x: 4, y: 8, z: 8, core: 2. Of those that a mesh axis runs over, the one named last changes fastest.
Arguments:
- linear_point: float32 [59, 32768], P(None, 'tiles'), may hold values from -6 to 6
- right_side: float32 [59, 32768], P(None, 'tiles'), may hold values from -75 to 75
- damping: float32 [59, 32768], P(None, 'tiles'), may hold values from 0.2 to 2
- projection: float32 [8, 59, 16], P('views'), may hold values from -0.75 to 0.75
- pixel_basis: float32 [8, 64, 12, 128], P('views', 'tiles'), may hold values from -1.8 to 1.8
- pixel_weight: float32 [8, 64, 128], P('views', 'tiles'), may hold values from 50 to 500
- depth_order: int32 [8, 64, 512], P('views', 'tiles'), may hold values from 0 to 511, each once within a row
- tile_dest: int32 [8, 4096, 1], P('views', 'tiles'), may hold values from 0 to 63; in each aligned block of 64 rows (0 to 63, 64 to 127, ..., all dimensions but the last counted through in order) at most 2 rows name the same one
- block_depth: int32 [8, 4096], P('views', 'tiles'), may hold values from 0 to 4095, each once within a row
Outputs:
- solution: float32 [59, 32768], P(None, 'tiles')
- residual: float32 [59, 32768], P(None, 'tiles')
The draws below stay inside these ranges and needn't reach their ends.
Inputs may be any that keep to these rules, and one draw needn't show every extreme that they name: `tile_dest`: each block of one owner in one view names one tile; no tile is named by more than 2 blocks of one owner in one view, a bound that the blocks of some owner reach; every tile is named by some block of every view. `depth_order`: for each view and owner, a permutation of the owner's local Gaussian numbers. `block_depth`: for each view, a permutation of the block numbers.
All inputs are finite; a program needn't handle non-finite values.
Results may differ from the reference program's by a relative error of at most 0.007.
Values sent between devices are 32-bit elements; how exact they have to be, the bound alone decides.
No kernel may reach another device: no remote copies, remote signals or barrier semaphores. Data moves between devices by JAX's collectives and lax.ppermute only.
A program may use at most 64 MiB of HBM per device.

```python
import math
import jax
import jax.numpy as jnp
import numpy as np
from jax import lax

PARAMS = 59
FEAT = 16
PIX = 128
ROWS = 8
ITERS = 2
BLK_DEV = 64
G_DEV = 512
VIEWS = 8
TILE_COUNT = 64
CAP = 2
GAUSS = 32768
BLOCKS = 4096


def draw_right_side(key, part):
    key = jax.random.fold_in(key, 11)
    key_base, key_cols, key_rows = jax.random.split(key, 3)
    base = jnp.clip(jax.random.normal(key_base, (PARAMS, GAUSS), jnp.float32), -4.0, 4.0)
    col_scale = jnp.exp(jax.random.uniform(key_cols, (1, GAUSS), jnp.float32) * math.log(10.0))
    row_scale = jnp.exp(jax.random.uniform(key_rows, (PARAMS, 1), jnp.float32) * math.log(3.0))
    trend = jnp.exp(jnp.arange(GAUSS, dtype=jnp.float32)[None, :] * (math.log(3.0) / GAUSS))
    return (base * col_scale * row_scale * trend / 6.0).astype(jnp.float32)


def block_levels(stream_key, dims, shards, least, largest):
    def one(position, blocks):
        steps = jax.random.uniform(jax.random.fold_in(jax.random.fold_in(stream_key, 6), position), (blocks,), jnp.float32, least / len(shards), largest / len(shards))
        return jnp.repeat(jnp.exp(steps), dims[position] // blocks).reshape((-1,) + (1,) * (len(dims) - position - 1))

    loudness = one(*shards[0])
    for cut in shards[1:]:
        loudness = loudness * one(*cut)
    return loudness


def routed_block(key, own, number, rows, number_of, top, limit, slope):
    order = jax.random.permutation(key, number_of)
    packed, ordinary = shares(number_of, rows * top, limit, slope, True), shares(number_of, rows * top, limit, slope, False)
    places = jnp.arange(number_of)

    def named(lengths, rotation):
        used = int((lengths > 0).sum())
        fixed = max(1, used // 4)
        passed = fixed + (places - fixed + rotation * (used - fixed)) % max(1, number_of - fixed)
        return jnp.zeros((number_of,), jnp.int32).at[order[jnp.where(places < fixed, places, passed)]].set(jnp.asarray(lengths, jnp.int32))

    lengths = jnp.where(number % 4 == 0, named(packed, number // 4), named(ordinary, number - number // 4 - 1))
    mixed = jax.random.permutation(jax.random.fold_in(own, 3), number_of)
    giver, taker = mixed[0:number_of // 2 * 2:2], mixed[1:number_of // 2 * 2:2]
    room = jnp.minimum(lengths[giver] - 1, limit - lengths[taker]) // 2
    room = jnp.where((giver == order[0]) | (taker == order[0]) | (lengths[taker] == 0), 0, jnp.maximum(room, 0))
    passed = jax.random.randint(jax.random.fold_in(own, 4), (number_of // 2,), 0, 1 << 20) % (room + 1)
    lengths = lengths.at[giver].add(-passed).at[taker].add(passed)
    items = jnp.searchsorted(jnp.cumsum(lengths), jnp.arange(rows * top), side="right").astype(jnp.int32)
    table = items.reshape(top, rows).T
    table = table[jax.random.permutation(jax.random.fold_in(own, 1), rows)]
    rotation = jax.random.randint(jax.random.fold_in(own, 2), (rows, 1), 0, top)
    return jnp.take_along_axis(table, (jnp.arange(top)[None, :] + rotation) % top, axis=1)


def shares(count, total, reach, skew, full):
    loads = [(1 << 20) // math.isqrt(grade ** skew) + 1 for grade in range(1, count + 1)]
    largest = reach if full else min(reach, max(-(-total // count), total * loads[0] // sum(loads)))
    least = 1 if total - largest >= count - 1 else 0
    counts, rest = [largest] + [least] * (count - 1), total - largest - least * (count - 1)
    while rest > 0:
        free = [i for i in range(1, count) if counts[i] < largest] or [i for i in range(1, count) if counts[i] < reach]
        mass, budget = sum([loads[i] for i in free]), rest
        for i in free:
            more = min(reach - counts[i], max(1, budget * loads[i] // mass), rest)
            counts[i] = counts[i] + more
            rest = rest - more
    return np.array(counts)


def bell_draw(own_key, extent, scale, reach, shards=(), kind=jnp.bfloat16):
    level = block_levels(own_key, extent, shards, -0.22, 0.18) if shards else 1.0
    result = jax.random.normal(own_key, extent, jnp.float32) * scale * level
    return jnp.minimum(jnp.maximum(result, -reach), reach).astype(kind)


def setup_inputs(seed: int = 0) -> dict:
    key_of = jax.random.split(jax.random.key(seed), 10)
    linear_point = bell_draw(key_of[0], (PARAMS, GAUSS), 1.0, 6.0, ((1, 64),), jnp.float32)
    right_side = draw_right_side(jax.random.fold_in(key_of[9], 71), 0)
    damping = jnp.clip(jnp.exp(math.log(2.0) - 2.3025851 * jax.random.uniform(key_of[2], (PARAMS, GAUSS), jnp.float32) ** block_levels(key_of[2], (PARAMS, GAUSS), ((1, 64),), -0.2, 0.2)), 0.2, 2.0)
    projection = bell_draw(key_of[3], (VIEWS, PARAMS, FEAT), PARAMS ** -0.5, 0.75, ((0, 8),), jnp.float32)
    pixel_basis = bell_draw(key_of[4], (VIEWS, TILE_COUNT, FEAT - 4, PIX), 0.3, 1.8, ((0, 8), (1, 64)), jnp.float32)
    pixel_weight = jnp.clip(jnp.exp(math.log(500.0) - 2.3025851 * jax.random.uniform(key_of[5], (VIEWS, TILE_COUNT, PIX), jnp.float32) ** block_levels(key_of[5], (VIEWS, TILE_COUNT, PIX), ((0, 8), (1, 64)), -0.2, 0.2)), 50.0, 500.0)
    depth_order = jax.vmap(lambda own: jax.random.permutation(own, G_DEV))(jax.random.split(key_of[6], VIEWS * TILE_COUNT)).reshape((VIEWS, TILE_COUNT, G_DEV)).astype(jnp.int32)
    tile_dest_keys = jax.random.split(jax.random.fold_in(key_of[7], 1), VIEWS * BLOCKS // BLK_DEV)
    tile_dest_turns = jax.random.permutation(jax.random.fold_in(key_of[7], 3), VIEWS * BLOCKS // BLK_DEV)
    tile_dest = jax.vmap(lambda own, number: routed_block(jax.random.fold_in(key_of[7], 2), own, number, BLK_DEV, TILE_COUNT, 1, CAP, 1))(tile_dest_keys, tile_dest_turns).reshape((VIEWS, BLOCKS, 1))
    block_depth = jax.vmap(lambda own: jax.random.permutation(own, BLOCKS))(jax.random.split(key_of[8], VIEWS)).reshape((VIEWS, BLOCKS)).astype(jnp.int32)
    return {"linear_point": linear_point, "right_side": right_side, "damping": damping, "projection": projection, "pixel_basis": pixel_basis, "pixel_weight": pixel_weight, "depth_order": depth_order, "tile_dest": tile_dest, "block_depth": block_depth}


PRECISE = lax.Precision.HIGHEST
OFFSET = 6.0

def view_images(params, view_proj, view_basis, view_order, view_dest, view_depth):
    owners = jnp.arange(TILE_COUNT, dtype=jnp.int32)[:, None] * G_DEV
    index = (owners + view_order).reshape(-1).astype(jnp.int32)
    picked = jnp.take(params, index, axis=1).reshape(PARAMS, BLOCKS, ROWS)
    blocks = jnp.einsum('kf,kbr->bfr', view_proj, picked, precision=PRECISE)
    basis_rows = jnp.take(view_basis, view_dest, axis=0)
    logits = blocks[:, 0, :, None] - OFFSET + jnp.einsum('bkr,bkp->brp', blocks[:, 4:, :], basis_rows, precision=PRECISE)
    alphas = jax.nn.sigmoid(logits)
    log_clear = -jax.nn.softplus(logits)
    before = jnp.cumsum(log_clear, axis=1) - log_clear
    colors = jnp.einsum('bcr,brp->bcp', blocks[:, 1:4, :], alphas * jnp.exp(before), precision=PRECISE)
    through = lax.optimization_barrier(jnp.sum(log_clear, axis=1))
    shared = view_dest[None, :] == view_dest[:, None]
    earlier = view_depth[None, :] < view_depth[:, None]
    ahead = jnp.dot((shared & earlier).astype(jnp.float32), through, precision=PRECISE)
    weighted = jnp.exp(ahead)[:, None, :] * colors
    return jax.ops.segment_sum(weighted, view_dest, TILE_COUNT)

def normal_views(direction, linear_point, projection, pixel_basis, pixel_weight, depth_order, tile_dest, block_depth):

    def one_view(view_index):

        def render(params):
            return view_images(params, projection[view_index], pixel_basis[view_index], depth_order[view_index], tile_dest[view_index, :, 0], block_depth[view_index])
        tangent = jax.jvp(render, (linear_point,), (direction,))[1]
        unused_out, pull = jax.vjp(render, linear_point)
        return pull(tangent * pixel_weight[view_index][:, None, :])[0]
    terms = lax.map(one_view, jnp.arange(VIEWS, dtype=jnp.int32))
    return lax.optimization_barrier(jnp.sum(terms, axis=0))

def reference(linear_point, right_side, damping, projection, pixel_basis, pixel_weight, depth_order, tile_dest, block_depth):
    solution = jnp.zeros_like(right_side)
    residual = right_side
    direction = right_side
    norm_now = jnp.sum(residual * residual)
    for iteration in range(ITERS):
        product = normal_views(direction, linear_point, projection, pixel_basis, pixel_weight, depth_order, tile_dest, block_depth) + damping * direction
        step_size = norm_now / jnp.sum(direction * product)
        solution = solution + step_size * direction
        residual = residual - step_size * product
        norm_next = jnp.sum(residual * residual)
        direction = residual + norm_next / norm_now * direction
        norm_now = norm_next
    return (solution, residual)
```

```python
import jax
import jax.numpy as jnp
from jax import lax
from jax.experimental import pallas as pl
from jax.experimental.pallas import tpu as pltpu
from jax.sharding import PartitionSpec as P

OFFSET = 6.0
PARAMS = 59
FEAT = 16
ROWS = 8
CAP = 2
PIECES = CAP * ROWS
OWNERS = 64
GAUSS = 512
PIX = 128
F32 = jnp.float32
BF16 = jnp.bfloat16

NN = (((1,), (0,)), ((), ()))
NT = (((1,), (1,)), ((), ()))
TN = (((0,), (0,)), ((), ()))


def iota(shape, axis):
    return lax.broadcasted_iota(jnp.int32, shape, axis)


def mm(a, b, dims=NN):
    return lax.dot_general(a, b, dims, preferred_element_type=F32)


def split(x):
    high = x.astype(BF16)
    low = (x - high.astype(F32)).astype(BF16)
    return high, low


def split3(x):
    high = x.astype(BF16)
    rest = x - high.astype(F32)
    mid = rest.astype(BF16)
    low = (rest - mid.astype(F32)).astype(BF16)
    return high, mid, low


def mm3(a, b, dims=NN):
    ah, al = split(a)
    bh, bl = split(b)
    return mm(ah, bh, dims) + mm(al, bh, dims) + mm(ah, bl, dims)


def total(x):
    return jnp.sum(jnp.sum(x, axis=1, keepdims=True), axis=0, keepdims=True)


def lanes(values, rows):
    lane = iota((rows, PIX), 1)
    out = jnp.zeros((rows, PIX), F32)
    for i, value in enumerate(values):
        out = jnp.where(lane == i, value, out)
    return out


def to_message(feats, select):
    stacked = jnp.concatenate(feats, axis=0)
    high, low = split(stacked)
    slots = mm(high, select, NT) + mm(low, select, NT)
    pieces = [slots[:, i * OWNERS : (i + 1) * OWNERS] for i in range(PIECES)]
    return jnp.concatenate(pieces, axis=0).T


def by_column(message, width):
    turned = message.T
    return jnp.concatenate([turned[i * width : (i + 1) * width] for i in range(PIECES)], axis=1)


def begin(point, right, damp, proj, order, dest, depth):
    blocks = dest.shape[1]
    mine = iota((OWNERS, blocks), 0) == dest
    mine_f = jnp.where(mine, 1.0, 0.0)
    earlier = jnp.where(iota((blocks, blocks), 0) < iota((blocks, blocks), 1), 1.0, 0.0)
    count = mm(mine_f.astype(BF16), earlier.astype(BF16))
    owns = [jnp.where(mine & (count == float(s)), 1.0, 0.0) for s in range(CAP)]
    depth_f = depth.astype(F32) + 1.0
    marks = [jnp.sum(own * depth_f, axis=1, keepdims=True) for own in owns]
    own_all = jnp.concatenate(owns, axis=0).astype(BF16)
    here = iota((blocks, GAUSS), 1) // ROWS == iota((blocks, GAUSS), 0)
    number = jnp.where(here, order + 1, 0)
    parts = jnp.concatenate(
        [(number // 16).astype(F32), (number % 16).astype(F32)], axis=0
    ).astype(BF16)
    pick = jnp.where(iota((GAUSS, PIX), 0) % ROWS == iota((GAUSS, PIX), 1), 1.0, 0.0).astype(BF16)
    table = mm(parts, pick).astype(BF16)
    ids = mm(own_all, table[:blocks]) * 16.0 + mm(own_all, table[blocks:])
    columns = (iota((OWNERS, GAUSS), 1) + 1).astype(F32)
    rows = []
    for s in range(CAP):
        for r in range(ROWS):
            chosen = ids[s * OWNERS : (s + 1) * OWNERS, r : r + 1] == columns
            rows.append(jnp.where(chosen, 1.0, 0.0).astype(BF16))
    select = jnp.concatenate(rows, axis=0)
    feats = mm3(proj, jnp.concatenate([point, right], axis=1), TN)
    message = to_message([feats[:, :GAUSS], feats[:, GAUSS:]], select)
    tail = lanes(marks + [total(right * right), total(damp * right * right)], OWNERS)
    return jnp.concatenate([message, tail], axis=1), select


def order_masks(marks):
    side = CAP * OWNERS
    by_row = jnp.broadcast_to(marks, (side, side))
    diagonal = iota((side, side), 0) == iota((side, side), 1)
    by_lane = jnp.sum(jnp.where(diagonal, by_row, 0.0), axis=0, keepdims=True)
    front = jnp.where((by_lane < by_row) & (by_lane > 0.0), 1.0, 0.0)
    behind = jnp.where((by_row < by_lane) & (by_row > 0.0), 1.0, 0.0)
    return front.astype(BF16), behind.astype(BF16)


def ordered_sum(mask, value):
    high, low = split(value)
    return mm(mask, high) + mm(mask, low)


def image_change(prim_cols, tang_cols, weights, slopes):
    wh, wl = split(weights)
    vh, vl = split(slopes)
    th, tl = split(tang_cols)
    ph, plow = split(prim_cols)
    change = mm(th, wh) + mm(tl, wh) + mm(th, wl) + mm(ph, vh) + mm(plow, vh) + mm(ph, vl)
    row = iota((FEAT, PIX), 0)
    return jnp.where((row >= 1) & (row < 4), change, 0.0)


def pull_back(prim_cols, basis, colour, alphas, clears, weights, behind):
    shade = mm3(prim_cols, colour, TN)
    pulls = [weights[i] * shade[i * OWNERS : (i + 1) * OWNERS] for i in range(PIECES)]
    sums = []
    for s in range(CAP):
        acc = pulls[s * ROWS]
        for r in range(1, ROWS):
            acc = acc + pulls[s * ROWS + r]
        sums.append(acc)
    through = ordered_sum(behind, jnp.concatenate(sums, axis=0))
    logits = [None] * PIECES
    for s in range(CAP):
        acc = through[s * OWNERS : (s + 1) * OWNERS]
        for r in reversed(range(ROWS)):
            i = s * ROWS + r
            logits[i] = clears[i] * pulls[i] - alphas[i] * acc
            acc = acc + pulls[i]
    both = jnp.concatenate(
        [jnp.concatenate(logits, axis=0), jnp.concatenate(weights, axis=0)], axis=1
    )
    back = mm3(both, jnp.concatenate([basis, colour], axis=1), NT)
    return back


def as_rows(back):
    return jnp.concatenate([back[i * OWNERS : (i + 1) * OWNERS] for i in range(PIECES)], axis=1)


def slope_terms(tangents, alphas, clears):
    slopes = []
    sums = []
    for s in range(CAP):
        acc = jnp.zeros((OWNERS, PIX), F32)
        for r in range(ROWS):
            i = s * ROWS + r
            slopes.append(clears[i] * tangents[i] + acc)
            acc = acc - alphas[i] * tangents[i]
        sums.append(acc)
    return slopes, jnp.concatenate(sums, axis=0)


def render_first(message, basis12, pixel_weight):
    width = 2 * FEAT
    columns = by_column(message[:, : PIECES * width], width)
    tail = message[:, PIECES * width :]
    totals = jnp.sum(tail, axis=0, keepdims=True)
    basis = full_basis(basis12)
    both = jnp.zeros((FEAT, PIX), F32)
    wide = jnp.concatenate(
        [jnp.concatenate([basis, both], axis=1), jnp.concatenate([both, basis], axis=1)], axis=0
    )
    logits_tangents = mm3(columns, wide, TN)
    front, behind = order_masks(jnp.concatenate([tail[:, 0:1], tail[:, 1:2]], axis=0))
    alphas, clears, plain, tangents, lengths = [], [], [], [], []
    for s in range(CAP):
        open_now = None
        length = None
        for r in range(ROWS):
            i = s * ROWS + r
            block = logits_tangents[i * OWNERS : (i + 1) * OWNERS]
            z = block[:, :PIX] - OFFSET
            tangents.append(block[:, PIX:])
            small = jnp.exp(-jnp.abs(z))
            grown = 1.0 + small
            part = 1.0 / grown
            rest = small * part
            alpha = jnp.where(z >= 0.0, part, rest)
            clear = jnp.where(z >= 0.0, rest, part)
            log_clear = -(jnp.maximum(z, 0.0) + jnp.log(grown))
            alphas.append(alpha)
            clears.append(clear)
            plain.append(alpha if open_now is None else alpha * open_now)
            open_now = clear if open_now is None else open_now * clear
            length = log_clear if length is None else length + log_clear
        lengths.append(length)
    high, mid, low = split3(jnp.concatenate(lengths, axis=0))
    ahead = jnp.exp(mm(front, high) + mm(front, mid) + mm(front, low))
    weights = [
        plain[i] * ahead[(i // ROWS) * OWNERS : (i // ROWS + 1) * OWNERS] for i in range(PIECES)
    ]
    slopes, sums = slope_terms(tangents, alphas, clears)
    ahead_tangent = ordered_sum(front, sums)
    slopes = [
        weights[i]
        * (slopes[i] + ahead_tangent[(i // ROWS) * OWNERS : (i // ROWS + 1) * OWNERS])
        for i in range(PIECES)
    ]
    prim_cols = columns[:FEAT]
    change = image_change(
        prim_cols,
        columns[FEAT:],
        jnp.concatenate(weights, axis=0),
        jnp.concatenate(slopes, axis=0),
    )
    colour = change * pixel_weight
    back = pull_back(prim_cols, basis, colour, alphas, clears, weights, behind)
    out = jnp.concatenate(
        [as_rows(back), lanes([total(colour * change)], OWNERS)], axis=1
    )
    return (
        out,
        jnp.concatenate(alphas, axis=0),
        jnp.concatenate(clears, axis=0),
        jnp.concatenate(weights, axis=0),
        prim_cols,
        front,
        behind,
        change,
        totals,
    )


def full_basis(basis12):
    first = jnp.where(iota((4, PIX), 0) == 0, 1.0, 0.0)
    return jnp.concatenate([first, basis12], axis=0)


def pieces_of(array):
    return [array[i * OWNERS : (i + 1) * OWNERS] for i in range(PIECES)]


def render_again(
    message, basis12, pixel_weight, alphas, clears, weights, prim_cols, front, behind, change0, totals0
):
    columns = by_column(message[:, : PIECES * FEAT], FEAT)
    totals = jnp.sum(message[:, PIECES * FEAT :], axis=0, keepdims=True)
    basis = full_basis(basis12)
    tangents = pieces_of(mm3(columns, basis, TN))
    alphas, clears, weight_list = pieces_of(alphas), pieces_of(clears), pieces_of(weights)
    slopes, sums = slope_terms(tangents, alphas, clears)
    ahead_tangent = ordered_sum(front, sums)
    slopes = [
        weight_list[i]
        * (slopes[i] + ahead_tangent[(i // ROWS) * OWNERS : (i // ROWS + 1) * OWNERS])
        for i in range(PIECES)
    ]
    ratio = totals[:, 0:1] / totals0[:, 2:3]
    change = (
        image_change(prim_cols, columns, weights, jnp.concatenate(slopes, axis=0))
        + ratio * change0
    )
    colour = change * pixel_weight
    back = pull_back(prim_cols, basis, colour, alphas, clears, weight_list, behind)
    out = jnp.concatenate([as_rows(back), lanes([total(colour * change)], OWNERS)], axis=1)
    return out, totals


def collect(message, select, proj):
    columns = by_column(message[:, : PIECES * FEAT], FEAT)
    high, low = split(columns)
    wide = mm(jnp.concatenate([high, low], axis=0), select)
    gathered = wide[:FEAT] + wide[FEAT:]
    tail = jnp.sum(message[:, PIECES * FEAT :], axis=0, keepdims=True)
    turned = jnp.concatenate(
        [proj.T, jnp.broadcast_to(tail[:, 0:1], (FEAT, PIX - PARAMS))], axis=1
    )
    return jnp.concatenate([gathered, turned], axis=1)


def product_of(message, views):
    rows = views * FEAT
    gathered = message[:, :, :GAUSS].reshape(rows, GAUSS)
    turned = message[:, :, GAUSS:].reshape(rows, PIX)
    product = mm3(turned, gathered, TN)[:PARAMS]
    energy = jnp.sum(turned, axis=0, keepdims=True)[:, PARAMS : PARAMS + 1] * (1.0 / FEAT)
    return product, energy


def step_first(message, right, damp, proj, select, totals0):
    product, energy = product_of(message, message.shape[0])
    product = product + damp * right
    step = totals0[:, 2:3] / (energy + totals0[:, 3:4])
    residual = right - step * product
    weighted = damp * residual
    feats = mm3(proj, residual, TN)
    tail = lanes(
        [total(residual * residual), total(weighted * residual), total(weighted * right)], OWNERS
    )
    out = jnp.concatenate([to_message([feats], select), tail], axis=1)
    return out, residual, step


def step_last(message, right, damp, residual, step, totals0, totals1):
    product, energy = product_of(message, message.shape[0])
    ratio = totals1[:, 0:1] / totals0[:, 2:3]
    direction = residual + ratio * right
    product = product + damp * direction
    damped = totals1[:, 1:2] + 2.0 * ratio * totals1[:, 2:3] + ratio * ratio * totals0[:, 3:4]
    step_now = totals1[:, 0:1] / (energy + damped)
    return step * right + step_now * direction, residual - step_now * product


def call(function, outs, *args):
    def kernel(*refs):
        results = function(*[ref[...] for ref in refs[: len(args)]])
        if len(outs) == 1:
            results = (results,) if not isinstance(results, tuple) else results
        for ref, result in zip(refs[len(args) :], results):
            ref[...] = result

    result = pl.pallas_call(
        kernel,
        out_shape=[jax.ShapeDtypeStruct(shape, dtype) for shape, dtype in outs],
        in_specs=[pl.BlockSpec(memory_space=pltpu.VMEM)] * len(args),
        out_specs=[pl.BlockSpec(memory_space=pltpu.VMEM)] * len(outs),
        compiler_params=pltpu.CompilerParams(vmem_limit_bytes=40 * 1024 * 1024),
        name=function.__name__,
    )(*args)
    return result


def body(
    linear_point,
    right_side,
    damping,
    projection,
    pixel_basis,
    pixel_weight,
    depth_order,
    tile_dest,
    block_depth,
):
    proj = projection[0]
    basis = pixel_basis[0, 0]
    weight = pixel_weight[0]
    dest = tile_dest.reshape(1, -1)
    views = lax.axis_size("views")
    rows = PIECES * OWNERS
    slots = CAP * OWNERS

    def over_tiles(message):
        return lax.all_to_all(message, "tiles", split_axis=0, concat_axis=0, tiled=True)

    def over_views(part):
        spread = jnp.broadcast_to(part[None], (views,) + part.shape)
        return lax.all_to_all(spread, "views", split_axis=0, concat_axis=0, tiled=True)

    message, select = call(
        begin,
        [((OWNERS, PIECES * 2 * FEAT + PIX), F32), ((rows, GAUSS), BF16)],
        linear_point, right_side, damping, proj, depth_order[0], dest, block_depth,
    )
    short = ((OWNERS, PIECES * FEAT + PIX), F32)
    message, alphas, clears, weights, prim, front, behind, change, totals0 = call(
        render_first,
        [short]
        + [((rows, PIX), F32)] * 3
        + [((FEAT, rows), F32)]
        + [((slots, slots), BF16)] * 2
        + [((FEAT, PIX), F32), ((1, PIX), F32)],
        over_tiles(message), basis, weight,
    )
    part_shape = ((FEAT, GAUSS + PIX), F32)
    (part,) = call(collect, [part_shape], over_tiles(message), select, proj)
    message, residual, step = call(
        step_first,
        [short, ((PARAMS, GAUSS), F32), ((1, 1), F32)],
        over_views(part), right_side, damping, proj, select, totals0,
    )
    message, totals1 = call(
        render_again,
        [short, ((1, PIX), F32)],
        over_tiles(message), basis, weight, alphas, clears, weights, prim, front, behind, change, totals0,
    )
    (part,) = call(collect, [part_shape], over_tiles(message), select, proj)
    return tuple(
        call(
            step_last,
            [((PARAMS, GAUSS), F32)] * 2,
            over_views(part), right_side, damping, residual, step, totals0, totals1,
        )
    )


def solution(mesh):
    in_specs = (
        P(None, "tiles"),
        P(None, "tiles"),
        P(None, "tiles"),
        P("views", None, None),
        P("views", "tiles", None, None),
        P("views", "tiles", None),
        P("views", "tiles", None),
        P("views", "tiles", None),
        P("views", "tiles"),
    )
    out_specs = (P(None, "tiles"), P(None, "tiles"))
    return jax.shard_map(body, mesh=mesh, in_specs=in_specs, out_specs=out_specs, check_vma=False)
```

```python
import jax
import jax.numpy as jnp
from jax import lax
from jax.experimental import pallas as pl
from jax.experimental.pallas import tpu as pltpu
from jax.sharding import PartitionSpec as P

OFFSET = 6.0
PARAMS = 59
FEAT = 16
ROWS = 8
CAP = 2
PIECES = CAP * ROWS
OWNERS = 64
GAUSS = 512
PIX = 128
F32 = jnp.float32
BF16 = jnp.bfloat16

NN = (((1,), (0,)), ((), ()))
NT = (((1,), (1,)), ((), ()))
TN = (((0,), (0,)), ((), ()))


def iota(shape, axis):
    return lax.broadcasted_iota(jnp.int32, shape, axis)


def mm(a, b, dims=NN):
    return lax.dot_general(a, b, dims, preferred_element_type=F32)


def split(x):
    high = x.astype(BF16)
    low = (x - high.astype(F32)).astype(BF16)
    return high, low


def split3(x):
    high = x.astype(BF16)
    rest = x - high.astype(F32)
    mid = rest.astype(BF16)
    low = (rest - mid.astype(F32)).astype(BF16)
    return high, mid, low


def mm3(a, b, dims=NN):
    ah, al = split(a)
    bh, bl = split(b)
    return mm(ah, bh, dims) + mm(al, bh, dims) + mm(ah, bl, dims)


def total(x):
    return jnp.sum(jnp.sum(x, axis=1, keepdims=True), axis=0, keepdims=True)


def lanes(values, rows):
    lane = iota((rows, PIX), 1)
    out = jnp.zeros((rows, PIX), F32)
    for i, value in enumerate(values):
        out = jnp.where(lane == i, value, out)
    return out


def to_message(feats, select):
    stacked = jnp.concatenate(feats, axis=0)
    high, low = split(stacked)
    slots = mm(high, select, NT) + mm(low, select, NT)
    pieces = [slots[:, i * OWNERS : (i + 1) * OWNERS] for i in range(PIECES)]
    return jnp.concatenate(pieces, axis=0).T


def by_column(message, width):
    turned = message.T
    return jnp.concatenate([turned[i * width : (i + 1) * width] for i in range(PIECES)], axis=1)


def choose(order, dest):
    blocks = dest.shape[1]
    mine = iota((OWNERS, blocks), 0) == dest
    mine_f = jnp.where(mine, 1.0, 0.0)
    earlier = jnp.where(iota((blocks, blocks), 0) < iota((blocks, blocks), 1), 1.0, 0.0)
    count = mm(mine_f.astype(BF16), earlier.astype(BF16))
    owns = [jnp.where(mine & (count == float(s)), 1.0, 0.0) for s in range(CAP)]
    own_all = jnp.concatenate(owns, axis=0).astype(BF16)
    here = iota((blocks, GAUSS), 1) // ROWS == iota((blocks, GAUSS), 0)
    number = jnp.where(here, order + 1, 0)
    parts = jnp.concatenate(
        [(number // 16).astype(F32), (number % 16).astype(F32)], axis=0
    ).astype(BF16)
    pick = jnp.where(iota((GAUSS, PIX), 0) % ROWS == iota((GAUSS, PIX), 1), 1.0, 0.0).astype(BF16)
    table = mm(parts, pick).astype(BF16)
    ids = mm(own_all, table[:blocks]) * 16.0 + mm(own_all, table[blocks:])
    columns = (iota((OWNERS, GAUSS), 1) + 1).astype(F32)
    rows = []
    for s in range(CAP):
        for r in range(ROWS):
            chosen = ids[s * OWNERS : (s + 1) * OWNERS, r : r + 1] == columns
            rows.append(jnp.where(chosen, 1.0, 0.0).astype(BF16))
    return owns, jnp.concatenate(rows, axis=0)


def begin_kernel(
    point_hbm, right_hbm, damp_hbm, proj_hbm, basis_hbm, weight_hbm, order_hbm, dest_hbm, depth_hbm,
    message_ref, select_ref, aux_ref, proj_ref,
    point, right, damp, proj, basis, weight, order, dest, depth, sems,
):
    pairs = [
        (order_hbm, order), (dest_hbm, dest), (depth_hbm, depth), (proj_hbm, proj),
        (point_hbm, point), (right_hbm, right), (damp_hbm, damp), (basis_hbm, basis), (weight_hbm, weight),
    ]
    copies = [pltpu.make_async_copy(a, b, sems.at[i]) for i, (a, b) in enumerate(pairs)]
    for copy in copies:
        copy.start()
    for copy in copies[:3]:
        copy.wait()
    owns, select = choose(order[...], dest[...])
    select_ref[...] = select
    depth_f = depth[...].astype(F32) + 1.0
    marks = [jnp.sum(own * depth_f, axis=1, keepdims=True) for own in owns]
    for copy in copies[3:7]:
        copy.wait()
    right_now = right[...]
    turned = proj[...]
    proj_ref[...] = jnp.concatenate([turned, jnp.zeros((FEAT, PIX - PARAMS), F32)], axis=1)
    feats = mm3(turned, jnp.concatenate([point[...], right_now], axis=1))
    message = to_message([feats[:, :GAUSS], feats[:, GAUSS:]], select)
    squared = right_now * right_now
    tail = lanes(marks + [total(squared), total(damp[...] * squared)], OWNERS)
    message_ref[...] = jnp.concatenate([message, tail], axis=1)
    for copy in copies[7:]:
        copy.wait()
    first = jnp.where(iota((4, PIX), 0) == 0, 1.0, 0.0)
    last = jnp.broadcast_to(weight[...], (8, PIX))
    aux_ref[...] = jnp.concatenate([first, basis[:, 0, :], last], axis=0)


def begin(*args):
    rows = PIECES * OWNERS
    return pl.pallas_call(
        begin_kernel,
        out_shape=[
            jax.ShapeDtypeStruct((OWNERS, PIECES * 2 * FEAT + PIX), F32),
            jax.ShapeDtypeStruct((rows, GAUSS), BF16),
            jax.ShapeDtypeStruct((FEAT + 8, PIX), F32),
            jax.ShapeDtypeStruct((FEAT, PIX), F32),
        ],
        in_specs=[pl.BlockSpec(memory_space=pltpu.HBM)] * len(args),
        out_specs=[pl.BlockSpec(memory_space=pltpu.VMEM)] * 4,
        scratch_shapes=[pltpu.VMEM(x.shape, x.dtype) for x in args]
        + [pltpu.SemaphoreType.DMA((len(args),))],
        compiler_params=pltpu.CompilerParams(vmem_limit_bytes=40 * 1024 * 1024),
        name="begin",
    )(*[pltpu.with_memory_space_constraint(x, pltpu.HBM) for x in args])


def order_masks(marks):
    side = CAP * OWNERS
    by_row = jnp.broadcast_to(marks, (side, side))
    diagonal = iota((side, side), 0) == iota((side, side), 1)
    by_lane = jnp.sum(jnp.where(diagonal, by_row, 0.0), axis=0, keepdims=True)
    front = jnp.where((by_lane < by_row) & (by_lane > 0.0), 1.0, 0.0)
    behind = jnp.where((by_row < by_lane) & (by_row > 0.0), 1.0, 0.0)
    return front.astype(BF16), behind.astype(BF16)


def ordered_sum(mask, value):
    high, low = split(value)
    return mm(mask, high) + mm(mask, low)


def image_change(prim_cols, tang_cols, weights, slopes):
    wh, wl = split(weights)
    vh, vl = split(slopes)
    th, tl = split(tang_cols)
    ph, plow = split(prim_cols)
    change = mm(th, wh) + mm(tl, wh) + mm(th, wl) + mm(ph, vh) + mm(plow, vh) + mm(ph, vl)
    row = iota((FEAT, PIX), 0)
    return jnp.where((row >= 1) & (row < 4), change, 0.0)


def pull_back(prim_cols, basis, colour, alphas, clears, weights, behind):
    shade = mm3(prim_cols, colour, TN)
    pulls = [weights[i] * shade[i * OWNERS : (i + 1) * OWNERS] for i in range(PIECES)]
    sums = []
    for s in range(CAP):
        acc = pulls[s * ROWS]
        for r in range(1, ROWS):
            acc = acc + pulls[s * ROWS + r]
        sums.append(acc)
    through = ordered_sum(behind, jnp.concatenate(sums, axis=0))
    logits = [None] * PIECES
    for s in range(CAP):
        acc = through[s * OWNERS : (s + 1) * OWNERS]
        for r in reversed(range(ROWS)):
            i = s * ROWS + r
            logits[i] = clears[i] * pulls[i] - alphas[i] * acc
            acc = acc + pulls[i]
    both = jnp.concatenate(
        [jnp.concatenate(logits, axis=0), jnp.concatenate(weights, axis=0)], axis=1
    )
    back = mm3(both, jnp.concatenate([basis, colour], axis=1), NT)
    return back


def as_rows(back):
    return jnp.concatenate([back[i * OWNERS : (i + 1) * OWNERS] for i in range(PIECES)], axis=1)


def slope_terms(tangents, alphas, clears):
    slopes = []
    sums = []
    for s in range(CAP):
        acc = jnp.zeros((OWNERS, PIX), F32)
        for r in range(ROWS):
            i = s * ROWS + r
            slopes.append(clears[i] * tangents[i] + acc)
            acc = acc - alphas[i] * tangents[i]
        sums.append(acc)
    return slopes, jnp.concatenate(sums, axis=0)


def render_first(message, aux):
    width = 2 * FEAT
    columns = by_column(message[:, : PIECES * width], width)
    tail = message[:, PIECES * width :]
    totals = jnp.sum(tail, axis=0, keepdims=True)
    basis, pixel_weight = aux[:FEAT], aux[FEAT : FEAT + 1]
    both = jnp.zeros((FEAT, PIX), F32)
    wide = jnp.concatenate(
        [jnp.concatenate([basis, both], axis=1), jnp.concatenate([both, basis], axis=1)], axis=0
    )
    logits_tangents = mm3(columns, wide, TN)
    front, behind = order_masks(jnp.concatenate([tail[:, 0:1], tail[:, 1:2]], axis=0))
    alphas, clears, plain, tangents, lengths = [], [], [], [], []
    for s in range(CAP):
        open_now = None
        length = None
        for r in range(ROWS):
            i = s * ROWS + r
            block = logits_tangents[i * OWNERS : (i + 1) * OWNERS]
            z = block[:, :PIX] - OFFSET
            tangents.append(block[:, PIX:])
            small = jnp.exp(-jnp.abs(z))
            grown = 1.0 + small
            part = 1.0 / grown
            rest = small * part
            alpha = jnp.where(z >= 0.0, part, rest)
            clear = jnp.where(z >= 0.0, rest, part)
            log_clear = -(jnp.maximum(z, 0.0) + jnp.log(grown))
            alphas.append(alpha)
            clears.append(clear)
            plain.append(alpha if open_now is None else alpha * open_now)
            open_now = clear if open_now is None else open_now * clear
            length = log_clear if length is None else length + log_clear
        lengths.append(length)
    high, mid, low = split3(jnp.concatenate(lengths, axis=0))
    ahead = jnp.exp(mm(front, high) + mm(front, mid) + mm(front, low))
    weights = [
        plain[i] * ahead[(i // ROWS) * OWNERS : (i // ROWS + 1) * OWNERS] for i in range(PIECES)
    ]
    slopes, sums = slope_terms(tangents, alphas, clears)
    ahead_tangent = ordered_sum(front, sums)
    slopes = [
        weights[i]
        * (slopes[i] + ahead_tangent[(i // ROWS) * OWNERS : (i // ROWS + 1) * OWNERS])
        for i in range(PIECES)
    ]
    prim_cols = columns[:FEAT]
    change = image_change(
        prim_cols,
        columns[FEAT:],
        jnp.concatenate(weights, axis=0),
        jnp.concatenate(slopes, axis=0),
    )
    colour = change * pixel_weight
    back = pull_back(prim_cols, basis, colour, alphas, clears, weights, behind)
    out = jnp.concatenate(
        [as_rows(back), lanes([total(colour * change)], OWNERS)], axis=1
    )
    return (
        out,
        jnp.concatenate(alphas, axis=0),
        jnp.concatenate(clears, axis=0),
        jnp.concatenate(weights, axis=0),
        prim_cols,
        front,
        behind,
        change,
        totals,
    )


def pieces_of(array):
    return [array[i * OWNERS : (i + 1) * OWNERS] for i in range(PIECES)]


def render_again(
    message, aux, alphas, clears, weights, prim_cols, front, behind, change0, totals0
):
    columns = by_column(message[:, : PIECES * FEAT], FEAT)
    totals = jnp.sum(message[:, PIECES * FEAT :], axis=0, keepdims=True)
    basis, pixel_weight = aux[:FEAT], aux[FEAT : FEAT + 1]
    tangents = pieces_of(mm3(columns, basis, TN))
    alphas, clears, weight_list = pieces_of(alphas), pieces_of(clears), pieces_of(weights)
    slopes, sums = slope_terms(tangents, alphas, clears)
    ahead_tangent = ordered_sum(front, sums)
    slopes = [
        weight_list[i]
        * (slopes[i] + ahead_tangent[(i // ROWS) * OWNERS : (i // ROWS + 1) * OWNERS])
        for i in range(PIECES)
    ]
    ratio = totals[:, 0:1] / totals0[:, 2:3]
    change = (
        image_change(prim_cols, columns, weights, jnp.concatenate(slopes, axis=0))
        + ratio * change0
    )
    colour = change * pixel_weight
    back = pull_back(prim_cols, basis, colour, alphas, clears, weight_list, behind)
    out = jnp.concatenate([as_rows(back), lanes([total(colour * change)], OWNERS)], axis=1)
    return out, totals


def collect(message, select, proj):
    columns = by_column(message[:, : PIECES * FEAT], FEAT)
    high, low = split(columns)
    wide = mm(jnp.concatenate([high, low], axis=0), select)
    gathered = wide[:FEAT] + wide[FEAT:]
    tail = jnp.sum(message[:, PIECES * FEAT :], axis=0, keepdims=True)
    turned = jnp.concatenate([proj[:ROWS, : PIX // 2], proj[ROWS:, : PIX // 2]], axis=1)
    turned = jnp.where(iota((ROWS, PIX), 1) == PIX - 1, tail[:, 0:1], turned)
    parts = [gathered[:, j : j + PIX] for j in range(0, GAUSS, PIX)]
    return jnp.concatenate(parts + [turned], axis=0)


def product_of(message):
    views = message.shape[0]
    count = GAUSS // PIX
    gathered = jnp.concatenate(
        [
            jnp.concatenate(
                [
                    message[:, j * FEAT + h : j * FEAT + h + ROWS].reshape(views * ROWS, PIX)
                    for j in range(count)
                ],
                axis=1,
            )
            for h in (0, ROWS)
        ],
        axis=0,
    )
    last = message[:, count * FEAT :].reshape(views * ROWS, PIX)
    turned = jnp.concatenate([last[:, : PIX // 2], last[:, PIX // 2 :]], axis=0)
    product = mm3(turned, gathered, TN)[:PARAMS]
    energy = jnp.sum(last, axis=0, keepdims=True)[:, PIX - 1 :] * (1.0 / ROWS)
    return product, energy


def step_first(message, right, damp, proj, select, totals0):
    product, energy = product_of(message)
    product = product + damp * right
    step = totals0[:, 2:3] / (energy + totals0[:, 3:4])
    residual = right - step * product
    weighted = damp * residual
    feats = mm3(proj[:, :PARAMS], residual)
    tail = lanes(
        [total(residual * residual), total(weighted * residual), total(weighted * right)], OWNERS
    )
    out = jnp.concatenate([to_message([feats], select), tail], axis=1)
    return out, residual, step


def step_last(message, right, damp, residual, step, totals0, totals1):
    product, energy = product_of(message)
    ratio = totals1[:, 0:1] / totals0[:, 2:3]
    direction = residual + ratio * right
    product = product + damp * direction
    damped = totals1[:, 1:2] + 2.0 * ratio * totals1[:, 2:3] + ratio * ratio * totals0[:, 3:4]
    step_now = totals1[:, 0:1] / (energy + damped)
    return step * right + step_now * direction, residual - step_now * product


def call(function, outs, *args):
    def kernel(*refs):
        results = function(*[ref[...] for ref in refs[: len(args)]])
        if len(outs) == 1:
            results = (results,) if not isinstance(results, tuple) else results
        for ref, result in zip(refs[len(args) :], results):
            ref[...] = result

    result = pl.pallas_call(
        kernel,
        out_shape=[jax.ShapeDtypeStruct(shape, dtype) for shape, dtype in outs],
        in_specs=[pl.BlockSpec(memory_space=pltpu.VMEM)] * len(args),
        out_specs=[pl.BlockSpec(memory_space=pltpu.VMEM)] * len(outs),
        compiler_params=pltpu.CompilerParams(vmem_limit_bytes=40 * 1024 * 1024),
        name=function.__name__,
    )(*args)
    return result


def body(
    linear_point,
    right_side,
    damping,
    projection,
    pixel_basis,
    pixel_weight,
    depth_order,
    tile_dest,
    block_depth,
):
    dest = tile_dest.reshape(1, -1)
    views = lax.axis_size("views")
    rows = PIECES * OWNERS
    slots = CAP * OWNERS

    def over_tiles(message):
        return lax.all_to_all(message, "tiles", split_axis=0, concat_axis=0, tiled=True)

    def over_views(part):
        spread = jnp.broadcast_to(part[None], (views,) + part.shape)
        return lax.all_to_all(spread, "views", split_axis=0, concat_axis=0, tiled=True)

    message, select, aux, proj = begin(
        linear_point, right_side, damping, jnp.swapaxes(projection, 1, 2)[0],
        pixel_basis.reshape(FEAT - 4, 1, PIX), pixel_weight[0], depth_order[0], dest, block_depth,
    )
    short = ((OWNERS, PIECES * FEAT + PIX), F32)
    message, alphas, clears, weights, prim, front, behind, change, totals0 = call(
        render_first,
        [short]
        + [((rows, PIX), F32)] * 3
        + [((FEAT, rows), F32)]
        + [((slots, slots), BF16)] * 2
        + [((FEAT, PIX), F32), ((1, PIX), F32)],
        over_tiles(message), aux,
    )
    part_shape = ((GAUSS // PIX * FEAT + ROWS, PIX), F32)
    (part,) = call(collect, [part_shape], over_tiles(message), select, proj)
    message, residual, step = call(
        step_first,
        [short, ((PARAMS, GAUSS), F32), ((1, 1), F32)],
        over_views(part), right_side, damping, proj, select, totals0,
    )
    message, totals1 = call(
        render_again,
        [short, ((1, PIX), F32)],
        over_tiles(message), aux, alphas, clears, weights, prim, front, behind, change, totals0,
    )
    (part,) = call(collect, [part_shape], over_tiles(message), select, proj)
    return tuple(
        call(
            step_last,
            [((PARAMS, GAUSS), F32)] * 2,
            over_views(part), right_side, damping, residual, step, totals0, totals1,
        )
    )


def solution(mesh):
    in_specs = (
        P(None, "tiles"),
        P(None, "tiles"),
        P(None, "tiles"),
        P("views", None, None),
        P("views", "tiles", None, None),
        P("views", "tiles", None),
        P("views", "tiles", None),
        P("views", "tiles", None),
        P("views", "tiles"),
    )
    out_specs = (P(None, "tiles"), P(None, "tiles"))
    return jax.shard_map(body, mesh=mesh, in_specs=in_specs, out_specs=out_specs, check_vma=False)
```

```python
import jax
import jax.numpy as jnp
from jax import lax
from jax.experimental import pallas as pl
from jax.experimental.pallas import tpu as pltpu
from jax.sharding import PartitionSpec as P

OFFSET = 6.0
PARAMS = 59
FEAT = 16
ROWS = 8
CAP = 2
PIECES = CAP * ROWS
OWNERS = 64
GAUSS = 512
PIX = 128
F32 = jnp.float32
BF16 = jnp.bfloat16

NN = (((1,), (0,)), ((), ()))
NT = (((1,), (1,)), ((), ()))
TN = (((0,), (0,)), ((), ()))


def iota(shape, axis):
    return lax.broadcasted_iota(jnp.int32, shape, axis)


def mm(a, b, dims=NN):
    return lax.dot_general(a, b, dims, preferred_element_type=F32)


def split(x):
    high = x.astype(BF16)
    low = (x - high.astype(F32)).astype(BF16)
    return high, low


def mm_short(a, b):
    ah, al = split(a)
    bh, bl = split(b)
    return mm(jnp.concatenate([ah, al, ah], axis=0), jnp.concatenate([bh, bh, bl], axis=0), TN)


def project(proj, vectors):
    tall = jnp.concatenate([vectors, jnp.zeros((PIX // 2 - PARAMS, vectors.shape[1]), F32)], axis=0)
    ph, pl_ = split(proj)
    th, tl = split(tall)
    return mm(jnp.concatenate([ph, pl_, ph], axis=1), jnp.concatenate([th, th, tl], axis=0))


def total(x):
    return jnp.sum(jnp.sum(x, axis=1, keepdims=True), axis=0, keepdims=True)


def lanes(values, rows):
    lane = iota((rows, PIX), 1)
    out = jnp.zeros((rows, PIX), F32)
    for i, value in enumerate(values):
        out = jnp.where(lane == i, value, out)
    return out


def to_message(feats, select):
    stacked = jnp.concatenate(feats, axis=0)
    rows = stacked.shape[0]
    both = mm(jnp.concatenate(split(stacked), axis=0), select, NT)
    slots = both[:rows] + both[rows:]
    return by_owner(slots)


def by_owner(slots):
    pieces = [slots[:, i * OWNERS : (i + 1) * OWNERS] for i in range(PIECES)]
    return jnp.concatenate(pieces, axis=0).T


def by_column(message, width):
    turned = message.T
    return jnp.concatenate([turned[i * width : (i + 1) * width] for i in range(PIECES)], axis=1)


def choose(order, dest):
    blocks = dest.shape[1]
    mine = iota((OWNERS, blocks), 0) == dest
    mine_f = jnp.where(mine, 1.0, 0.0)
    earlier = jnp.where(iota((blocks, blocks), 0) < iota((blocks, blocks), 1), 1.0, 0.0)
    count = mm(mine_f.astype(BF16), earlier.astype(BF16))
    owns = [jnp.where(mine & (count == float(s)), 1.0, 0.0) for s in range(CAP)]
    own_all = jnp.concatenate(owns, axis=0).astype(BF16)
    here = iota((blocks, GAUSS), 1) // ROWS == iota((blocks, GAUSS), 0)
    number = jnp.where(here, order + 1, 0)
    parts = jnp.concatenate(
        [(number // 16).astype(F32), (number % 16).astype(F32)], axis=0
    ).astype(BF16)
    pick = jnp.where(iota((GAUSS, PIX), 0) % ROWS == iota((GAUSS, PIX), 1), 1.0, 0.0).astype(BF16)
    table = mm(parts, pick).astype(BF16)
    ids = mm(own_all, table[:blocks]) * 16.0 + mm(own_all, table[blocks:])
    columns = (iota((OWNERS, GAUSS), 1) + 1).astype(F32)
    rows = []
    for s in range(CAP):
        for r in range(ROWS):
            chosen = ids[s * OWNERS : (s + 1) * OWNERS, r : r + 1] == columns
            rows.append(jnp.where(chosen, 1.0, 0.0).astype(BF16))
    return owns, jnp.concatenate(rows, axis=0)


def begin_kernel(
    point_hbm, right_hbm, damp_hbm, proj_hbm, basis_hbm, weight_hbm, order_hbm, dest_hbm, depth_hbm,
    message_ref, select_ref, aux_ref, proj_ref,
    point, right, damp, proj, basis, weight, order, dest, depth, sems,
):
    pairs = [
        (order_hbm, order), (dest_hbm, dest), (depth_hbm, depth), (proj_hbm, proj),
        (point_hbm, point), (right_hbm, right), (damp_hbm, damp), (basis_hbm, basis), (weight_hbm, weight),
    ]
    copies = [pltpu.make_async_copy(a, b, sems.at[i]) for i, (a, b) in enumerate(pairs)]
    for copy in copies:
        copy.start()
    for copy in copies[:3]:
        copy.wait()
    owns, select = choose(order[...], dest[...])
    select_ref[...] = select
    depth_f = depth[...].astype(F32) + 1.0
    marks = [jnp.sum(own * depth_f, axis=1, keepdims=True) for own in owns]
    for copy in copies[3:7]:
        copy.wait()
    right_now = right[...]
    padded = jnp.concatenate([proj[...], jnp.zeros((FEAT, PIX - PARAMS), F32)], axis=1)
    proj_ref[...] = padded
    feats = project(padded[:, : PIX // 2], jnp.concatenate([point[...], right_now], axis=1))
    message = to_message([feats[:, :GAUSS], feats[:, GAUSS:]], select)
    squared = right_now * right_now
    tail = lanes(marks + [total(squared), total(damp[...] * squared)], OWNERS)
    message_ref[...] = jnp.concatenate([message, tail], axis=1)
    for copy in copies[7:]:
        copy.wait()
    first = jnp.where(iota((4, PIX), 0) == 0, 1.0, 0.0)
    last = jnp.broadcast_to(weight[...], (8, PIX))
    aux_ref[...] = jnp.concatenate([first, basis[:, 0, :], last], axis=0)


def begin(*args):
    rows = PIECES * OWNERS
    return pl.pallas_call(
        begin_kernel,
        out_shape=[
            jax.ShapeDtypeStruct((OWNERS, PIECES * 2 * FEAT + PIX), F32),
            jax.ShapeDtypeStruct((rows, GAUSS), BF16),
            jax.ShapeDtypeStruct((FEAT + 8, PIX), F32),
            jax.ShapeDtypeStruct((FEAT, PIX), F32),
        ],
        in_specs=[pl.BlockSpec(memory_space=pltpu.HBM)] * len(args),
        out_specs=[pl.BlockSpec(memory_space=pltpu.VMEM)] * 4,
        scratch_shapes=[pltpu.VMEM(x.shape, x.dtype) for x in args]
        + [pltpu.SemaphoreType.DMA((len(args),))],
        compiler_params=pltpu.CompilerParams(vmem_limit_bytes=40 * 1024 * 1024),
        name="begin",
    )(*[pltpu.with_memory_space_constraint(x, pltpu.HBM) for x in args])


def order_masks(marks):
    side = CAP * OWNERS
    by_row = jnp.broadcast_to(marks, (side, side))
    diagonal = iota((side, side), 0) == iota((side, side), 1)
    by_lane = jnp.sum(jnp.where(diagonal, by_row, 0.0), axis=0, keepdims=True)
    front = jnp.where((by_lane < by_row) & (by_lane > 0.0), 1.0, 0.0)
    behind = jnp.where((by_row < by_lane) & (by_row > 0.0), 1.0, 0.0)
    return front.astype(BF16), behind.astype(BF16)


def ordered_sum(mask, value):
    high, low = split(value)
    return mm(jnp.concatenate([mask, mask], axis=1), jnp.concatenate([high, low], axis=0))


def image_change(columns, both):
    high, low = split(columns)
    bh, bl = split(both)
    main = mm(jnp.concatenate([high, low], axis=0), bh)
    rest = mm(high, bl)
    change = (
        main[FEAT : 2 * FEAT, :PIX]
        + main[3 * FEAT :, :PIX]
        + rest[FEAT:, :PIX]
        + main[:FEAT, PIX:]
        + main[2 * FEAT : 3 * FEAT, PIX:]
        + rest[:FEAT, PIX:]
    )
    row = iota((FEAT, PIX), 0)
    return jnp.where((row >= 1) & (row < 4), change, 0.0)


def pull_back(prim_cols, basis, colour, alphas, clears, weights, behind):
    shade = mm_short(prim_cols, colour)
    pulls = [weights[i] * shade[i * OWNERS : (i + 1) * OWNERS] for i in range(PIECES)]
    sums = []
    for s in range(CAP):
        acc = pulls[s * ROWS]
        for r in range(1, ROWS):
            acc = acc + pulls[s * ROWS + r]
        sums.append(acc)
    through = ordered_sum(behind, jnp.concatenate(sums, axis=0))
    logits = [None] * PIECES
    for s in range(CAP):
        acc = through[s * OWNERS : (s + 1) * OWNERS]
        for r in reversed(range(ROWS)):
            i = s * ROWS + r
            logits[i] = clears[i] * pulls[i] - alphas[i] * acc
            acc = acc + pulls[i]
    both = jnp.concatenate(
        [jnp.concatenate(logits, axis=0), jnp.concatenate(weights, axis=0)], axis=1
    )
    high, low = split(both)
    bh, bl = split(jnp.concatenate([basis, colour], axis=1))
    main = mm(jnp.concatenate([bh, bl], axis=0), high, NT)
    return by_owner(main[:FEAT] + main[FEAT:] + mm(bh, low, NT))


def slope_terms(tangents, alphas, clears):
    slopes = []
    sums = []
    for s in range(CAP):
        acc = jnp.zeros((OWNERS, PIX), F32)
        for r in range(ROWS):
            i = s * ROWS + r
            slopes.append(clears[i] * tangents[i] + acc)
            acc = acc - alphas[i] * tangents[i]
        sums.append(acc)
    return slopes, jnp.concatenate(sums, axis=0)


def render_first(message, aux):
    width = 2 * FEAT
    columns = by_column(message[:, : PIECES * width], width)
    tail = message[:, PIECES * width :]
    totals = jnp.sum(tail, axis=0, keepdims=True)
    basis, pixel_weight = aux[:FEAT], aux[FEAT : FEAT + 1]
    both = jnp.zeros((FEAT, PIX), F32)
    wide = jnp.concatenate(
        [jnp.concatenate([basis, both], axis=1), jnp.concatenate([both, basis], axis=1)], axis=0
    )
    logits_tangents = mm_short(columns, wide)
    front, behind = order_masks(jnp.concatenate([tail[:, 0:1], tail[:, 1:2]], axis=0))
    alphas, clears, plain, tangents, lengths = [], [], [], [], []
    for s in range(CAP):
        open_now = None
        length = None
        for r in range(ROWS):
            i = s * ROWS + r
            block = logits_tangents[i * OWNERS : (i + 1) * OWNERS]
            z = block[:, :PIX] - OFFSET
            tangents.append(block[:, PIX:])
            small = jnp.exp(-jnp.abs(z))
            grown = 1.0 + small
            part = 1.0 / grown
            rest = small * part
            alpha = jnp.where(z >= 0.0, part, rest)
            clear = jnp.where(z >= 0.0, rest, part)
            log_clear = -(jnp.maximum(z, 0.0) + jnp.log(grown))
            alphas.append(alpha)
            clears.append(clear)
            plain.append(alpha if open_now is None else alpha * open_now)
            open_now = clear if open_now is None else open_now * clear
            length = log_clear if length is None else length + log_clear
        lengths.append(length)
    ahead = jnp.exp(ordered_sum(front, jnp.concatenate(lengths, axis=0)))
    weights = [
        plain[i] * ahead[(i // ROWS) * OWNERS : (i // ROWS + 1) * OWNERS] for i in range(PIECES)
    ]
    slopes, sums = slope_terms(tangents, alphas, clears)
    ahead_tangent = ordered_sum(front, sums)
    slopes = [
        weights[i]
        * (slopes[i] + ahead_tangent[(i // ROWS) * OWNERS : (i // ROWS + 1) * OWNERS])
        for i in range(PIECES)
    ]
    prim_cols = columns[:FEAT]
    change = image_change(
        columns,
        jnp.concatenate(
            [jnp.concatenate(weights, axis=0), jnp.concatenate(slopes, axis=0)], axis=1
        ),
    )
    colour = change * pixel_weight
    back = pull_back(prim_cols, basis, colour, alphas, clears, weights, behind)
    out = jnp.concatenate(
        [back, lanes([total(colour * change)], OWNERS)], axis=1
    )
    return (
        out,
        jnp.concatenate(alphas, axis=0),
        jnp.concatenate(clears, axis=0),
        jnp.concatenate(weights, axis=0),
        prim_cols,
        front,
        behind,
        change,
        totals,
    )


def pieces_of(array):
    return [array[i * OWNERS : (i + 1) * OWNERS] for i in range(PIECES)]


def render_again(
    message, aux, alphas, clears, weights, prim_cols, front, behind, change0, totals0
):
    columns = by_column(message[:, : PIECES * FEAT], FEAT)
    totals = jnp.sum(message[:, PIECES * FEAT :], axis=0, keepdims=True)
    basis, pixel_weight = aux[:FEAT], aux[FEAT : FEAT + 1]
    tangents = pieces_of(mm_short(columns, basis))
    alphas, clears, weight_list = pieces_of(alphas), pieces_of(clears), pieces_of(weights)
    slopes, sums = slope_terms(tangents, alphas, clears)
    ahead_tangent = ordered_sum(front, sums)
    slopes = [
        weight_list[i]
        * (slopes[i] + ahead_tangent[(i // ROWS) * OWNERS : (i // ROWS + 1) * OWNERS])
        for i in range(PIECES)
    ]
    ratio = totals[:, 0:1] / totals0[:, 2:3]
    change = (
        image_change(
            jnp.concatenate([prim_cols, columns], axis=0),
            jnp.concatenate([weights, jnp.concatenate(slopes, axis=0)], axis=1),
        )
        + ratio * change0
    )
    colour = change * pixel_weight
    back = pull_back(prim_cols, basis, colour, alphas, clears, weight_list, behind)
    out = jnp.concatenate([back, lanes([total(colour * change)], OWNERS)], axis=1)
    return out, totals


def collect(message, select, proj):
    columns = by_column(message[:, : PIECES * FEAT], FEAT)
    high, low = split(columns)
    wide = mm(jnp.concatenate([high, low], axis=0), select)
    gathered = wide[:FEAT] + wide[FEAT:]
    tail = jnp.sum(message[:, PIECES * FEAT :], axis=0, keepdims=True)
    turned = jnp.concatenate([proj[:ROWS, : PIX // 2], proj[ROWS:, : PIX // 2]], axis=1)
    turned = jnp.where(iota((ROWS, PIX), 1) == PIX - 1, tail[:, 0:1], turned)
    parts = [gathered[:, j : j + PIX] for j in range(0, GAUSS, PIX)]
    return jnp.concatenate(parts + [turned], axis=0)


def product_of(message):
    views = message.shape[0]
    count = GAUSS // PIX
    gathered = jnp.concatenate(
        [
            jnp.concatenate(
                [
                    message[:, j * FEAT + h : j * FEAT + h + ROWS].reshape(views * ROWS, PIX)
                    for j in range(count)
                ],
                axis=1,
            )
            for h in (0, ROWS)
        ],
        axis=0,
    )
    last = message[:, count * FEAT :].reshape(views * ROWS, PIX)
    turned = jnp.concatenate([last[:, : PIX // 2], last[:, PIX // 2 :]], axis=0).T
    th, tl = split(turned)
    wide = jnp.concatenate(
        [
            jnp.concatenate([th, th], axis=1),
            jnp.concatenate([tl, jnp.zeros(tl.shape, BF16)], axis=1),
        ],
        axis=0,
    )
    product = mm(wide, jnp.concatenate(split(gathered), axis=0))
    half = PIX // 2
    product = (product[:half] + product[half:])[:PARAMS]
    energy = jnp.sum(last, axis=0, keepdims=True)[:, PIX - 1 :] * (1.0 / ROWS)
    return product, energy


def step_first(message, right, damp, proj, select, totals0):
    product, energy = product_of(message)
    product = product + damp * right
    step = totals0[:, 2:3] / (energy + totals0[:, 3:4])
    residual = right - step * product
    weighted = damp * residual
    feats = project(proj[:, : PIX // 2], residual)
    tail = lanes(
        [total(residual * residual), total(weighted * residual), total(weighted * right)], OWNERS
    )
    out = jnp.concatenate([to_message([feats], select), tail], axis=1)
    return out, residual, step


def step_last(message, right, damp, residual, step, totals0, totals1):
    product, energy = product_of(message)
    ratio = totals1[:, 0:1] / totals0[:, 2:3]
    direction = residual + ratio * right
    product = product + damp * direction
    damped = totals1[:, 1:2] + 2.0 * ratio * totals1[:, 2:3] + ratio * ratio * totals0[:, 3:4]
    step_now = totals1[:, 0:1] / (energy + damped)
    return step * right + step_now * direction, residual - step_now * product


def call(function, outs, *args):
    def kernel(*refs):
        results = function(*[ref[...] for ref in refs[: len(args)]])
        if len(outs) == 1:
            results = (results,) if not isinstance(results, tuple) else results
        for ref, result in zip(refs[len(args) :], results):
            ref[...] = result

    result = pl.pallas_call(
        kernel,
        out_shape=[jax.ShapeDtypeStruct(shape, dtype) for shape, dtype in outs],
        in_specs=[pl.BlockSpec(memory_space=pltpu.VMEM)] * len(args),
        out_specs=[pl.BlockSpec(memory_space=pltpu.VMEM)] * len(outs),
        compiler_params=pltpu.CompilerParams(vmem_limit_bytes=40 * 1024 * 1024),
        name=function.__name__,
    )(*args)
    return result


def body(
    linear_point,
    right_side,
    damping,
    projection,
    pixel_basis,
    pixel_weight,
    depth_order,
    tile_dest,
    block_depth,
):
    dest = tile_dest.reshape(1, -1)
    views = lax.axis_size("views")
    rows = PIECES * OWNERS
    slots = CAP * OWNERS

    def over_tiles(message):
        return lax.all_to_all(message, "tiles", split_axis=0, concat_axis=0, tiled=True)

    def over_views(part):
        spread = jnp.broadcast_to(part[None], (views,) + part.shape)
        return lax.all_to_all(spread, "views", split_axis=0, concat_axis=0, tiled=True)

    message, select, aux, proj = begin(
        linear_point, right_side, damping, jnp.swapaxes(projection, 1, 2)[0],
        pixel_basis.reshape(FEAT - 4, 1, PIX), pixel_weight[0], depth_order[0], dest, block_depth,
    )
    short = ((OWNERS, PIECES * FEAT + PIX), F32)
    message, alphas, clears, weights, prim, front, behind, change, totals0 = call(
        render_first,
        [short]
        + [((rows, PIX), F32)] * 3
        + [((FEAT, rows), F32)]
        + [((slots, slots), BF16)] * 2
        + [((FEAT, PIX), F32), ((1, PIX), F32)],
        over_tiles(message), aux,
    )
    part_shape = ((GAUSS // PIX * FEAT + ROWS, PIX), F32)
    (part,) = call(collect, [part_shape], over_tiles(message), select, proj)
    message, residual, step = call(
        step_first,
        [short, ((PARAMS, GAUSS), F32), ((1, 1), F32)],
        over_views(part), right_side, damping, proj, select, totals0,
    )
    message, totals1 = call(
        render_again,
        [short, ((1, PIX), F32)],
        over_tiles(message), aux, alphas, clears, weights, prim, front, behind, change, totals0,
    )
    (part,) = call(collect, [part_shape], over_tiles(message), select, proj)
    return tuple(
        call(
            step_last,
            [((PARAMS, GAUSS), F32)] * 2,
            over_views(part), right_side, damping, residual, step, totals0, totals1,
        )
    )


def solution(mesh):
    in_specs = (
        P(None, "tiles"),
        P(None, "tiles"),
        P(None, "tiles"),
        P("views", None, None),
        P("views", "tiles", None, None),
        P("views", "tiles", None),
        P("views", "tiles", None),
        P("views", "tiles", None),
        P("views", "tiles"),
    )
    out_specs = (P(None, "tiles"), P(None, "tiles"))
    return jax.shard_map(body, mesh=mesh, in_specs=in_specs, out_specs=out_specs, check_vma=False)
```

```python
import functools

import jax
import jax.numpy as jnp
from jax import lax
from jax.experimental import pallas as pl
from jax.experimental.pallas import tpu as pltpu
from jax.sharding import PartitionSpec as P

OFFSET = 6.0
PARAMS = 59
FEAT = 16
ROWS = 8
CAP = 2
PIECES = CAP * ROWS
OWNERS = 64
GAUSS = 512
PIX = 128
F32 = jnp.float32
BF16 = jnp.bfloat16

NN = (((1,), (0,)), ((), ()))
NT = (((1,), (1,)), ((), ()))
TN = (((0,), (0,)), ((), ()))


def iota(shape, axis):
    return lax.broadcasted_iota(jnp.int32, shape, axis)


def mm(a, b, dims=NN):
    return lax.dot_general(a, b, dims, preferred_element_type=F32)


def split(x):
    high = x.astype(BF16)
    low = (x - high.astype(F32)).astype(BF16)
    return high, low


def mm_short(a, b):
    ah, al = split(a)
    bh, bl = split(b)
    return mm(jnp.concatenate([ah, al, ah], axis=0), jnp.concatenate([bh, bh, bl], axis=0), TN)


def project(proj, vectors):
    tall = jnp.concatenate([vectors, jnp.zeros((PIX // 2 - PARAMS, vectors.shape[1]), F32)], axis=0)
    ph, pl_ = split(proj)
    th, tl = split(tall)
    return mm(jnp.concatenate([ph, pl_, ph], axis=1), jnp.concatenate([th, th, tl], axis=0))


def total(x):
    return jnp.sum(jnp.sum(x, axis=1, keepdims=True), axis=0, keepdims=True)


def lanes(values, rows):
    lane = iota((rows, PIX), 1)
    out = jnp.zeros((rows, PIX), F32)
    for i, value in enumerate(values):
        out = jnp.where(lane == i, value, out)
    return out


def to_message(feats, select):
    stacked = jnp.concatenate(feats, axis=0)
    rows = stacked.shape[0]
    both = mm(jnp.concatenate(split(stacked), axis=0), select, NT)
    slots = both[:rows] + both[rows:]
    return by_owner(slots)


def by_owner(slots):
    pieces = [slots[:, i * OWNERS : (i + 1) * OWNERS] for i in range(PIECES)]
    return jnp.concatenate(pieces, axis=0).T


def by_column(message, width):
    turned = message.T
    return jnp.concatenate([turned[i * width : (i + 1) * width] for i in range(PIECES)], axis=1)


def choose(order, dest):
    blocks = dest.shape[1]
    mine = iota((OWNERS, blocks), 0) == dest
    mine_f = jnp.where(mine, 1.0, 0.0)
    earlier = jnp.where(iota((blocks, blocks), 0) < iota((blocks, blocks), 1), 1.0, 0.0)
    count = mm(mine_f.astype(BF16), earlier.astype(BF16))
    owns = [jnp.where(mine & (count == float(s)), 1.0, 0.0) for s in range(CAP)]
    own_all = jnp.concatenate(owns, axis=0).astype(BF16)
    here = iota((blocks, GAUSS), 1) // ROWS == iota((blocks, GAUSS), 0)
    number = jnp.where(here, order + 1, 0)
    parts = jnp.concatenate(
        [(number // 16).astype(F32), (number % 16).astype(F32)], axis=0
    ).astype(BF16)
    pick = jnp.where(iota((GAUSS, PIX), 0) % ROWS == iota((GAUSS, PIX), 1), 1.0, 0.0).astype(BF16)
    table = mm(parts, pick).astype(BF16)
    ids = mm(own_all, table[:blocks]) * 16.0 + mm(own_all, table[blocks:])
    columns = (iota((OWNERS, GAUSS), 1) + 1).astype(F32)
    rows = []
    for s in range(CAP):
        for r in range(ROWS):
            chosen = ids[s * OWNERS : (s + 1) * OWNERS, r : r + 1] == columns
            rows.append(jnp.where(chosen, 1.0, 0.0).astype(BF16))
    return owns, jnp.concatenate(rows, axis=0)


def begin_kernel(
    point_hbm, right_hbm, damp_hbm, proj_hbm, basis_hbm, weight_hbm, order_hbm, dest_hbm, depth_hbm,
    message_ref, select_ref, aux_ref, proj_ref,
    point, right, damp, proj, basis, weight, order, dest, depth, sems,
):
    pairs = [
        (order_hbm, order), (dest_hbm, dest), (depth_hbm, depth), (proj_hbm, proj),
        (point_hbm, point), (right_hbm, right), (damp_hbm, damp), (basis_hbm, basis), (weight_hbm, weight),
    ]
    copies = [pltpu.make_async_copy(a, b, sems.at[i]) for i, (a, b) in enumerate(pairs)]
    for copy in copies:
        copy.start()
    for copy in copies[:3]:
        copy.wait()
    owns, select = choose(order[...], dest[...])
    select_ref[...] = select
    depth_f = depth[...].astype(F32) + 1.0
    marks = [jnp.sum(own * depth_f, axis=1, keepdims=True) for own in owns]
    for copy in copies[3:7]:
        copy.wait()
    right_now = right[...]
    padded = jnp.concatenate([proj[...], jnp.zeros((FEAT, PIX - PARAMS), F32)], axis=1)
    proj_ref[...] = padded
    feats = project(padded[:, : PIX // 2], jnp.concatenate([point[...], right_now], axis=1))
    message = to_message([feats[:, :GAUSS], feats[:, GAUSS:]], select)
    squared = right_now * right_now
    tail = lanes(marks + [total(squared), total(damp[...] * squared)], OWNERS)
    message_ref[:, 0, :] = jnp.concatenate([message, tail], axis=1)
    for copy in copies[7:]:
        copy.wait()
    first = jnp.where(iota((4, PIX), 0) == 0, 1.0, 0.0)
    last = jnp.broadcast_to(weight[...], (8, PIX))
    aux_ref[...] = jnp.concatenate([first, basis[:, 0, :], last], axis=0)


def begin(*args):
    rows = PIECES * OWNERS
    return pl.pallas_call(
        begin_kernel,
        out_shape=[
            jax.ShapeDtypeStruct((OWNERS, 1, PIECES * 2 * FEAT + PIX), F32),
            jax.ShapeDtypeStruct((rows, GAUSS), BF16),
            jax.ShapeDtypeStruct((FEAT + 8, PIX), F32),
            jax.ShapeDtypeStruct((FEAT, PIX), F32),
        ],
        in_specs=[pl.BlockSpec(memory_space=pltpu.HBM)] * len(args),
        out_specs=[pl.BlockSpec(memory_space=pltpu.VMEM)] * 4,
        scratch_shapes=[pltpu.VMEM(x.shape, x.dtype) for x in args]
        + [pltpu.SemaphoreType.DMA((len(args),))],
        compiler_params=pltpu.CompilerParams(vmem_limit_bytes=40 * 1024 * 1024),
        name="begin",
    )(*[pltpu.with_memory_space_constraint(x, pltpu.HBM) for x in args])


def order_masks(marks):
    side = CAP * OWNERS
    by_row = jnp.broadcast_to(marks, (side, side))
    diagonal = iota((side, side), 0) == iota((side, side), 1)
    by_lane = jnp.sum(jnp.where(diagonal, by_row, 0.0), axis=0, keepdims=True)
    front = jnp.where((by_lane < by_row) & (by_lane > 0.0), 1.0, 0.0)
    behind = jnp.where((by_row < by_lane) & (by_row > 0.0), 1.0, 0.0)
    return front.astype(BF16), behind.astype(BF16)


def ordered_sum(mask, value):
    high, low = split(value)
    return mm(jnp.concatenate([mask, mask], axis=1), jnp.concatenate([high, low], axis=0))


def image_change(columns, both):
    high, low = split(columns)
    bh, bl = split(both)
    main = mm(jnp.concatenate([high, low], axis=0), bh)
    rest = mm(high, bl)
    change = (
        main[FEAT : 2 * FEAT, :PIX]
        + main[3 * FEAT :, :PIX]
        + rest[FEAT:, :PIX]
        + main[:FEAT, PIX:]
        + main[2 * FEAT : 3 * FEAT, PIX:]
        + rest[:FEAT, PIX:]
    )
    row = iota((FEAT, PIX), 0)
    return jnp.where((row >= 1) & (row < 4), change, 0.0)


def pull_back(prim_cols, basis, colour, alphas, clears, weights, behind):
    shade = mm_short(prim_cols, colour)
    pulls = [weights[i] * shade[i * OWNERS : (i + 1) * OWNERS] for i in range(PIECES)]
    sums = []
    for s in range(CAP):
        acc = pulls[s * ROWS]
        for r in range(1, ROWS):
            acc = acc + pulls[s * ROWS + r]
        sums.append(acc)
    through = ordered_sum(behind, jnp.concatenate(sums, axis=0))
    logits = [None] * PIECES
    for s in range(CAP):
        acc = through[s * OWNERS : (s + 1) * OWNERS]
        for r in reversed(range(ROWS)):
            i = s * ROWS + r
            logits[i] = clears[i] * pulls[i] - alphas[i] * acc
            acc = acc + pulls[i]
    both = jnp.concatenate(
        [jnp.concatenate(logits, axis=0), jnp.concatenate(weights, axis=0)], axis=1
    )
    high, low = split(both)
    bh, bl = split(jnp.concatenate([basis, colour], axis=1))
    main = mm(jnp.concatenate([bh, bl], axis=0), high, NT)
    return by_owner(main[:FEAT] + main[FEAT:] + mm(bh, low, NT))


def slope_terms(tangents, alphas, clears):
    slopes = []
    sums = []
    for s in range(CAP):
        acc = jnp.zeros((OWNERS, PIX), F32)
        for r in range(ROWS):
            i = s * ROWS + r
            slopes.append(clears[i] * tangents[i] + acc)
            acc = acc - alphas[i] * tangents[i]
        sums.append(acc)
    return slopes, jnp.concatenate(sums, axis=0)


def render_first(message, aux):
    width = 2 * FEAT
    columns = by_column(message[:, : PIECES * width], width)
    tail = message[:, PIECES * width :]
    totals = jnp.sum(tail, axis=0, keepdims=True)
    basis, pixel_weight = aux[:FEAT], aux[FEAT : FEAT + 1]
    both = jnp.zeros((FEAT, PIX), F32)
    wide = jnp.concatenate(
        [jnp.concatenate([basis, both], axis=1), jnp.concatenate([both, basis], axis=1)], axis=0
    )
    logits_tangents = mm_short(columns, wide)
    front, behind = order_masks(jnp.concatenate([tail[:, 0:1], tail[:, 1:2]], axis=0))
    alphas, clears, plain, tangents, lengths = [], [], [], [], []
    for s in range(CAP):
        open_now = None
        length = None
        for r in range(ROWS):
            i = s * ROWS + r
            block = logits_tangents[i * OWNERS : (i + 1) * OWNERS]
            z = block[:, :PIX] - OFFSET
            tangents.append(block[:, PIX:])
            small = jnp.exp(-jnp.abs(z))
            grown = 1.0 + small
            part = 1.0 / grown
            rest = small * part
            alpha = jnp.where(z >= 0.0, part, rest)
            clear = jnp.where(z >= 0.0, rest, part)
            log_clear = -(jnp.maximum(z, 0.0) + jnp.log(grown))
            alphas.append(alpha)
            clears.append(clear)
            plain.append(alpha if open_now is None else alpha * open_now)
            open_now = clear if open_now is None else open_now * clear
            length = log_clear if length is None else length + log_clear
        lengths.append(length)
    ahead = jnp.exp(ordered_sum(front, jnp.concatenate(lengths, axis=0)))
    weights = [
        plain[i] * ahead[(i // ROWS) * OWNERS : (i // ROWS + 1) * OWNERS] for i in range(PIECES)
    ]
    slopes, sums = slope_terms(tangents, alphas, clears)
    ahead_tangent = ordered_sum(front, sums)
    slopes = [
        weights[i]
        * (slopes[i] + ahead_tangent[(i // ROWS) * OWNERS : (i // ROWS + 1) * OWNERS])
        for i in range(PIECES)
    ]
    prim_cols = columns[:FEAT]
    change = image_change(
        columns,
        jnp.concatenate(
            [jnp.concatenate(weights, axis=0), jnp.concatenate(slopes, axis=0)], axis=1
        ),
    )
    colour = change * pixel_weight
    back = pull_back(prim_cols, basis, colour, alphas, clears, weights, behind)
    out = jnp.concatenate(
        [back, lanes([total(colour * change)], OWNERS)], axis=1
    )
    return (
        out,
        jnp.concatenate(alphas, axis=0),
        jnp.concatenate(clears, axis=0),
        jnp.concatenate(weights, axis=0),
        prim_cols,
        front,
        behind,
        change,
        totals,
    )


def pieces_of(array):
    return [array[i * OWNERS : (i + 1) * OWNERS] for i in range(PIECES)]


def render_again(
    message, aux, alphas, clears, weights, prim_cols, front, behind, change0, totals0
):
    columns = by_column(message[:, : PIECES * FEAT], FEAT)
    totals = jnp.sum(message[:, PIECES * FEAT :], axis=0, keepdims=True)
    basis, pixel_weight = aux[:FEAT], aux[FEAT : FEAT + 1]
    tangents = pieces_of(mm_short(columns, basis))
    alphas, clears, weight_list = pieces_of(alphas), pieces_of(clears), pieces_of(weights)
    slopes, sums = slope_terms(tangents, alphas, clears)
    ahead_tangent = ordered_sum(front, sums)
    slopes = [
        weight_list[i]
        * (slopes[i] + ahead_tangent[(i // ROWS) * OWNERS : (i // ROWS + 1) * OWNERS])
        for i in range(PIECES)
    ]
    ratio = totals[:, 0:1] / totals0[:, 2:3]
    change = (
        image_change(
            jnp.concatenate([prim_cols, columns], axis=0),
            jnp.concatenate([weights, jnp.concatenate(slopes, axis=0)], axis=1),
        )
        + ratio * change0
    )
    colour = change * pixel_weight
    back = pull_back(prim_cols, basis, colour, alphas, clears, weight_list, behind)
    out = jnp.concatenate([back, lanes([total(colour * change)], OWNERS)], axis=1)
    return out, totals


def collect(views, message, select, proj):
    columns = by_column(message[:, : PIECES * FEAT], FEAT)
    high, low = split(columns)
    wide = mm(jnp.concatenate([high, low], axis=0), select)
    gathered = wide[:FEAT] + wide[FEAT:]
    tail = jnp.sum(message[:, PIECES * FEAT :], axis=0, keepdims=True)
    turned = jnp.concatenate([proj[:ROWS, : PIX // 2], proj[ROWS:, : PIX // 2]], axis=1)
    turned = jnp.where(iota((ROWS, PIX), 1) == PIX - 1, tail[:, 0:1], turned)
    parts = [gathered[:, j : j + PIX] for j in range(0, GAUSS, PIX)]
    part = jnp.concatenate(parts + [turned], axis=0)
    return jnp.broadcast_to(part[None], (views,) + part.shape)


def product_of(message):
    views = message.shape[0]
    count = GAUSS // PIX
    gathered = jnp.concatenate(
        [
            jnp.concatenate(
                [
                    message[:, j * FEAT + h : j * FEAT + h + ROWS].reshape(views * ROWS, PIX)
                    for j in range(count)
                ],
                axis=1,
            )
            for h in (0, ROWS)
        ],
        axis=0,
    )
    last = message[:, count * FEAT :].reshape(views * ROWS, PIX)
    turned = jnp.concatenate([last[:, : PIX // 2], last[:, PIX // 2 :]], axis=0).T
    th, tl = split(turned)
    wide = jnp.concatenate(
        [
            jnp.concatenate([th, th], axis=1),
            jnp.concatenate([tl, jnp.zeros(tl.shape, BF16)], axis=1),
        ],
        axis=0,
    )
    product = mm(wide, jnp.concatenate(split(gathered), axis=0))
    half = PIX // 2
    product = (product[:half] + product[half:])[:PARAMS]
    energy = jnp.sum(last, axis=0, keepdims=True)[:, PIX - 1 :] * (1.0 / ROWS)
    return product, energy


def step_first(message, right, damp, proj, select, totals0):
    product, energy = product_of(message)
    product = product + damp * right
    step = totals0[:, 2:3] / (energy + totals0[:, 3:4])
    residual = right - step * product
    weighted = damp * residual
    feats = project(proj[:, : PIX // 2], residual)
    tail = lanes(
        [total(residual * residual), total(weighted * residual), total(weighted * right)], OWNERS
    )
    out = jnp.concatenate([to_message([feats], select), tail], axis=1)
    return out, residual, jnp.broadcast_to(step, (1, PIX))


def finish_kernel(
    message, right_ref, damp_ref, residual_ref, step, totals0, totals1,
    solution_hbm, final_hbm, solution, final, sems,
):
    product, energy = product_of(message[...])
    totals0, totals1 = totals0[...], totals1[...]
    right, residual = right_ref[...], residual_ref[...]
    ratio = totals1[:, 0:1] / totals0[:, 2:3]
    direction = residual + ratio * right
    damped = totals1[:, 1:2] + 2.0 * ratio * totals1[:, 2:3] + ratio * ratio * totals0[:, 3:4]
    step_now = totals1[:, 0:1] / (energy + damped)
    solution[...] = step[:, 0:1] * right + step_now * direction
    first = pltpu.make_async_copy(solution, solution_hbm, sems.at[0])
    first.start()
    final[...] = residual - step_now * (product + damp_ref[...] * direction)
    second = pltpu.make_async_copy(final, final_hbm, sems.at[1])
    second.start()
    first.wait()
    second.wait()


def finish(*args):
    shape = (PARAMS, GAUSS)
    return pl.pallas_call(
        finish_kernel,
        out_shape=[jax.ShapeDtypeStruct(shape, F32)] * 2,
        in_specs=[pl.BlockSpec(memory_space=pltpu.VMEM)] * len(args),
        out_specs=[pl.BlockSpec(memory_space=pltpu.HBM)] * 2,
        scratch_shapes=[pltpu.VMEM(shape, F32)] * 2 + [pltpu.SemaphoreType.DMA((2,))],
        compiler_params=pltpu.CompilerParams(vmem_limit_bytes=40 * 1024 * 1024),
        name="finish",
    )(*args)


def call(function, outs, *args):
    def kernel(*refs):
        results = function(*[ref[:, 0, :] if len(ref.shape) == 3 and ref.shape[1] == 1 else ref[...] for ref in refs[: len(args)]])
        if len(outs) == 1:
            results = (results,) if not isinstance(results, tuple) else results
        for ref, result in zip(refs[len(args) :], results):
            if result.ndim == 2 and len(ref.shape) == 3:
                ref[:, 0, :] = result
            else:
                ref[...] = result

    result = pl.pallas_call(
        kernel,
        out_shape=[jax.ShapeDtypeStruct(shape, dtype) for shape, dtype in outs],
        in_specs=[pl.BlockSpec(memory_space=pltpu.VMEM)] * len(args),
        out_specs=[pl.BlockSpec(memory_space=pltpu.VMEM)] * len(outs),
        compiler_params=pltpu.CompilerParams(vmem_limit_bytes=40 * 1024 * 1024),
        name=function.__name__,
    )(*args)
    return result


def body(
    linear_point,
    right_side,
    damping,
    projection,
    pixel_basis,
    pixel_weight,
    depth_order,
    tile_dest,
    block_depth,
):
    dest = tile_dest.reshape(1, -1)
    views = lax.axis_size("views")
    rows = PIECES * OWNERS
    slots = CAP * OWNERS

    def over_tiles(message):
        return lax.all_to_all(message, "tiles", split_axis=0, concat_axis=0, tiled=True)

    def over_views(part):
        return lax.all_to_all(part, "views", split_axis=0, concat_axis=0, tiled=True)

    message, select, aux, proj = begin(
        linear_point, right_side, damping, jnp.swapaxes(projection, 1, 2)[0],
        pixel_basis.reshape(FEAT - 4, 1, PIX), pixel_weight[0], depth_order[0], dest, block_depth,
    )
    short = ((OWNERS, 1, PIECES * FEAT + PIX), F32)
    message, alphas, clears, weights, prim, front, behind, change, totals0 = call(
        render_first,
        [short]
        + [((rows, PIX), F32)] * 3
        + [((FEAT, rows), F32)]
        + [((slots, slots), BF16)] * 2
        + [((FEAT, PIX), F32), ((1, PIX), F32)],
        over_tiles(message), aux,
    )
    part_shape = ((views, GAUSS // PIX * FEAT + ROWS, PIX), F32)
    gather = functools.partial(collect, views)
    gather.__name__ = "collect"
    (part,) = call(gather, [part_shape], over_tiles(message), select, proj)
    message, residual, step = call(
        step_first,
        [short, ((PARAMS, GAUSS), F32), ((1, PIX), F32)],
        over_views(part), right_side, damping, proj, select, totals0,
    )
    message, totals1 = call(
        render_again,
        [short, ((1, PIX), F32)],
        over_tiles(message), aux, alphas, clears, weights, prim, front, behind, change, totals0,
    )
    (part,) = call(gather, [part_shape], over_tiles(message), select, proj)
    return tuple(
        finish(over_views(part), right_side, damping, residual, step, totals0, totals1)
    )


def solution(mesh):
    in_specs = (
        P(None, "tiles"),
        P(None, "tiles"),
        P(None, "tiles"),
        P("views", None, None),
        P("views", "tiles", None, None),
        P("views", "tiles", None),
        P("views", "tiles", None),
        P("views", "tiles", None),
        P("views", "tiles"),
    )
    out_specs = (P(None, "tiles"), P(None, "tiles"))
    return jax.shard_map(body, mesh=mesh, in_specs=in_specs, out_specs=out_specs, check_vma=False)
```

```python
import functools

import jax
import jax.numpy as jnp
from jax import lax
from jax.experimental import pallas as pl
from jax.experimental.pallas import tpu as pltpu
from jax.sharding import PartitionSpec as P

OFFSET = 6.0
PARAMS = 59
FEAT = 16
ROWS = 8
CAP = 2
PIECES = CAP * ROWS
OWNERS = 64
GAUSS = 512
PIX = 128
F32 = jnp.float32
BF16 = jnp.bfloat16

NN = (((1,), (0,)), ((), ()))
NT = (((1,), (1,)), ((), ()))
TN = (((0,), (0,)), ((), ()))


def iota(shape, axis):
    return lax.broadcasted_iota(jnp.int32, shape, axis)


def mm(a, b, dims=NN):
    return lax.dot_general(a, b, dims, preferred_element_type=F32)


def split(x):
    high = x.astype(BF16)
    low = (x - high.astype(F32)).astype(BF16)
    return high, low


def mm_short(a, b):
    ah, al = split(a)
    bh, bl = split(b)
    return mm(jnp.concatenate([ah, al, ah], axis=0), jnp.concatenate([bh, bh, bl], axis=0), TN)


def project(proj, vectors):
    tall = jnp.concatenate([vectors, jnp.zeros((PIX // 2 - PARAMS, vectors.shape[1]), F32)], axis=0)
    ph, pl_ = split(proj)
    th, tl = split(tall)
    return mm(jnp.concatenate([ph, pl_, ph], axis=1), jnp.concatenate([th, th, tl], axis=0))


def total(x):
    return jnp.sum(jnp.sum(x, axis=1, keepdims=True), axis=0, keepdims=True)


def lanes(values, rows):
    lane = iota((rows, PIX), 1)
    out = jnp.zeros((rows, PIX), F32)
    for i, value in enumerate(values):
        out = jnp.where(lane == i, value, out)
    return out


def to_message(feats, select):
    stacked = jnp.concatenate(feats, axis=0)
    rows = stacked.shape[0]
    both = mm(jnp.concatenate(split(stacked), axis=0), select, NT)
    slots = both[:rows] + both[rows:]
    return by_owner(slots)


def by_owner(slots):
    pieces = [slots[:, i * OWNERS : (i + 1) * OWNERS] for i in range(PIECES)]
    return jnp.concatenate(pieces, axis=0).T


def by_column(message, width):
    turned = message.T
    return jnp.concatenate([turned[i * width : (i + 1) * width] for i in range(PIECES)], axis=1)


def choose(order, dest):
    blocks = dest.shape[1]
    mine = iota((OWNERS, blocks), 0) == dest
    mine_f = jnp.where(mine, 1.0, 0.0)
    earlier = jnp.where(iota((blocks, blocks), 0) < iota((blocks, blocks), 1), 1.0, 0.0)
    count = mm(mine_f.astype(BF16), earlier.astype(BF16))
    owns = [jnp.where(mine & (count == float(s)), 1.0, 0.0) for s in range(CAP)]
    own_all = jnp.concatenate(owns, axis=0).astype(BF16)
    here = iota((blocks, GAUSS), 1) // ROWS == iota((blocks, GAUSS), 0)
    number = jnp.where(here, order + 1, 0)
    parts = jnp.concatenate(
        [(number // 16).astype(F32), (number % 16).astype(F32)], axis=0
    ).astype(BF16)
    pick = jnp.where(iota((GAUSS, PIX), 0) % ROWS == iota((GAUSS, PIX), 1), 1.0, 0.0).astype(BF16)
    table = mm(parts, pick).astype(BF16)
    ids = mm(own_all, table[:blocks]) * 16.0 + mm(own_all, table[blocks:])
    return owns, ids


def chosen_rows(ids):
    columns = (iota((OWNERS, GAUSS), 1) + 1).astype(F32)
    rows = []
    for s in range(CAP):
        for r in range(ROWS):
            chosen = ids[s * OWNERS : (s + 1) * OWNERS, r : r + 1] == columns
            rows.append(jnp.where(chosen, 1.0, 0.0).astype(BF16))
    return jnp.concatenate(rows, axis=0)


def begin_kernel(
    point_hbm, right_hbm, damp_hbm, proj_hbm, basis_hbm, weight_hbm, order_hbm, dest_hbm, depth_hbm,
    message_ref, select_ref, aux_ref, proj_ref,
    point, right, damp, proj, basis, weight, order, dest, depth, sems,
):
    pairs = [
        (order_hbm, order), (dest_hbm, dest), (depth_hbm, depth), (proj_hbm, proj),
        (point_hbm, point), (right_hbm, right), (damp_hbm, damp), (basis_hbm, basis), (weight_hbm, weight),
    ]
    copies = [pltpu.make_async_copy(a, b, sems.at[i]) for i, (a, b) in enumerate(pairs)]
    for copy in copies:
        copy.start()
    for copy in copies[:3]:
        copy.wait()
    owns, ids = choose(order[...], dest[...])
    depth_f = depth[...].astype(F32) + 1.0
    marks = [jnp.sum(own * depth_f, axis=1, keepdims=True) for own in owns]
    for copy in copies[3:7]:
        copy.wait()
    right_now = right[...]
    padded = jnp.concatenate([proj[...], jnp.zeros((FEAT, PIX - PARAMS), F32)], axis=1)
    proj_ref[...] = padded
    feats = project(padded[:, : PIX // 2], jnp.concatenate([point[...], right_now], axis=1))
    select = chosen_rows(ids)
    select_ref[...] = select
    message = to_message([feats[:, :GAUSS], feats[:, GAUSS:]], select)
    squared = right_now * right_now
    tail = lanes(marks + [total(squared), total(damp[...] * squared)], OWNERS)
    message_ref[:, 0, :] = jnp.concatenate([message, tail], axis=1)
    for copy in copies[7:]:
        copy.wait()
    first = jnp.where(iota((4, PIX), 0) == 0, 1.0, 0.0)
    last = jnp.broadcast_to(weight[...], (8, PIX))
    aux_ref[...] = jnp.concatenate([first, basis[:, 0, :], last], axis=0)


def begin(*args):
    rows = PIECES * OWNERS
    return pl.pallas_call(
        begin_kernel,
        out_shape=[
            jax.ShapeDtypeStruct((OWNERS, 1, PIECES * 2 * FEAT + PIX), F32),
            jax.ShapeDtypeStruct((rows, GAUSS), BF16),
            jax.ShapeDtypeStruct((FEAT + 8, PIX), F32),
            jax.ShapeDtypeStruct((FEAT, PIX), F32),
        ],
        in_specs=[pl.BlockSpec(memory_space=pltpu.HBM)] * len(args),
        out_specs=[pl.BlockSpec(memory_space=pltpu.VMEM)] * 4,
        scratch_shapes=[pltpu.VMEM(x.shape, x.dtype) for x in args]
        + [pltpu.SemaphoreType.DMA((len(args),))],
        compiler_params=pltpu.CompilerParams(vmem_limit_bytes=40 * 1024 * 1024),
        name="begin",
    )(*[pltpu.with_memory_space_constraint(x, pltpu.HBM) for x in args])


def order_masks(marks):
    side = CAP * OWNERS
    by_row = jnp.broadcast_to(marks, (side, side))
    diagonal = iota((side, side), 0) == iota((side, side), 1)
    by_lane = jnp.sum(jnp.where(diagonal, by_row, 0.0), axis=0, keepdims=True)
    front = jnp.where((by_lane < by_row) & (by_lane > 0.0), 1.0, 0.0)
    behind = jnp.where((by_row < by_lane) & (by_row > 0.0), 1.0, 0.0)
    return front.astype(BF16), behind.astype(BF16)


def ordered_sum(mask, value):
    high, low = split(value)
    return mm(jnp.concatenate([mask, mask], axis=1), jnp.concatenate([high, low], axis=0))


def image_change(columns, both):
    high, low = split(columns)
    bh, bl = split(both)
    main = mm(jnp.concatenate([high, low], axis=0), bh)
    rest = mm(high, bl)
    change = (
        main[FEAT : 2 * FEAT, :PIX]
        + main[3 * FEAT :, :PIX]
        + rest[FEAT:, :PIX]
        + main[:FEAT, PIX:]
        + main[2 * FEAT : 3 * FEAT, PIX:]
        + rest[:FEAT, PIX:]
    )
    return colours_only(change)


def change_of(columns, values):
    high, low = split(columns)
    vh, vl = split(values)
    main = mm(jnp.concatenate([high, low], axis=0), vh)
    return main[:FEAT] + main[FEAT:] + mm(high, vl)


def colours_only(change):
    row = iota((FEAT, PIX), 0)
    return jnp.where((row >= 1) & (row < 4), change, 0.0)


def pull_back(prim_cols, basis, colour, alphas, clears, weights, behind):
    shade = mm_short(prim_cols, colour)
    pulls = [weights[i] * shade[i * OWNERS : (i + 1) * OWNERS] for i in range(PIECES)]
    sums = []
    for s in range(CAP):
        acc = pulls[s * ROWS]
        for r in range(1, ROWS):
            acc = acc + pulls[s * ROWS + r]
        sums.append(acc)
    through = ordered_sum(behind, jnp.concatenate(sums, axis=0))
    logits = [None] * PIECES
    for s in range(CAP):
        acc = through[s * OWNERS : (s + 1) * OWNERS]
        for r in reversed(range(ROWS)):
            i = s * ROWS + r
            logits[i] = clears[i] * pulls[i] - alphas[i] * acc
            acc = acc + pulls[i]
    def over_pixels(first, second):
        high, low = split(second)
        fh, fl = split(first)
        main = mm(jnp.concatenate([fh, fl], axis=0), high, NT)
        return main[:FEAT] + main[FEAT:] + mm(fh, low, NT)

    early = over_pixels(colour, jnp.concatenate(weights, axis=0))
    return by_owner(early + over_pixels(basis, jnp.concatenate(logits, axis=0)))


def slope_terms(tangents, alphas, clears):
    slopes = []
    sums = []
    for s in range(CAP):
        acc = jnp.zeros((OWNERS, PIX), F32)
        for r in range(ROWS):
            i = s * ROWS + r
            slopes.append(clears[i] * tangents[i] + acc)
            acc = acc - alphas[i] * tangents[i]
        sums.append(acc)
    return slopes, jnp.concatenate(sums, axis=0)


def render_first(message, aux):
    width = 2 * FEAT
    columns = by_column(message[:, : PIECES * width], width)
    tail = message[:, PIECES * width :]
    totals = jnp.sum(tail, axis=0, keepdims=True)
    basis, pixel_weight = aux[:FEAT], aux[FEAT : FEAT + 1]
    both = jnp.zeros((FEAT, PIX), F32)
    wide = jnp.concatenate(
        [jnp.concatenate([basis, both], axis=1), jnp.concatenate([both, basis], axis=1)], axis=0
    )
    logits_tangents = mm_short(columns, wide)
    front, behind = order_masks(jnp.concatenate([tail[:, 0:1], tail[:, 1:2]], axis=0))
    alphas, clears, plain, tangents, lengths = [], [], [], [], []
    for s in range(CAP):
        open_now = None
        length = None
        for r in range(ROWS):
            i = s * ROWS + r
            block = logits_tangents[i * OWNERS : (i + 1) * OWNERS]
            z = block[:, :PIX] - OFFSET
            tangents.append(block[:, PIX:])
            small = jnp.exp(-jnp.abs(z))
            grown = 1.0 + small
            part = 1.0 / grown
            rest = small * part
            alpha = jnp.where(z >= 0.0, part, rest)
            clear = jnp.where(z >= 0.0, rest, part)
            log_clear = -(jnp.maximum(z, 0.0) + jnp.log(grown))
            alphas.append(alpha)
            clears.append(clear)
            plain.append(alpha if open_now is None else alpha * open_now)
            open_now = clear if open_now is None else open_now * clear
            length = log_clear if length is None else length + log_clear
        lengths.append(length)
    ahead = jnp.exp(ordered_sum(front, jnp.concatenate(lengths, axis=0)))
    weights = [
        plain[i] * ahead[(i // ROWS) * OWNERS : (i // ROWS + 1) * OWNERS] for i in range(PIECES)
    ]
    slopes, sums = slope_terms(tangents, alphas, clears)
    ahead_tangent = ordered_sum(front, sums)
    slopes = [
        weights[i]
        * (slopes[i] + ahead_tangent[(i // ROWS) * OWNERS : (i // ROWS + 1) * OWNERS])
        for i in range(PIECES)
    ]
    prim_cols = columns[:FEAT]
    change = image_change(
        columns,
        jnp.concatenate(
            [jnp.concatenate(weights, axis=0), jnp.concatenate(slopes, axis=0)], axis=1
        ),
    )
    colour = change * pixel_weight
    back = pull_back(prim_cols, basis, colour, alphas, clears, weights, behind)
    out = jnp.concatenate(
        [back, lanes([total(colour * change)], OWNERS)], axis=1
    )
    return (
        out,
        jnp.concatenate(alphas, axis=0),
        jnp.concatenate(clears, axis=0),
        jnp.concatenate(weights, axis=0),
        prim_cols,
        front,
        behind,
        change,
        totals,
    )


def pieces_of(array):
    return [array[i * OWNERS : (i + 1) * OWNERS] for i in range(PIECES)]


def render_again(
    message, aux, alphas, clears, weights, prim_cols, front, behind, change0, totals0
):
    columns = by_column(message[:, : PIECES * FEAT], FEAT)
    totals = jnp.sum(message[:, PIECES * FEAT :], axis=0, keepdims=True)
    basis, pixel_weight = aux[:FEAT], aux[FEAT : FEAT + 1]
    tangents = pieces_of(mm_short(columns, basis))
    alphas, clears, weight_list = pieces_of(alphas), pieces_of(clears), pieces_of(weights)
    slopes, sums = slope_terms(tangents, alphas, clears)
    ahead_tangent = ordered_sum(front, sums)
    slopes = [
        weight_list[i]
        * (slopes[i] + ahead_tangent[(i // ROWS) * OWNERS : (i // ROWS + 1) * OWNERS])
        for i in range(PIECES)
    ]
    ratio = totals[:, 0:1] / totals0[:, 2:3]
    change = (
        colours_only(
            change_of(columns, weights) + change_of(prim_cols, jnp.concatenate(slopes, axis=0))
        )
        + ratio * change0
    )
    colour = change * pixel_weight
    back = pull_back(prim_cols, basis, colour, alphas, clears, weight_list, behind)
    out = jnp.concatenate([back, lanes([total(colour * change)], OWNERS)], axis=1)
    return out, totals


def gathered_parts(message, select):
    columns = by_column(message[:, : PIECES * FEAT], FEAT)
    high, low = split(columns)
    wide = mm(jnp.concatenate([high, low], axis=0), select)
    gathered = wide[:FEAT] + wide[FEAT:]
    tail = jnp.sum(message[:, PIECES * FEAT :], axis=0, keepdims=True)
    return [gathered[:, j : j + PIX] for j in range(0, GAUSS, PIX)], tail


def collect(views, message, select, proj):
    parts, tail = gathered_parts(message, select)
    turned = jnp.concatenate([proj[:ROWS, : PIX // 2], proj[ROWS:, : PIX // 2]], axis=1)
    turned = jnp.where(iota((ROWS, PIX), 1) == PIX - 1, tail[:, 0:1], turned)
    part = jnp.concatenate(parts + [turned], axis=0)
    return jnp.broadcast_to(part[None], (views,) + part.shape)


def collect_last(views, message, select):
    parts, tail = gathered_parts(message, select)
    part = jnp.concatenate(parts + [tail], axis=0)
    return jnp.broadcast_to(part[None], (views,) + part.shape)


def turned_pair(message):
    views = message.shape[0]
    last = message[:, GAUSS // PIX * FEAT :].reshape(views * ROWS, PIX)
    turned = jnp.concatenate([last[:, : PIX // 2], last[:, PIX // 2 :]], axis=0).T
    th, tl = split(turned)
    wide = jnp.concatenate(
        [
            jnp.concatenate([th, th], axis=1),
            jnp.concatenate([tl, jnp.zeros(tl.shape, BF16)], axis=1),
        ],
        axis=0,
    )
    energy = jnp.sum(last, axis=0, keepdims=True)[:, PIX - 1 :] * (1.0 / ROWS)
    return wide, energy


def product_of(message, wide):
    views = message.shape[0]
    gathered = jnp.concatenate(
        [
            jnp.concatenate(
                [
                    message[:, j * FEAT + h : j * FEAT + h + ROWS].reshape(views * ROWS, PIX)
                    for j in range(GAUSS // PIX)
                ],
                axis=1,
            )
            for h in (0, ROWS)
        ],
        axis=0,
    )
    product = mm(wide, jnp.concatenate(split(gathered), axis=0))
    half = PIX // 2
    return (product[:half] + product[half:])[:PARAMS]


def step_first(message, right, damp, proj, select, totals0):
    wide, energy = turned_pair(message)
    product = product_of(message, wide) + damp * right
    step = totals0[:, 2:3] / (energy + totals0[:, 3:4])
    residual = right - step * product
    weighted = damp * residual
    feats = project(proj[:, : PIX // 2], residual)
    tail = lanes(
        [total(residual * residual), total(weighted * residual), total(weighted * right)], OWNERS
    )
    out = jnp.concatenate([to_message([feats], select), tail], axis=1)
    return out, residual, jnp.broadcast_to(step, (1, PIX)), wide


def finish_kernel(
    message_ref, right_ref, damp_ref, residual_ref, step, wide, totals0, totals1,
    solution_hbm, final_hbm, solution, final, sems,
):
    message = message_ref[:, :, 0, :]
    product = product_of(message, wide[...])
    energy = jnp.sum(message[:, GAUSS // PIX * FEAT], axis=0, keepdims=True)[:, 0:1]
    totals0, totals1 = totals0[...], totals1[...]
    right, residual = right_ref[...], residual_ref[...]
    ratio = totals1[:, 0:1] / totals0[:, 2:3]
    direction = residual + ratio * right
    damped = totals1[:, 1:2] + 2.0 * ratio * totals1[:, 2:3] + ratio * ratio * totals0[:, 3:4]
    step_now = totals1[:, 0:1] / (energy + damped)
    solution[...] = step[:, 0:1] * right + step_now * direction
    first = pltpu.make_async_copy(solution, solution_hbm, sems.at[0])
    first.start()
    final[...] = residual - step_now * (product + damp_ref[...] * direction)
    second = pltpu.make_async_copy(final, final_hbm, sems.at[1])
    second.start()
    first.wait()
    second.wait()


def finish(*args):
    shape = (PARAMS, GAUSS)
    return pl.pallas_call(
        finish_kernel,
        out_shape=[jax.ShapeDtypeStruct(shape, F32)] * 2,
        in_specs=[pl.BlockSpec(memory_space=pltpu.VMEM)] * len(args),
        out_specs=[pl.BlockSpec(memory_space=pltpu.HBM)] * 2,
        scratch_shapes=[pltpu.VMEM(shape, F32)] * 2 + [pltpu.SemaphoreType.DMA((2,))],
        compiler_params=pltpu.CompilerParams(vmem_limit_bytes=40 * 1024 * 1024),
        name="finish",
    )(*args)


def call(function, outs, *args):
    def kernel(*refs):
        results = function(*[ref[:, 0, :] if len(ref.shape) == 3 and ref.shape[1] == 1 else ref[...] for ref in refs[: len(args)]])
        if len(outs) == 1:
            results = (results,) if not isinstance(results, tuple) else results
        for ref, result in zip(refs[len(args) :], results):
            if result.ndim < len(ref.shape):
                ref[..., 0, :] = result
            else:
                ref[...] = result

    result = pl.pallas_call(
        kernel,
        out_shape=[jax.ShapeDtypeStruct(shape, dtype) for shape, dtype in outs],
        in_specs=[pl.BlockSpec(memory_space=pltpu.VMEM)] * len(args),
        out_specs=[pl.BlockSpec(memory_space=pltpu.VMEM)] * len(outs),
        compiler_params=pltpu.CompilerParams(vmem_limit_bytes=40 * 1024 * 1024),
        name=function.__name__,
    )(*args)
    return result


def body(
    linear_point,
    right_side,
    damping,
    projection,
    pixel_basis,
    pixel_weight,
    depth_order,
    tile_dest,
    block_depth,
):
    dest = tile_dest.reshape(1, -1)
    views = lax.axis_size("views")
    rows = PIECES * OWNERS
    slots = CAP * OWNERS

    def over_tiles(message):
        return lax.all_to_all(message, "tiles", split_axis=0, concat_axis=0, tiled=True)

    def over_views(part):
        return lax.all_to_all(part, "views", split_axis=0, concat_axis=0, tiled=True)

    message, select, aux, proj = begin(
        linear_point, right_side, damping, jnp.swapaxes(projection, 1, 2)[0],
        pixel_basis.reshape(FEAT - 4, 1, PIX), pixel_weight[0], depth_order[0], dest, block_depth,
    )
    short = ((OWNERS, 1, PIECES * FEAT + PIX), F32)
    message, alphas, clears, weights, prim, front, behind, change, totals0 = call(
        render_first,
        [short]
        + [((rows, PIX), F32)] * 3
        + [((FEAT, rows), F32)]
        + [((slots, slots), BF16)] * 2
        + [((FEAT, PIX), F32), ((1, PIX), F32)],
        over_tiles(message), aux,
    )
    part_shape = ((views, GAUSS // PIX * FEAT + ROWS, PIX), F32)
    gather = functools.partial(collect, views)
    gather.__name__ = "collect"
    (part,) = call(gather, [part_shape], over_tiles(message), select, proj)
    message, residual, step, wide = call(
        step_first,
        [short, ((PARAMS, GAUSS), F32), ((1, PIX), F32), ((PIX, 2 * views * FEAT), BF16)],
        over_views(part), right_side, damping, proj, select, totals0,
    )
    message, totals1 = call(
        render_again,
        [short, ((1, PIX), F32)],
        over_tiles(message), aux, alphas, clears, weights, prim, front, behind, change, totals0,
    )
    gather = functools.partial(collect_last, views)
    gather.__name__ = "collect_last"
    last_shape = ((views, GAUSS // PIX * FEAT + 1, 1, PIX), F32)
    (part,) = call(gather, [last_shape], over_tiles(message), select)
    return tuple(
        finish(over_views(part), right_side, damping, residual, step, wide, totals0, totals1)
    )


def solution(mesh):
    in_specs = (
        P(None, "tiles"),
        P(None, "tiles"),
        P(None, "tiles"),
        P("views", None, None),
        P("views", "tiles", None, None),
        P("views", "tiles", None),
        P("views", "tiles", None),
        P("views", "tiles", None),
        P("views", "tiles"),
    )
    out_specs = (P(None, "tiles"), P(None, "tiles"))
    return jax.shard_map(body, mesh=mesh, in_specs=in_specs, out_specs=out_specs, check_vma=False)
```

```python
import functools

import jax
import jax.numpy as jnp
from jax import lax
from jax.experimental import pallas as pl
from jax.experimental.pallas import tpu as pltpu
from jax.sharding import PartitionSpec as P

OFFSET = 6.0
PARAMS = 59
FEAT = 16
ROWS = 8
CAP = 2
PIECES = CAP * ROWS
OWNERS = 64
GAUSS = 512
PIX = 128
F32 = jnp.float32
BF16 = jnp.bfloat16

NN = (((1,), (0,)), ((), ()))
NT = (((1,), (1,)), ((), ()))
TN = (((0,), (0,)), ((), ()))


def iota(shape, axis):
    return lax.broadcasted_iota(jnp.int32, shape, axis)


def mm(a, b, dims=NN):
    return lax.dot_general(a, b, dims, preferred_element_type=F32)


def split(x):
    high = x.astype(BF16)
    low = (x - high.astype(F32)).astype(BF16)
    return high, low


def mm_short(a, b):
    ah, al = split(a)
    bh, bl = split(b)
    return mm(jnp.concatenate([ah, al, ah], axis=0), jnp.concatenate([bh, bh, bl], axis=0), TN)


def project(proj, vectors):
    tall = jnp.concatenate([vectors, jnp.zeros((PIX // 2 - PARAMS, vectors.shape[1]), F32)], axis=0)
    ph, pl_ = split(proj)
    th, tl = split(tall)
    return mm(jnp.concatenate([ph, pl_, ph], axis=1), jnp.concatenate([th, th, tl], axis=0))


def total(x):
    return jnp.sum(jnp.sum(x, axis=1, keepdims=True), axis=0, keepdims=True)


def lanes(values, rows):
    lane = iota((rows, PIX), 1)
    out = jnp.zeros((rows, PIX), F32)
    for i, value in enumerate(values):
        out = jnp.where(lane == i, value, out)
    return out


def to_message(feats, select):
    stacked = jnp.concatenate(feats, axis=0)
    fields = [slice(i, i + FEAT) for i in range(0, stacked.shape[0], FEAT)]
    rows = stacked.shape[0]
    both = mm(jnp.concatenate(split(stacked), axis=0), select, NT)
    slots = both[:rows] + both[rows:]
    return jnp.concatenate([by_owner(slots[field]) for field in fields], axis=1)


def by_owner(slots):
    pieces = [slots[:, i * OWNERS : (i + 1) * OWNERS] for i in range(PIECES)]
    return jnp.concatenate(pieces, axis=0).T


def by_column(message, width):
    turned = message.T
    return jnp.concatenate([turned[i * width : (i + 1) * width] for i in range(PIECES)], axis=1)


def choose(order, dest):
    blocks = dest.shape[1]
    mine = iota((OWNERS, blocks), 0) == dest
    mine_f = jnp.where(mine, 1.0, 0.0)
    earlier = jnp.where(iota((blocks, blocks), 0) < iota((blocks, blocks), 1), 1.0, 0.0)
    count = mm(mine_f.astype(BF16), earlier.astype(BF16))
    owns = [jnp.where(mine & (count == float(s)), 1.0, 0.0) for s in range(CAP)]
    own_all = jnp.concatenate(owns, axis=0).astype(BF16)
    here = iota((blocks, GAUSS), 1) // ROWS == iota((blocks, GAUSS), 0)
    number = jnp.where(here, order + 1, 0)
    parts = jnp.concatenate(
        [(number // 16).astype(F32), (number % 16).astype(F32)], axis=0
    ).astype(BF16)
    pick = jnp.where(iota((GAUSS, PIX), 0) % ROWS == iota((GAUSS, PIX), 1), 1.0, 0.0).astype(BF16)
    table = mm(parts, pick).astype(BF16)
    ids = mm(own_all, table[:blocks]) * 16.0 + mm(own_all, table[blocks:])
    return owns, ids


def chosen_rows(ids):
    columns = (iota((OWNERS, GAUSS), 1) + 1).astype(F32)
    rows = []
    for s in range(CAP):
        for r in range(ROWS):
            chosen = ids[s * OWNERS : (s + 1) * OWNERS, r : r + 1] == columns
            rows.append(jnp.where(chosen, 1.0, 0.0).astype(BF16))
    return jnp.concatenate(rows, axis=0)


def begin_kernel(
    point_hbm, right_hbm, proj_hbm, basis_hbm, weight_hbm, order_hbm, dest_hbm, depth_hbm,
    message_ref, select_ref, aux_ref, proj_ref,
    point, right, proj, basis, weight, order, dest, depth, sems,
):
    pairs = [
        (order_hbm, order), (dest_hbm, dest), (depth_hbm, depth), (proj_hbm, proj),
        (point_hbm, point), (right_hbm, right), (basis_hbm, basis), (weight_hbm, weight),
    ]
    copies = [pltpu.make_async_copy(a, b, sems.at[i]) for i, (a, b) in enumerate(pairs)]
    for copy in copies:
        copy.start()
    for copy in copies[:3]:
        copy.wait()
    owns, ids = choose(order[...], dest[...])
    depth_f = depth[...].astype(F32) + 1.0
    marks = [jnp.sum(own * depth_f, axis=1, keepdims=True) for own in owns]
    for copy in copies[3:6]:
        copy.wait()
    right_now = right[...]
    padded = jnp.concatenate([proj[...], jnp.zeros((FEAT, PIX - PARAMS), F32)], axis=1)
    proj_ref[...] = padded
    feats = project(padded[:, : PIX // 2], jnp.concatenate([point[...], right_now], axis=1))
    select = chosen_rows(ids)
    select_ref[...] = select
    message = to_message([feats[:, :GAUSS], feats[:, GAUSS:]], select)
    tail = lanes(marks, OWNERS)
    message_ref[:, 0, :] = jnp.concatenate([message, tail], axis=1)
    for copy in copies[6:]:
        copy.wait()
    first = jnp.where(iota((4, PIX), 0) == 0, 1.0, 0.0)
    last = jnp.broadcast_to(weight[...], (8, PIX))
    aux_ref[...] = jnp.concatenate([first, basis[:, 0, :], last], axis=0)


def begin(*args):
    rows = PIECES * OWNERS
    return pl.pallas_call(
        begin_kernel,
        out_shape=[
            jax.ShapeDtypeStruct((OWNERS, 1, PIECES * 2 * FEAT + PIX), F32),
            jax.ShapeDtypeStruct((rows, GAUSS), BF16),
            jax.ShapeDtypeStruct((FEAT + 8, PIX), F32),
            jax.ShapeDtypeStruct((FEAT, PIX), F32),
        ],
        in_specs=[pl.BlockSpec(memory_space=pltpu.HBM)] * len(args),
        out_specs=[pl.BlockSpec(memory_space=pltpu.VMEM)] * 4,
        scratch_shapes=[pltpu.VMEM(x.shape, x.dtype) for x in args]
        + [pltpu.SemaphoreType.DMA((len(args),))],
        compiler_params=pltpu.CompilerParams(vmem_limit_bytes=40 * 1024 * 1024),
        name="begin",
    )(*[pltpu.with_memory_space_constraint(x, pltpu.HBM) for x in args])


def order_masks(marks):
    side = CAP * OWNERS
    by_row = jnp.broadcast_to(marks, (side, side))
    diagonal = iota((side, side), 0) == iota((side, side), 1)
    by_lane = jnp.sum(jnp.where(diagonal, by_row, 0.0), axis=0, keepdims=True)
    front = jnp.where((by_lane < by_row) & (by_lane > 0.0), 1.0, 0.0)
    behind = jnp.where((by_row < by_lane) & (by_row > 0.0), 1.0, 0.0)
    return front.astype(BF16), behind.astype(BF16)


def ordered_sum(mask, value):
    high, low = split(value)
    return mm(jnp.concatenate([mask, mask], axis=1), jnp.concatenate([high, low], axis=0))


def image_change(columns, both):
    high, low = split(columns)
    bh, bl = split(both)
    main = mm(jnp.concatenate([high, low], axis=0), bh)
    rest = mm(high, bl)
    change = (
        main[FEAT : 2 * FEAT, :PIX]
        + main[3 * FEAT :, :PIX]
        + rest[FEAT:, :PIX]
        + main[:FEAT, PIX:]
        + main[2 * FEAT : 3 * FEAT, PIX:]
        + rest[:FEAT, PIX:]
    )
    return colours_only(change)


def change_of(columns, values):
    high, low = split(columns)
    vh, vl = split(values)
    main = mm(jnp.concatenate([high, low], axis=0), vh)
    return main[:FEAT] + main[FEAT:] + mm(high, vl)


def colours_only(change):
    row = iota((FEAT, PIX), 0)
    return jnp.where((row >= 1) & (row < 4), change, 0.0)


def pull_back(prim_cols, basis, colour, alphas, clears, weights, blended, behind):
    shade = mm_short(prim_cols, colour)
    pulls = [weights[i] * shade[i * OWNERS : (i + 1) * OWNERS] for i in range(PIECES)]
    sums = sum(colour[1 + c : 2 + c] * blended[:, c * PIX : (c + 1) * PIX] for c in range(3))
    through = ordered_sum(behind, sums)
    logits = [None] * PIECES
    for s in range(CAP):
        acc = through[s * OWNERS : (s + 1) * OWNERS]
        for r in reversed(range(ROWS)):
            i = s * ROWS + r
            logits[i] = clears[i] * pulls[i] - alphas[i] * acc
            acc = acc + pulls[i]
    def over_pixels(first, second):
        high, low = split(second)
        fh, fl = split(first)
        main = mm(jnp.concatenate([fh, fl], axis=0), high, NT)
        return main[:FEAT] + main[FEAT:] + mm(fh, low, NT)

    early = over_pixels(colour, jnp.concatenate(weights, axis=0))
    return by_owner(early + over_pixels(basis, jnp.concatenate(logits, axis=0)))


def slope_terms(tangents, alphas, clears):
    slopes = []
    sums = []
    for s in range(CAP):
        acc = jnp.zeros((OWNERS, PIX), F32)
        for r in range(ROWS):
            i = s * ROWS + r
            slopes.append(clears[i] * tangents[i] + acc)
            acc = acc - alphas[i] * tangents[i]
        sums.append(acc)
    return slopes, jnp.concatenate(sums, axis=0)


def render_first(message, aux):
    width = PIECES * FEAT
    columns = jnp.concatenate(
        [by_column(message[:, :width], FEAT), by_column(message[:, width : 2 * width], FEAT)], axis=0
    )
    tail = message[:, 2 * width :]
    basis, pixel_weight = aux[:FEAT], aux[FEAT : FEAT + 1]
    both = jnp.zeros((FEAT, PIX), F32)
    wide = jnp.concatenate(
        [jnp.concatenate([basis, both], axis=1), jnp.concatenate([both, basis], axis=1)], axis=0
    )
    logits_tangents = mm_short(columns, wide)
    front, behind = order_masks(jnp.concatenate([tail[:, 0:1], tail[:, 1:2]], axis=0))
    alphas, clears, plain, tangents, lengths = [], [], [], [], []
    for s in range(CAP):
        open_now = None
        length = None
        for r in range(ROWS):
            i = s * ROWS + r
            block = logits_tangents[i * OWNERS : (i + 1) * OWNERS]
            z = block[:, :PIX] - OFFSET
            tangents.append(block[:, PIX:])
            small = jnp.exp(-jnp.abs(z))
            grown = 1.0 + small
            part = 1.0 / grown
            rest = small * part
            alpha = jnp.where(z >= 0.0, part, rest)
            clear = jnp.where(z >= 0.0, rest, part)
            log_clear = -(jnp.maximum(z, 0.0) + jnp.log(grown))
            alphas.append(alpha)
            clears.append(clear)
            plain.append(alpha if open_now is None else alpha * open_now)
            open_now = clear if open_now is None else open_now * clear
            length = log_clear if length is None else length + log_clear
        lengths.append(length)
    ahead = jnp.exp(ordered_sum(front, jnp.concatenate(lengths, axis=0)))
    weights = [
        plain[i] * ahead[(i // ROWS) * OWNERS : (i // ROWS + 1) * OWNERS] for i in range(PIECES)
    ]
    slopes, sums = slope_terms(tangents, alphas, clears)
    ahead_tangent = ordered_sum(front, sums)
    slopes = [
        weights[i]
        * (slopes[i] + ahead_tangent[(i // ROWS) * OWNERS : (i // ROWS + 1) * OWNERS])
        for i in range(PIECES)
    ]
    prim_cols = columns[:FEAT]
    row, lane = iota((FEAT, 3 * PIX), 0), iota((FEAT, 3 * PIX), 1)
    colours = mm(
        jnp.concatenate(split(prim_cols), axis=0),
        jnp.concatenate([jnp.where(row == lane // PIX + 1, 1.0, 0.0).astype(BF16)] * 2, axis=0),
        TN,
    )
    blended = []
    for c in range(3):
        shades = pieces_of(colours[:, c * PIX : (c + 1) * PIX])
        blended.append(
            jnp.concatenate(
                [
                    sum(weights[i] * shades[i] for i in range(s * ROWS, (s + 1) * ROWS))
                    for s in range(CAP)
                ],
                axis=0,
            )
        )
    blended = jnp.concatenate(blended, axis=1)
    change = image_change(
        columns,
        jnp.concatenate(
            [jnp.concatenate(weights, axis=0), jnp.concatenate(slopes, axis=0)], axis=1
        ),
    )
    colour = change * pixel_weight
    back = pull_back(prim_cols, basis, colour, alphas, clears, weights, blended, behind)
    return (
        back,
        jnp.concatenate(alphas, axis=0),
        jnp.concatenate(clears, axis=0),
        jnp.concatenate(weights, axis=0),
        prim_cols,
        blended,
        front,
        behind,
    )


def pieces_of(array):
    return [array[i * OWNERS : (i + 1) * OWNERS] for i in range(PIECES)]


def next_direction(message, before):
    width = PIECES * FEAT
    tail = message[:, width:]
    cross, guess, aa, ab, bb, daa, dab, dbb = [tail[:, i : i + 1] for i in range(8)]

    def over_owners(value):
        return jnp.sum(value, axis=0, keepdims=True)

    start = over_owners(bb)
    step = start / over_owners(cross)
    share = step / guess
    rest = 1.0 - share
    square = over_owners(share * share * aa + 2.0 * share * rest * ab + rest * rest * bb)
    ratio = square / start
    rest = rest + ratio
    damped = over_owners(share * share * daa + 2.0 * share * rest * dab + rest * rest * dbb)
    feats = share * message[:, :width] + rest * before[:, width : 2 * width]
    return feats, lanes([step, ratio, square, damped], 1)


def render_again(
    message, before, aux, alphas, clears, weights, prim_cols, blended, front, behind
):
    feats, scalars = next_direction(message, before)
    columns = by_column(feats, FEAT)
    basis, pixel_weight = aux[:FEAT], aux[FEAT : FEAT + 1]
    tangents = pieces_of(mm_short(columns, basis))
    alphas, clears, weight_list = pieces_of(alphas), pieces_of(clears), pieces_of(weights)
    slopes, sums = slope_terms(tangents, alphas, clears)
    ahead_tangent = ordered_sum(front, sums)
    slopes = [
        weight_list[i]
        * (slopes[i] + ahead_tangent[(i // ROWS) * OWNERS : (i // ROWS + 1) * OWNERS])
        for i in range(PIECES)
    ]
    change = colours_only(
        change_of(columns, weights) + change_of(prim_cols, jnp.concatenate(slopes, axis=0))
    )
    colour = change * pixel_weight
    back = pull_back(prim_cols, basis, colour, alphas, clears, weight_list, blended, behind)
    out = jnp.concatenate([back, lanes([total(colour * change)], OWNERS)], axis=1)
    return out, scalars


def gathered_parts(message, select):
    columns = by_column(message[:, : PIECES * FEAT], FEAT)
    high, low = split(columns)
    wide = mm(jnp.concatenate([high, low], axis=0), select)
    gathered = wide[:FEAT] + wide[FEAT:]
    return [gathered[:, j : j + PIX] for j in range(0, GAUSS, PIX)]


def collect(views, message, select, proj):
    parts = gathered_parts(message, select)
    turned = jnp.concatenate([proj[:ROWS, : PIX // 2], proj[ROWS:, : PIX // 2]], axis=1)
    part = jnp.concatenate(parts + [turned], axis=0)
    return jnp.broadcast_to(part[None], (views,) + part.shape)


def collect_last(views, message, select):
    parts = gathered_parts(message, select)
    tail = jnp.sum(message[:, PIECES * FEAT :], axis=0, keepdims=True)
    part = jnp.concatenate(parts + [tail], axis=0)
    return jnp.broadcast_to(part[None], (views,) + part.shape)


def turned_pair(message):
    views = message.shape[0]
    last = message[:, GAUSS // PIX * FEAT :].reshape(views * ROWS, PIX)
    turned = jnp.concatenate([last[:, : PIX // 2], last[:, PIX // 2 :]], axis=0).T
    th, tl = split(turned)
    wide = jnp.concatenate(
        [
            jnp.concatenate([th, th], axis=1),
            jnp.concatenate([tl, jnp.zeros(tl.shape, BF16)], axis=1),
        ],
        axis=0,
    )
    return wide


def product_of(message, wide):
    views = message.shape[0]
    gathered = jnp.concatenate(
        [
            jnp.concatenate(
                [
                    message[:, j * FEAT + h : j * FEAT + h + ROWS].reshape(views * ROWS, PIX)
                    for j in range(GAUSS // PIX)
                ],
                axis=1,
            )
            for h in (0, ROWS)
        ],
        axis=0,
    )
    product = mm(wide, jnp.concatenate(split(gathered), axis=0))
    half = PIX // 2
    return (product[:half] + product[half:])[:PARAMS]


def step_first(message, right, damp, proj, select):
    wide = turned_pair(message)
    product = product_of(message, wide) + damp * right
    weighted = damp * right
    bb, dbb = total(right * right), total(weighted * right)
    cross = total(right * product)
    guess = jnp.where(bb > 0.0, bb / jnp.maximum(cross, dbb), 1.0)
    near = right - guess * product
    tail = lanes(
        [
            cross,
            guess,
            total(near * near),
            total(near * right),
            bb,
            total(damp * near * near),
            total(weighted * near),
            dbb,
        ],
        OWNERS,
    )
    out = jnp.concatenate([to_message([project(proj[:, : PIX // 2], near)], select), tail], axis=1)
    return out, product, wide


def finish_kernel(
    message_ref, right_ref, damp_ref, product_ref, wide, scalars_ref,
    solution_hbm, final_hbm, solution, final, sems,
):
    message = message_ref[:, :, 0, :]
    product = product_of(message, wide[...])
    energy = jnp.sum(message[:, GAUSS // PIX * FEAT], axis=0, keepdims=True)[:, 0:1]
    scalars = scalars_ref[...]
    step, ratio = scalars[:, 0:1], scalars[:, 1:2]
    right = right_ref[...]
    residual = right - step * product_ref[...]
    direction = residual + ratio * right
    step_now = scalars[:, 2:3] / (energy + scalars[:, 3:4])
    solution[...] = step * right + step_now * direction
    first = pltpu.make_async_copy(solution, solution_hbm, sems.at[0])
    first.start()
    final[...] = residual - step_now * (product + damp_ref[...] * direction)
    second = pltpu.make_async_copy(final, final_hbm, sems.at[1])
    second.start()
    first.wait()
    second.wait()


def finish(*args):
    shape = (PARAMS, GAUSS)
    return pl.pallas_call(
        finish_kernel,
        out_shape=[jax.ShapeDtypeStruct(shape, F32)] * 2,
        in_specs=[pl.BlockSpec(memory_space=pltpu.VMEM)] * len(args),
        out_specs=[pl.BlockSpec(memory_space=pltpu.HBM)] * 2,
        scratch_shapes=[pltpu.VMEM(shape, F32)] * 2 + [pltpu.SemaphoreType.DMA((2,))],
        compiler_params=pltpu.CompilerParams(vmem_limit_bytes=40 * 1024 * 1024),
        name="finish",
    )(*args)


def call(function, outs, *args):
    def kernel(*refs):
        results = function(*[ref[:, 0, :] if len(ref.shape) == 3 and ref.shape[1] == 1 else ref[...] for ref in refs[: len(args)]])
        if len(outs) == 1:
            results = (results,) if not isinstance(results, tuple) else results
        for ref, result in zip(refs[len(args) :], results):
            if result.ndim < len(ref.shape):
                ref[..., 0, :] = result
            else:
                ref[...] = result

    result = pl.pallas_call(
        kernel,
        out_shape=[jax.ShapeDtypeStruct(shape, dtype) for shape, dtype in outs],
        in_specs=[pl.BlockSpec(memory_space=pltpu.VMEM)] * len(args),
        out_specs=[pl.BlockSpec(memory_space=pltpu.VMEM)] * len(outs),
        compiler_params=pltpu.CompilerParams(vmem_limit_bytes=40 * 1024 * 1024),
        name=function.__name__,
    )(*args)
    return result


def body(
    linear_point,
    right_side,
    damping,
    projection,
    pixel_basis,
    pixel_weight,
    depth_order,
    tile_dest,
    block_depth,
):
    dest = tile_dest.reshape(1, -1)
    views = lax.axis_size("views")
    rows = PIECES * OWNERS
    slots = CAP * OWNERS

    def over_tiles(message):
        return lax.all_to_all(message, "tiles", split_axis=0, concat_axis=0, tiled=True)

    def over_views(part):
        return lax.all_to_all(part, "views", split_axis=0, concat_axis=0, tiled=True)

    message, select, aux, proj = begin(
        linear_point, right_side, jnp.swapaxes(projection, 1, 2)[0],
        pixel_basis.reshape(FEAT - 4, 1, PIX), pixel_weight[0], depth_order[0], dest, block_depth,
    )
    width = PIECES * FEAT
    first_message = over_tiles(message)
    message, alphas, clears, weights, prim, blended, front, behind = call(
        render_first,
        [((OWNERS, 1, width), F32)]
        + [((rows, PIX), F32)] * 3
        + [((FEAT, rows), F32), ((slots, 3 * PIX), F32)]
        + [((slots, slots), BF16)] * 2,
        first_message, aux,
    )
    short = ((OWNERS, 1, width + PIX), F32)
    part_shape = ((views, GAUSS // PIX * FEAT + ROWS, PIX), F32)
    gather = functools.partial(collect, views)
    gather.__name__ = "collect"
    (part,) = call(gather, [part_shape], over_tiles(message), select, proj)
    message, product, wide = call(
        step_first,
        [short, ((PARAMS, GAUSS), F32), ((PIX, 2 * views * FEAT), BF16)],
        over_views(part), right_side, damping, proj, select,
    )
    message, scalars = call(
        render_again,
        [short, ((1, PIX), F32)],
        over_tiles(message), first_message, aux, alphas, clears, weights, prim, blended, front, behind,
    )
    gather = functools.partial(collect_last, views)
    gather.__name__ = "collect_last"
    last_shape = ((views, GAUSS // PIX * FEAT + 1, 1, PIX), F32)
    (part,) = call(gather, [last_shape], over_tiles(message), select)
    return tuple(
        finish(over_views(part), right_side, damping, product, wide, scalars)
    )


def solution(mesh):
    in_specs = (
        P(None, "tiles"),
        P(None, "tiles"),
        P(None, "tiles"),
        P("views", None, None),
        P("views", "tiles", None, None),
        P("views", "tiles", None),
        P("views", "tiles", None),
        P("views", "tiles", None),
        P("views", "tiles"),
    )
    out_specs = (P(None, "tiles"), P(None, "tiles"))
    return jax.shard_map(body, mesh=mesh, in_specs=in_specs, out_specs=out_specs, check_vma=False)
```

```python
import functools

import jax
import jax.numpy as jnp
from jax import lax
from jax.experimental import pallas as pl
from jax.experimental.pallas import tpu as pltpu
from jax.sharding import PartitionSpec as P

OFFSET = 6.0
PARAMS = 59
FEAT = 16
ROWS = 8
CAP = 2
PIECES = CAP * ROWS
OWNERS = 64
GAUSS = 512
PIX = 128
F32 = jnp.float32
BF16 = jnp.bfloat16

NN = (((1,), (0,)), ((), ()))
NT = (((1,), (1,)), ((), ()))
TN = (((0,), (0,)), ((), ()))


def iota(shape, axis):
    return lax.broadcasted_iota(jnp.int32, shape, axis)


def mm(a, b, dims=NN):
    return lax.dot_general(a, b, dims, preferred_element_type=F32)


def split(x):
    high = x.astype(BF16)
    low = (x - high.astype(F32)).astype(BF16)
    return high, low


def mm_short(a, b):
    ah, al = split(a)
    bh, bl = split(b)
    return mm(jnp.concatenate([ah, al, ah], axis=0), jnp.concatenate([bh, bh, bl], axis=0), TN)


def project(proj, vectors):
    tall = jnp.concatenate([vectors, jnp.zeros((PIX // 2 - PARAMS, vectors.shape[1]), F32)], axis=0)
    ph, pl_ = split(proj)
    th, tl = split(tall)
    return mm(jnp.concatenate([ph, pl_, ph], axis=1), jnp.concatenate([th, th, tl], axis=0))


def total(x):
    return jnp.sum(jnp.sum(x, axis=1, keepdims=True), axis=0, keepdims=True)


def lanes(values, rows):
    lane = iota((rows, PIX), 1)
    out = jnp.zeros((rows, PIX), F32)
    for i, value in enumerate(values):
        out = jnp.where(lane == i, value, out)
    return out


def to_message(feats, select):
    stacked = jnp.concatenate(feats, axis=0)
    fields = [slice(i, i + FEAT) for i in range(0, stacked.shape[0], FEAT)]
    rows = stacked.shape[0]
    both = mm(jnp.concatenate(split(stacked), axis=0), select, NT)
    slots = both[:rows] + both[rows:]
    return jnp.concatenate([by_owner(slots[field]) for field in fields], axis=1)


def by_owner(slots):
    pieces = [slots[:, i * OWNERS : (i + 1) * OWNERS] for i in range(PIECES)]
    return jnp.concatenate(pieces, axis=0).T


def by_column(message, width):
    turned = message.T
    return jnp.concatenate([turned[i * width : (i + 1) * width] for i in range(PIECES)], axis=1)


def choose(order, dest):
    blocks = dest.shape[1]
    mine = iota((OWNERS, blocks), 0) == dest
    mine_f = jnp.where(mine, 1.0, 0.0)
    earlier = jnp.where(iota((blocks, blocks), 0) < iota((blocks, blocks), 1), 1.0, 0.0)
    count = mm(mine_f.astype(BF16), earlier.astype(BF16))
    owns = [jnp.where(mine & (count == float(s)), 1.0, 0.0) for s in range(CAP)]
    own_all = jnp.concatenate(owns, axis=0).astype(BF16)
    here = iota((blocks, GAUSS), 1) // ROWS == iota((blocks, GAUSS), 0)
    number = jnp.where(here, order + 1, 0)
    parts = jnp.concatenate(
        [(number // 16).astype(F32), (number % 16).astype(F32)], axis=0
    ).astype(BF16)
    pick = jnp.where(iota((GAUSS, PIX), 0) % ROWS == iota((GAUSS, PIX), 1), 1.0, 0.0).astype(BF16)
    table = mm(parts, pick).astype(BF16)
    ids = mm(own_all, table[:blocks]) * 16.0 + mm(own_all, table[blocks:])
    return owns, ids


def chosen_rows(ids):
    columns = (iota((OWNERS, GAUSS), 1) + 1).astype(F32)
    rows = []
    for s in range(CAP):
        for r in range(ROWS):
            chosen = ids[s * OWNERS : (s + 1) * OWNERS, r : r + 1] == columns
            rows.append(jnp.where(chosen, 1.0, 0.0).astype(BF16))
    return jnp.concatenate(rows, axis=0)


def begin_kernel(
    point_hbm, right_hbm, damp_hbm, proj_hbm, basis_hbm, weight_hbm, order_hbm, dest_hbm, depth_hbm,
    message_ref, select_ref, aux_ref, proj_ref,
    point, right, damp, proj, basis, weight, order, dest, depth, sems,
):
    pairs = [
        (order_hbm, order), (dest_hbm, dest), (depth_hbm, depth), (proj_hbm, proj),
        (point_hbm, point), (right_hbm, right), (damp_hbm, damp), (basis_hbm, basis), (weight_hbm, weight),
    ]
    copies = [pltpu.make_async_copy(a, b, sems.at[i]) for i, (a, b) in enumerate(pairs)]
    for copy in copies:
        copy.start()
    for copy in copies[:3]:
        copy.wait()
    owns, ids = choose(order[...], dest[...])
    depth_f = depth[...].astype(F32) + 1.0
    marks = [jnp.sum(own * depth_f, axis=1, keepdims=True) for own in owns]
    for copy in copies[3:7]:
        copy.wait()
    right_now = right[...]
    padded = jnp.concatenate([proj[...], jnp.zeros((FEAT, PIX - PARAMS), F32)], axis=1)
    proj_ref[...] = padded
    feats = project(padded[:, : PIX // 2], jnp.concatenate([point[...], right_now], axis=1))
    select = chosen_rows(ids)
    select_ref[...] = select
    message = to_message([feats[:, :GAUSS], feats[:, GAUSS:]], select)
    squared = right_now * right_now
    tail = lanes(marks + [total(squared), total(damp[...] * squared)], OWNERS)
    message_ref[:, 0, :] = jnp.concatenate([message, tail], axis=1)
    for copy in copies[7:]:
        copy.wait()
    first = jnp.where(iota((4, PIX), 0) == 0, 1.0, 0.0)
    last = jnp.broadcast_to(weight[...], (8, PIX))
    aux_ref[...] = jnp.concatenate([first, basis[:, 0, :], last], axis=0)


def begin(*args):
    rows = PIECES * OWNERS
    return pl.pallas_call(
        begin_kernel,
        out_shape=[
            jax.ShapeDtypeStruct((OWNERS, 1, PIECES * 2 * FEAT + PIX), F32),
            jax.ShapeDtypeStruct((rows, GAUSS), BF16),
            jax.ShapeDtypeStruct((FEAT + 8, PIX), F32),
            jax.ShapeDtypeStruct((FEAT, PIX), F32),
        ],
        in_specs=[pl.BlockSpec(memory_space=pltpu.HBM)] * len(args),
        out_specs=[pl.BlockSpec(memory_space=pltpu.VMEM)] * 4,
        scratch_shapes=[pltpu.VMEM(x.shape, x.dtype) for x in args]
        + [pltpu.SemaphoreType.DMA((len(args),))],
        compiler_params=pltpu.CompilerParams(vmem_limit_bytes=40 * 1024 * 1024),
        name="begin",
    )(*[pltpu.with_memory_space_constraint(x, pltpu.HBM) for x in args])


def order_masks(marks):
    side = CAP * OWNERS
    by_row = jnp.broadcast_to(marks, (side, side))
    diagonal = iota((side, side), 0) == iota((side, side), 1)
    by_lane = jnp.sum(jnp.where(diagonal, by_row, 0.0), axis=0, keepdims=True)
    front = jnp.where((by_lane < by_row) & (by_lane > 0.0), 1.0, 0.0)
    behind = jnp.where((by_row < by_lane) & (by_row > 0.0), 1.0, 0.0)
    return front.astype(BF16), behind.astype(BF16)


def ordered_sum(mask, value):
    high, low = split(value)
    return mm(jnp.concatenate([mask, mask], axis=1), jnp.concatenate([high, low], axis=0))


def image_change(columns, both):
    high, low = split(columns)
    bh, bl = split(both)
    main = mm(jnp.concatenate([high, low], axis=0), bh)
    rest = mm(high, bl)
    change = (
        main[FEAT : 2 * FEAT, :PIX]
        + main[3 * FEAT :, :PIX]
        + rest[FEAT:, :PIX]
        + main[:FEAT, PIX:]
        + main[2 * FEAT : 3 * FEAT, PIX:]
        + rest[:FEAT, PIX:]
    )
    return colours_only(change)


def change_of(columns, values):
    high, low = split(columns)
    vh, vl = split(values)
    main = mm(jnp.concatenate([high, low], axis=0), vh)
    return main[:FEAT] + main[FEAT:] + mm(high, vl)


def colours_only(change):
    row = iota((FEAT, PIX), 0)
    return jnp.where((row >= 1) & (row < 4), change, 0.0)


def pull_back(prim_cols, basis, colour, alphas, clears, weights, blended, behind):
    shade = mm_short(prim_cols, colour)
    pulls = [weights[i] * shade[i * OWNERS : (i + 1) * OWNERS] for i in range(PIECES)]
    sums = sum(colour[1 + c : 2 + c] * blended[:, c * PIX : (c + 1) * PIX] for c in range(3))
    through = ordered_sum(behind, sums)
    logits = [None] * PIECES
    for s in range(CAP):
        acc = through[s * OWNERS : (s + 1) * OWNERS]
        for r in reversed(range(ROWS)):
            i = s * ROWS + r
            logits[i] = clears[i] * pulls[i] - alphas[i] * acc
            acc = acc + pulls[i]
    def over_pixels(first, second):
        high, low = split(second)
        fh, fl = split(first)
        main = mm(jnp.concatenate([fh, fl], axis=0), high, NT)
        return main[:FEAT] + main[FEAT:] + mm(fh, low, NT)

    early = over_pixels(colour, jnp.concatenate(weights, axis=0))
    return by_owner(early + over_pixels(basis, jnp.concatenate(logits, axis=0)))


def slope_terms(tangents, alphas, clears):
    slopes = []
    sums = []
    for s in range(CAP):
        acc = jnp.zeros((OWNERS, PIX), F32)
        for r in range(ROWS):
            i = s * ROWS + r
            slopes.append(clears[i] * tangents[i] + acc)
            acc = acc - alphas[i] * tangents[i]
        sums.append(acc)
    return slopes, jnp.concatenate(sums, axis=0)


def render_first(message, aux):
    width = PIECES * FEAT
    columns = jnp.concatenate(
        [by_column(message[:, :width], FEAT), by_column(message[:, width : 2 * width], FEAT)], axis=0
    )
    tail = message[:, 2 * width :]
    basis, pixel_weight = aux[:FEAT], aux[FEAT : FEAT + 1]
    both = jnp.zeros((FEAT, PIX), F32)
    wide = jnp.concatenate(
        [jnp.concatenate([basis, both], axis=1), jnp.concatenate([both, basis], axis=1)], axis=0
    )
    logits_tangents = mm_short(columns, wide)
    front, behind = order_masks(jnp.concatenate([tail[:, 0:1], tail[:, 1:2]], axis=0))
    alphas, clears, plain, tangents, lengths = [], [], [], [], []
    for s in range(CAP):
        open_now = None
        length = None
        for r in range(ROWS):
            i = s * ROWS + r
            block = logits_tangents[i * OWNERS : (i + 1) * OWNERS]
            z = block[:, :PIX] - OFFSET
            tangents.append(block[:, PIX:])
            small = jnp.exp(-jnp.abs(z))
            grown = 1.0 + small
            part = 1.0 / grown
            rest = small * part
            alpha = jnp.where(z >= 0.0, part, rest)
            clear = jnp.where(z >= 0.0, rest, part)
            log_clear = -(jnp.maximum(z, 0.0) + jnp.log(grown))
            alphas.append(alpha)
            clears.append(clear)
            plain.append(alpha if open_now is None else alpha * open_now)
            open_now = clear if open_now is None else open_now * clear
            length = log_clear if length is None else length + log_clear
        lengths.append(length)
    ahead = jnp.exp(ordered_sum(front, jnp.concatenate(lengths, axis=0)))
    weights = [
        plain[i] * ahead[(i // ROWS) * OWNERS : (i // ROWS + 1) * OWNERS] for i in range(PIECES)
    ]
    slopes, sums = slope_terms(tangents, alphas, clears)
    ahead_tangent = ordered_sum(front, sums)
    slopes = [
        weights[i]
        * (slopes[i] + ahead_tangent[(i // ROWS) * OWNERS : (i // ROWS + 1) * OWNERS])
        for i in range(PIECES)
    ]
    prim_cols = columns[:FEAT]
    row, lane = iota((FEAT, 3 * PIX), 0), iota((FEAT, 3 * PIX), 1)
    colours = mm(
        jnp.concatenate(split(prim_cols), axis=0),
        jnp.concatenate([jnp.where(row == lane // PIX + 1, 1.0, 0.0).astype(BF16)] * 2, axis=0),
        TN,
    )
    blended = []
    for c in range(3):
        shades = pieces_of(colours[:, c * PIX : (c + 1) * PIX])
        blended.append(
            jnp.concatenate(
                [
                    sum(weights[i] * shades[i] for i in range(s * ROWS, (s + 1) * ROWS))
                    for s in range(CAP)
                ],
                axis=0,
            )
        )
    blended = jnp.concatenate(blended, axis=1)
    change = image_change(
        columns,
        jnp.concatenate(
            [jnp.concatenate(weights, axis=0), jnp.concatenate(slopes, axis=0)], axis=1
        ),
    )
    colour = change * pixel_weight
    back = pull_back(prim_cols, basis, colour, alphas, clears, weights, blended, behind)
    return (
        back,
        jnp.concatenate(alphas, axis=0),
        jnp.concatenate(clears, axis=0),
        jnp.concatenate(weights, axis=0),
        prim_cols,
        blended,
        front,
        behind,
        jnp.sum(tail, axis=0, keepdims=True),
    )


def pieces_of(array):
    return [array[i * OWNERS : (i + 1) * OWNERS] for i in range(PIECES)]


def render_again(
    message, own_sums, aux, alphas, clears, weights, prim_cols, blended, front, behind
):
    columns = by_column(message, FEAT)
    basis, pixel_weight = aux[:FEAT], aux[FEAT : FEAT + 1]
    tangents = pieces_of(mm_short(columns, basis))
    alphas, clears, weight_list = pieces_of(alphas), pieces_of(clears), pieces_of(weights)
    slopes, sums = slope_terms(tangents, alphas, clears)
    ahead_tangent = ordered_sum(front, sums)
    slopes = [
        weight_list[i]
        * (slopes[i] + ahead_tangent[(i // ROWS) * OWNERS : (i // ROWS + 1) * OWNERS])
        for i in range(PIECES)
    ]
    change = colours_only(
        change_of(columns, weights) + change_of(prim_cols, jnp.concatenate(slopes, axis=0))
    )
    colour = change * pixel_weight
    back = pull_back(prim_cols, basis, colour, alphas, clears, weight_list, blended, behind)
    tail = jnp.where(iota((1, PIX), 1) == 0, total(colour * change), own_sums)
    return jnp.concatenate([back, jnp.broadcast_to(tail, (OWNERS, PIX))], axis=1)


def gathered_parts(message, select):
    columns = by_column(message[:, : PIECES * FEAT], FEAT)
    high, low = split(columns)
    wide = mm(jnp.concatenate([high, low], axis=0), select)
    gathered = wide[:FEAT] + wide[FEAT:]
    return [gathered[:, j : j + PIX] for j in range(0, GAUSS, PIX)]


def collect(views, message, select, proj):
    parts = gathered_parts(message, select)
    turned = jnp.concatenate([proj[:ROWS, : PIX // 2], proj[ROWS:, : PIX // 2]], axis=1)
    part = jnp.concatenate(parts + [turned], axis=0)
    return jnp.broadcast_to(part[None], (views,) + part.shape)


def collect_last(views, message, select):
    parts = gathered_parts(message, select)
    tail = jnp.sum(message[:, PIECES * FEAT :], axis=0, keepdims=True)
    part = jnp.concatenate(parts + [tail], axis=0)
    return jnp.broadcast_to(part[None], (views,) + part.shape)


def turned_pair(message):
    views = message.shape[0]
    last = message[:, GAUSS // PIX * FEAT :].reshape(views * ROWS, PIX)
    turned = jnp.concatenate([last[:, : PIX // 2], last[:, PIX // 2 :]], axis=0).T
    th, tl = split(turned)
    wide = jnp.concatenate(
        [
            jnp.concatenate([th, th], axis=1),
            jnp.concatenate([tl, jnp.zeros(tl.shape, BF16)], axis=1),
        ],
        axis=0,
    )
    return wide


def product_of(message, wide):
    views = message.shape[0]
    gathered = jnp.concatenate(
        [
            jnp.concatenate(
                [
                    message[:, j * FEAT + h : j * FEAT + h + ROWS].reshape(views * ROWS, PIX)
                    for j in range(GAUSS // PIX)
                ],
                axis=1,
            )
            for h in (0, ROWS)
        ],
        axis=0,
    )
    product = mm(wide, jnp.concatenate(split(gathered), axis=0))
    half = PIX // 2
    return (product[:half] + product[half:])[:PARAMS]


def first_guess(sums):
    square, damped = sums[:, 2:3], sums[:, 3:4]
    return jnp.where(damped > 0.0, square / damped, 1.0)


def step_first(message, right, damp, proj, select, start):
    wide = turned_pair(message)
    product = product_of(message, wide) + damp * right
    near = right - first_guess(start) * product
    out = to_message([project(proj[:, : PIX // 2], near)], select)
    sums = [
        jnp.zeros((1, 1), F32),
        total(right * product),
        total(near * near),
        total(near * right),
        total(near * product),
        total(damp * near * near),
    ]
    return out, product, wide, lanes(sums, 1)


def finish_kernel(
    message_ref, right_ref, damp_ref, product_ref, wide, start_ref,
    solution_hbm, final_hbm, solution, final, sems,
):
    message = message_ref[:, :, 0, :]
    product = product_of(message, wide[...])
    energy = jnp.sum(message[:, GAUSS // PIX * FEAT], axis=0, keepdims=True)[:, 0:1]
    start = start_ref[...]
    guess, square = first_guess(start), start[:, 2:3]
    sums = message[0, GAUSS // PIX * FEAT :]
    cross, nn, nb, ny, ndn = [sums[:, i : i + 1] for i in range(1, 6)]
    step = square / cross
    share = step / guess
    rest = 1.0 - share
    square_now = share * share * nn + 2.0 * share * rest * nb + rest * rest * square
    part = rest + square_now / square
    bent = share * share * (energy + ndn) + 2.0 * share * part * ny + part * part * cross
    step_now = square_now / bent
    right, before = right_ref[...], product_ref[...]
    near = right - guess * before
    solution[...] = step * right + step_now * (share * near + part * right)
    first = pltpu.make_async_copy(solution, solution_hbm, sems.at[0])
    first.start()
    final[...] = (right - step * before) - step_now * (
        share * (product + damp_ref[...] * near) + part * before
    )
    second = pltpu.make_async_copy(final, final_hbm, sems.at[1])
    second.start()
    first.wait()
    second.wait()


def finish(*args):
    shape = (PARAMS, GAUSS)
    return pl.pallas_call(
        finish_kernel,
        out_shape=[jax.ShapeDtypeStruct(shape, F32)] * 2,
        in_specs=[pl.BlockSpec(memory_space=pltpu.VMEM)] * len(args),
        out_specs=[pl.BlockSpec(memory_space=pltpu.HBM)] * 2,
        scratch_shapes=[pltpu.VMEM(shape, F32)] * 2 + [pltpu.SemaphoreType.DMA((2,))],
        compiler_params=pltpu.CompilerParams(vmem_limit_bytes=40 * 1024 * 1024),
        name="finish",
    )(*args)


def call(function, outs, *args):
    def kernel(*refs):
        results = function(*[ref[:, 0, :] if len(ref.shape) == 3 and ref.shape[1] == 1 else ref[...] for ref in refs[: len(args)]])
        if len(outs) == 1:
            results = (results,) if not isinstance(results, tuple) else results
        for ref, result in zip(refs[len(args) :], results):
            if result.ndim < len(ref.shape):
                ref[..., 0, :] = result
            else:
                ref[...] = result

    result = pl.pallas_call(
        kernel,
        out_shape=[jax.ShapeDtypeStruct(shape, dtype) for shape, dtype in outs],
        in_specs=[pl.BlockSpec(memory_space=pltpu.VMEM)] * len(args),
        out_specs=[pl.BlockSpec(memory_space=pltpu.VMEM)] * len(outs),
        compiler_params=pltpu.CompilerParams(vmem_limit_bytes=40 * 1024 * 1024),
        name=function.__name__,
    )(*args)
    return result


def body(
    linear_point,
    right_side,
    damping,
    projection,
    pixel_basis,
    pixel_weight,
    depth_order,
    tile_dest,
    block_depth,
):
    dest = tile_dest.reshape(1, -1)
    views = lax.axis_size("views")
    rows = PIECES * OWNERS
    slots = CAP * OWNERS

    def over_tiles(message):
        return lax.all_to_all(message, "tiles", split_axis=0, concat_axis=0, tiled=True)

    def over_views(part):
        return lax.all_to_all(part, "views", split_axis=0, concat_axis=0, tiled=True)

    message, select, aux, proj = begin(
        linear_point, right_side, damping, jnp.swapaxes(projection, 1, 2)[0],
        pixel_basis.reshape(FEAT - 4, 1, PIX), pixel_weight[0], depth_order[0], dest, block_depth,
    )
    width = PIECES * FEAT
    message, alphas, clears, weights, prim, blended, front, behind, start = call(
        render_first,
        [((OWNERS, 1, width), F32)]
        + [((rows, PIX), F32)] * 3
        + [((FEAT, rows), F32), ((slots, 3 * PIX), F32)]
        + [((slots, slots), BF16)] * 2
        + [((1, PIX), F32)],
        over_tiles(message), aux,
    )
    part_shape = ((views, GAUSS // PIX * FEAT + ROWS, PIX), F32)
    gather = functools.partial(collect, views)
    gather.__name__ = "collect"
    (part,) = call(gather, [part_shape], over_tiles(message), select, proj)
    message, product, wide, sums = call(
        step_first,
        [
            ((OWNERS, 1, width), F32),
            ((PARAMS, GAUSS), F32),
            ((PIX, 2 * views * FEAT), BF16),
            ((1, PIX), F32),
        ],
        over_views(part), right_side, damping, proj, select, start,
    )
    (message,) = call(
        render_again,
        [((OWNERS, 1, width + PIX), F32)],
        over_tiles(message), sums, aux, alphas, clears, weights, prim, blended, front, behind,
    )
    gather = functools.partial(collect_last, views)
    gather.__name__ = "collect_last"
    last_shape = ((views, GAUSS // PIX * FEAT + 1, 1, PIX), F32)
    (part,) = call(gather, [last_shape], over_tiles(message), select)
    return tuple(
        finish(over_views(part), right_side, damping, product, wide, start)
    )


def solution(mesh):
    in_specs = (
        P(None, "tiles"),
        P(None, "tiles"),
        P(None, "tiles"),
        P("views", None, None),
        P("views", "tiles", None, None),
        P("views", "tiles", None),
        P("views", "tiles", None),
        P("views", "tiles", None),
        P("views", "tiles"),
    )
    out_specs = (P(None, "tiles"), P(None, "tiles"))
    return jax.shard_map(body, mesh=mesh, in_specs=in_specs, out_specs=out_specs, check_vma=False)
```

```python
import functools

import jax
import jax.numpy as jnp
from jax import lax
from jax.experimental import pallas as pl
from jax.experimental.pallas import tpu as pltpu
from jax.sharding import PartitionSpec as P

OFFSET = 6.0
PARAMS = 59
FEAT = 16
ROWS = 8
CAP = 2
PIECES = CAP * ROWS
OWNERS = 64
GAUSS = 512
PIX = 128
F32 = jnp.float32
BF16 = jnp.bfloat16

NN = (((1,), (0,)), ((), ()))
NT = (((1,), (1,)), ((), ()))
TN = (((0,), (0,)), ((), ()))


def iota(shape, axis):
    return lax.broadcasted_iota(jnp.int32, shape, axis)


def mm(a, b, dims=NN):
    return lax.dot_general(a, b, dims, preferred_element_type=F32)


def split(x):
    high = x.astype(BF16)
    low = (x - high.astype(F32)).astype(BF16)
    return high, low


def mm_short(a, b):
    ah, al = split(a)
    bh, bl = split(b)
    return mm(jnp.concatenate([ah, al, ah], axis=0), jnp.concatenate([bh, bh, bl], axis=0), TN)


def project(proj, vectors):
    tall = jnp.concatenate([vectors, jnp.zeros((PIX // 2 - PARAMS, vectors.shape[1]), F32)], axis=0)
    ph, pl_ = split(proj)
    th, tl = split(tall)
    return mm(jnp.concatenate([ph, pl_, ph], axis=1), jnp.concatenate([th, th, tl], axis=0))


def total(x):
    return jnp.sum(jnp.sum(x, axis=1, keepdims=True), axis=0, keepdims=True)


def lanes(values, rows):
    lane = iota((rows, PIX), 1)
    out = jnp.zeros((rows, PIX), F32)
    for i, value in enumerate(values):
        out = jnp.where(lane == i, value, out)
    return out


def to_message(feats, select):
    stacked = jnp.concatenate(feats, axis=0)
    fields = [slice(i, i + FEAT) for i in range(0, stacked.shape[0], FEAT)]
    rows = stacked.shape[0]
    both = mm(jnp.concatenate(split(stacked), axis=0), select, NT)
    slots = both[:rows] + both[rows:]
    return jnp.concatenate([by_owner(slots[field]) for field in fields], axis=1)


def by_owner(slots):
    pieces = [slots[:, i * OWNERS : (i + 1) * OWNERS] for i in range(PIECES)]
    return jnp.concatenate(pieces, axis=0).T


def by_column(message, width):
    turned = message.T
    return jnp.concatenate([turned[i * width : (i + 1) * width] for i in range(PIECES)], axis=1)


def choose(order, dest):
    blocks = dest.shape[1]
    mine = iota((OWNERS, blocks), 0) == dest
    block = iota((OWNERS, blocks), 1).astype(F32)
    first = jnp.min(jnp.where(mine, block, float(blocks)), axis=1, keepdims=True)
    last = jnp.max(jnp.where(mine, block, -1.0), axis=1, keepdims=True)
    owns = [
        jnp.where(block == first, 1.0, 0.0),
        jnp.where((block == last) & (last > first), 1.0, 0.0),
    ]
    own_all = jnp.concatenate(owns, axis=0).astype(BF16)
    here = iota((blocks, GAUSS), 1) // ROWS == iota((blocks, GAUSS), 0)
    number = jnp.where(here, order + 1, 0)
    parts = jnp.concatenate(
        [(number >> 4).astype(F32), (number & 15).astype(F32)], axis=0
    ).astype(BF16)
    pick = jnp.where(iota((GAUSS, PIX), 0) % ROWS == iota((GAUSS, PIX), 1), 1.0, 0.0).astype(BF16)
    table = mm(parts, pick).astype(BF16)
    ids = mm(own_all, table[:blocks]) * 16.0 + mm(own_all, table[blocks:])
    return owns, ids


def chosen_rows(ids):
    columns = (iota((OWNERS, GAUSS), 1) + 1).astype(F32)
    rows = []
    for s in range(CAP):
        for r in range(ROWS):
            chosen = ids[s * OWNERS : (s + 1) * OWNERS, r : r + 1] == columns
            rows.append(jnp.where(chosen, 1.0, 0.0).astype(BF16))
    return jnp.concatenate(rows, axis=0)


def begin_kernel(
    point_hbm, right_hbm, damp_hbm, proj_hbm, basis_hbm, weight_hbm, order_hbm, dest_hbm, depth_hbm,
    message_ref, select_ref, aux_ref, proj_ref,
    point, right, damp, proj, basis, weight, order, dest, depth, sems,
):
    pairs = [
        (order_hbm, order), (dest_hbm, dest), (depth_hbm, depth), (proj_hbm, proj),
        (point_hbm, point), (right_hbm, right), (damp_hbm, damp), (basis_hbm, basis), (weight_hbm, weight),
    ]
    copies = [pltpu.make_async_copy(a, b, sems.at[i]) for i, (a, b) in enumerate(pairs)]
    for copy in copies:
        copy.start()
    for copy in copies[:3]:
        copy.wait()
    owns, ids = choose(order[...], dest[...])
    depth_f = depth[...].astype(F32) + 1.0
    marks = [jnp.sum(own * depth_f, axis=1, keepdims=True) for own in owns]
    for copy in copies[3:7]:
        copy.wait()
    right_now = right[...]
    padded = jnp.concatenate([proj[...], jnp.zeros((FEAT, PIX - PARAMS), F32)], axis=1)
    proj_ref[...] = padded
    feats = project(padded[:, : PIX // 2], jnp.concatenate([point[...], right_now], axis=1))
    select = chosen_rows(ids)
    select_ref[...] = select
    message = to_message([feats[:, :GAUSS], feats[:, GAUSS:]], select)
    squared = right_now * right_now
    tail = lanes(marks + [total(squared), total(damp[...] * squared)], OWNERS)
    message_ref[:, 0, :] = jnp.concatenate([message, tail], axis=1)
    for copy in copies[7:]:
        copy.wait()
    first = jnp.where(iota((4, PIX), 0) == 0, 1.0, 0.0)
    last = jnp.broadcast_to(weight[...], (8, PIX))
    aux_ref[...] = jnp.concatenate([first, basis[:, 0, :], last], axis=0)


def begin(*args):
    rows = PIECES * OWNERS
    return pl.pallas_call(
        begin_kernel,
        out_shape=[
            jax.ShapeDtypeStruct((OWNERS, 1, PIECES * 2 * FEAT + PIX), F32),
            jax.ShapeDtypeStruct((rows, GAUSS), BF16),
            jax.ShapeDtypeStruct((FEAT + 8, PIX), F32),
            jax.ShapeDtypeStruct((FEAT, PIX), F32),
        ],
        in_specs=[pl.BlockSpec(memory_space=pltpu.HBM)] * len(args),
        out_specs=[pl.BlockSpec(memory_space=pltpu.VMEM)] * 4,
        scratch_shapes=[pltpu.VMEM(x.shape, x.dtype) for x in args]
        + [pltpu.SemaphoreType.DMA((len(args),))],
        compiler_params=pltpu.CompilerParams(vmem_limit_bytes=40 * 1024 * 1024),
        name="begin",
    )(*[pltpu.with_memory_space_constraint(x, pltpu.HBM) for x in args])


def order_masks(marks):
    side = CAP * OWNERS
    by_row = jnp.broadcast_to(marks, (side, side))
    diagonal = iota((side, side), 0) == iota((side, side), 1)
    by_lane = jnp.sum(jnp.where(diagonal, by_row, 0.0), axis=0, keepdims=True)
    front = jnp.where((by_lane < by_row) & (by_lane > 0.0), 1.0, 0.0)
    behind = jnp.where((by_row < by_lane) & (by_row > 0.0), 1.0, 0.0)
    return front.astype(BF16), behind.astype(BF16)


def ordered_sum(mask, value):
    high, low = split(value)
    return mm(jnp.concatenate([mask, mask], axis=1), jnp.concatenate([high, low], axis=0))


def image_change(columns, both):
    high, low = split(columns)
    bh, bl = split(both)
    main = mm(jnp.concatenate([high, low], axis=0), bh)
    rest = mm(high, bl)
    change = (
        main[FEAT : 2 * FEAT, :PIX]
        + main[3 * FEAT :, :PIX]
        + rest[FEAT:, :PIX]
        + main[:FEAT, PIX:]
        + main[2 * FEAT : 3 * FEAT, PIX:]
        + rest[:FEAT, PIX:]
    )
    return colours_only(change)


def change_of(columns, values):
    high, low = split(columns)
    vh, vl = split(values)
    main = mm(jnp.concatenate([high, low], axis=0), vh)
    return main[:FEAT] + main[FEAT:] + mm(high, vl)


def colours_only(change):
    row = iota((FEAT, PIX), 0)
    return jnp.where((row >= 1) & (row < 4), change, 0.0)


def pull_back(prim_cols, basis, colour, alphas, clears, weights, blended, behind):
    shade = mm_short(prim_cols, colour)
    pulls = [weights[i] * shade[i * OWNERS : (i + 1) * OWNERS] for i in range(PIECES)]
    sums = sum(colour[1 + c : 2 + c] * blended[:, c * PIX : (c + 1) * PIX] for c in range(3))
    through = ordered_sum(behind, sums)
    logits = [None] * PIECES
    for s in range(CAP):
        acc = through[s * OWNERS : (s + 1) * OWNERS]
        for r in reversed(range(ROWS)):
            i = s * ROWS + r
            logits[i] = clears[i] * pulls[i] - alphas[i] * acc
            acc = acc + pulls[i]
    def over_pixels(first, second):
        high, low = split(second)
        fh, fl = split(first)
        main = mm(jnp.concatenate([fh, fl], axis=0), high, NT)
        return main[:FEAT] + main[FEAT:] + mm(fh, low, NT)

    early = over_pixels(colour, jnp.concatenate(weights, axis=0))
    return by_owner(early + over_pixels(basis, jnp.concatenate(logits, axis=0)))


def slope_terms(tangents, alphas, clears):
    slopes = []
    sums = []
    for s in range(CAP):
        acc = jnp.zeros((OWNERS, PIX), F32)
        for r in range(ROWS):
            i = s * ROWS + r
            slopes.append(clears[i] * tangents[i] + acc)
            acc = acc - alphas[i] * tangents[i]
        sums.append(acc)
    return slopes, jnp.concatenate(sums, axis=0)


def render_first(message, aux):
    width = PIECES * FEAT
    columns = jnp.concatenate(
        [by_column(message[:, :width], FEAT), by_column(message[:, width : 2 * width], FEAT)], axis=0
    )
    tail = message[:, 2 * width :]
    basis, pixel_weight = aux[:FEAT], aux[FEAT : FEAT + 1]
    both = jnp.zeros((FEAT, PIX), F32)
    wide = jnp.concatenate(
        [jnp.concatenate([basis, both], axis=1), jnp.concatenate([both, basis], axis=1)], axis=0
    )
    logits_tangents = mm_short(columns, wide)
    front, behind = order_masks(jnp.concatenate([tail[:, 0:1], tail[:, 1:2]], axis=0))
    alphas, clears, plain, tangents, lengths = [], [], [], [], []
    for s in range(CAP):
        open_now = None
        length = None
        for r in range(ROWS):
            i = s * ROWS + r
            block = logits_tangents[i * OWNERS : (i + 1) * OWNERS]
            z = block[:, :PIX] - OFFSET
            tangents.append(block[:, PIX:])
            small = jnp.exp(-jnp.abs(z))
            grown = 1.0 + small
            part = 1.0 / grown
            rest = small * part
            alpha = jnp.where(z >= 0.0, part, rest)
            clear = jnp.where(z >= 0.0, rest, part)
            log_clear = -(jnp.maximum(z, 0.0) + jnp.log(grown))
            alphas.append(alpha)
            clears.append(clear)
            plain.append(alpha if open_now is None else alpha * open_now)
            open_now = clear if open_now is None else open_now * clear
            length = log_clear if length is None else length + log_clear
        lengths.append(length)
    ahead = jnp.exp(ordered_sum(front, jnp.concatenate(lengths, axis=0)))
    weights = [
        plain[i] * ahead[(i // ROWS) * OWNERS : (i // ROWS + 1) * OWNERS] for i in range(PIECES)
    ]
    slopes, sums = slope_terms(tangents, alphas, clears)
    ahead_tangent = ordered_sum(front, sums)
    slopes = [
        weights[i]
        * (slopes[i] + ahead_tangent[(i // ROWS) * OWNERS : (i // ROWS + 1) * OWNERS])
        for i in range(PIECES)
    ]
    prim_cols = columns[:FEAT]
    row, lane = iota((FEAT, 3 * PIX), 0), iota((FEAT, 3 * PIX), 1)
    colours = mm(
        jnp.concatenate(split(prim_cols), axis=0),
        jnp.concatenate([jnp.where(row == lane // PIX + 1, 1.0, 0.0).astype(BF16)] * 2, axis=0),
        TN,
    )
    blended = []
    for c in range(3):
        shades = pieces_of(colours[:, c * PIX : (c + 1) * PIX])
        blended.append(
            jnp.concatenate(
                [
                    sum(weights[i] * shades[i] for i in range(s * ROWS, (s + 1) * ROWS))
                    for s in range(CAP)
                ],
                axis=0,
            )
        )
    blended = jnp.concatenate(blended, axis=1)
    change = image_change(
        columns,
        jnp.concatenate(
            [jnp.concatenate(weights, axis=0), jnp.concatenate(slopes, axis=0)], axis=1
        ),
    )
    colour = change * pixel_weight
    back = pull_back(prim_cols, basis, colour, alphas, clears, weights, blended, behind)
    return (
        back,
        jnp.concatenate(alphas, axis=0),
        jnp.concatenate(clears, axis=0),
        jnp.concatenate(weights, axis=0),
        prim_cols,
        blended,
        front,
        behind,
        jnp.sum(tail, axis=0, keepdims=True),
    )


def pieces_of(array):
    return [array[i * OWNERS : (i + 1) * OWNERS] for i in range(PIECES)]


def render_again(
    message, own_sums, aux, alphas, clears, weights, prim_cols, blended, front, behind
):
    columns = by_column(message, FEAT)
    basis, pixel_weight = aux[:FEAT], aux[FEAT : FEAT + 1]
    tangents = pieces_of(mm_short(columns, basis))
    alphas, clears, weight_list = pieces_of(alphas), pieces_of(clears), pieces_of(weights)
    slopes, sums = slope_terms(tangents, alphas, clears)
    ahead_tangent = ordered_sum(front, sums)
    slopes = [
        weight_list[i]
        * (slopes[i] + ahead_tangent[(i // ROWS) * OWNERS : (i // ROWS + 1) * OWNERS])
        for i in range(PIECES)
    ]
    change = colours_only(
        change_of(columns, weights) + change_of(prim_cols, jnp.concatenate(slopes, axis=0))
    )
    colour = change * pixel_weight
    back = pull_back(prim_cols, basis, colour, alphas, clears, weight_list, blended, behind)
    tail = jnp.where(iota((1, PIX), 1) == 0, total(colour * change), own_sums)
    return jnp.concatenate([back, jnp.broadcast_to(tail, (OWNERS, PIX))], axis=1)


def gathered_parts(message, select):
    columns = by_column(message[:, : PIECES * FEAT], FEAT)
    high, low = split(columns)
    wide = mm(jnp.concatenate([high, low], axis=0), select)
    gathered = wide[:FEAT] + wide[FEAT:]
    return [gathered[:, j : j + PIX] for j in range(0, GAUSS, PIX)]


def collect(views, message, select, proj):
    parts = gathered_parts(message, select)
    turned = jnp.concatenate([proj[:ROWS, : PIX // 2], proj[ROWS:, : PIX // 2]], axis=1)
    part = jnp.concatenate(parts + [turned], axis=0)
    return jnp.broadcast_to(part[None], (views,) + part.shape)


def collect_last(views, message, select):
    parts = gathered_parts(message, select)
    tail = jnp.sum(message[:, PIECES * FEAT :], axis=0, keepdims=True)
    part = jnp.concatenate(parts + [tail], axis=0)
    return jnp.broadcast_to(part[None], (views,) + part.shape)


def turned_pair(message):
    views = message.shape[0]
    last = message[:, GAUSS // PIX * FEAT :].reshape(views * ROWS, PIX)
    turned = jnp.concatenate([last[:, : PIX // 2], last[:, PIX // 2 :]], axis=0).T
    th, tl = split(turned)
    wide = jnp.concatenate(
        [
            jnp.concatenate([th, th], axis=1),
            jnp.concatenate([tl, jnp.zeros(tl.shape, BF16)], axis=1),
        ],
        axis=0,
    )
    return wide


def product_of(message, wide):
    views = message.shape[0]
    gathered = jnp.concatenate(
        [
            jnp.concatenate(
                [
                    message[:, j * FEAT + h : j * FEAT + h + ROWS].reshape(views * ROWS, PIX)
                    for j in range(GAUSS // PIX)
                ],
                axis=1,
            )
            for h in (0, ROWS)
        ],
        axis=0,
    )
    product = mm(wide, jnp.concatenate(split(gathered), axis=0))
    half = PIX // 2
    return (product[:half] + product[half:])[:PARAMS]


def first_guess(sums):
    square, damped = sums[:, 2:3], sums[:, 3:4]
    return jnp.where(damped > 0.0, square / damped, 1.0)


def step_first(message, right, damp, proj, select, start):
    wide = turned_pair(message)
    back = product_of(message, wide)
    product = back + damp * right
    near = right - first_guess(start) * product
    out = to_message([project(proj[:, : PIX // 2], near)], select)
    sums = [
        jnp.zeros((1, 1), F32),
        total(right * back),
        total(near * near),
        total(near * right),
        total(near * product),
        total(damp * near * near),
    ]
    return out, product, wide, lanes(sums, 1)


def finish_kernel(
    message_ref, right_ref, damp_ref, product_ref, wide, start_ref,
    solution_hbm, final_hbm, solution, final, sems,
):
    message = message_ref[:, :, 0, :]
    product = product_of(message, wide[...])
    energy = jnp.sum(message[:, GAUSS // PIX * FEAT], axis=0, keepdims=True)[:, 0:1]
    start = start_ref[...]
    guess, square, damped = first_guess(start), start[:, 2:3], start[:, 3:4]
    sums = message[0, GAUSS // PIX * FEAT :]
    seen, nn, nb, ny, ndn = [sums[:, i : i + 1] for i in range(1, 6)]
    cross = seen + damped
    step, share, rest = square / cross, damped / cross, seen / cross
    square_now = share * share * nn + 2.0 * share * rest * nb + rest * rest * square
    ratio = square_now / square
    part = rest + ratio
    bent = share * share * (energy + ndn) + 2.0 * share * part * ny + part * part * cross
    step_now = square_now / bent
    right, before = right_ref[...], product_ref[...]
    near = right - guess * before
    residual = share * near + rest * right
    solution[...] = step * right + step_now * (residual + ratio * right)
    first = pltpu.make_async_copy(solution, solution_hbm, sems.at[0])
    first.start()
    final[...] = residual - step_now * (
        share * (product + damp_ref[...] * near) + part * before
    )
    second = pltpu.make_async_copy(final, final_hbm, sems.at[1])
    second.start()
    first.wait()
    second.wait()


def finish(*args):
    shape = (PARAMS, GAUSS)
    return pl.pallas_call(
        finish_kernel,
        out_shape=[jax.ShapeDtypeStruct(shape, F32)] * 2,
        in_specs=[pl.BlockSpec(memory_space=pltpu.VMEM)] * len(args),
        out_specs=[pl.BlockSpec(memory_space=pltpu.HBM)] * 2,
        scratch_shapes=[pltpu.VMEM(shape, F32)] * 2 + [pltpu.SemaphoreType.DMA((2,))],
        compiler_params=pltpu.CompilerParams(vmem_limit_bytes=40 * 1024 * 1024),
        name="finish",
    )(*args)


def call(function, outs, *args):
    def kernel(*refs):
        results = function(*[ref[:, 0, :] if len(ref.shape) == 3 and ref.shape[1] == 1 else ref[...] for ref in refs[: len(args)]])
        if len(outs) == 1:
            results = (results,) if not isinstance(results, tuple) else results
        for ref, result in zip(refs[len(args) :], results):
            if result.ndim < len(ref.shape):
                ref[..., 0, :] = result
            else:
                ref[...] = result

    result = pl.pallas_call(
        kernel,
        out_shape=[jax.ShapeDtypeStruct(shape, dtype) for shape, dtype in outs],
        in_specs=[pl.BlockSpec(memory_space=pltpu.VMEM)] * len(args),
        out_specs=[pl.BlockSpec(memory_space=pltpu.VMEM)] * len(outs),
        compiler_params=pltpu.CompilerParams(vmem_limit_bytes=40 * 1024 * 1024),
        name=function.__name__,
    )(*args)
    return result


def body(
    linear_point,
    right_side,
    damping,
    projection,
    pixel_basis,
    pixel_weight,
    depth_order,
    tile_dest,
    block_depth,
):
    dest = tile_dest.reshape(1, -1)
    views = lax.axis_size("views")
    rows = PIECES * OWNERS
    slots = CAP * OWNERS

    def over_tiles(message):
        return lax.all_to_all(message, "tiles", split_axis=0, concat_axis=0, tiled=True)

    def over_views(part):
        return lax.all_to_all(part, "views", split_axis=0, concat_axis=0, tiled=True)

    message, select, aux, proj = begin(
        linear_point, right_side, damping, jnp.swapaxes(projection, 1, 2)[0],
        pixel_basis.reshape(FEAT - 4, 1, PIX), pixel_weight[0], depth_order[0], dest, block_depth,
    )
    width = PIECES * FEAT
    message, alphas, clears, weights, prim, blended, front, behind, start = call(
        render_first,
        [((OWNERS, 1, width), F32)]
        + [((rows, PIX), F32)] * 3
        + [((FEAT, rows), F32), ((slots, 3 * PIX), F32)]
        + [((slots, slots), BF16)] * 2
        + [((1, PIX), F32)],
        over_tiles(message), aux,
    )
    part_shape = ((views, GAUSS // PIX * FEAT + ROWS, PIX), F32)
    gather = functools.partial(collect, views)
    gather.__name__ = "collect"
    (part,) = call(gather, [part_shape], over_tiles(message), select, proj)
    message, product, wide, sums = call(
        step_first,
        [
            ((OWNERS, 1, width), F32),
            ((PARAMS, GAUSS), F32),
            ((PIX, 2 * views * FEAT), BF16),
            ((1, PIX), F32),
        ],
        over_views(part), right_side, damping, proj, select, start,
    )
    (message,) = call(
        render_again,
        [((OWNERS, 1, width + PIX), F32)],
        over_tiles(message), sums, aux, alphas, clears, weights, prim, blended, front, behind,
    )
    gather = functools.partial(collect_last, views)
    gather.__name__ = "collect_last"
    last_shape = ((views, GAUSS // PIX * FEAT + 1, 1, PIX), F32)
    (part,) = call(gather, [last_shape], over_tiles(message), select)
    return tuple(
        finish(over_views(part), right_side, damping, product, wide, start)
    )


def solution(mesh):
    in_specs = (
        P(None, "tiles"),
        P(None, "tiles"),
        P(None, "tiles"),
        P("views", None, None),
        P("views", "tiles", None, None),
        P("views", "tiles", None),
        P("views", "tiles", None),
        P("views", "tiles", None),
        P("views", "tiles"),
    )
    out_specs = (P(None, "tiles"), P(None, "tiles"))
    return jax.shard_map(body, mesh=mesh, in_specs=in_specs, out_specs=out_specs, check_vma=False)
```

```python
import functools

import jax
import jax.numpy as jnp
from jax import lax
from jax.experimental import pallas as pl
from jax.experimental.pallas import tpu as pltpu
from jax.sharding import PartitionSpec as P

OFFSET = 6.0
PARAMS = 59
FEAT = 16
ROWS = 8
CAP = 2
PIECES = CAP * ROWS
OWNERS = 64
GAUSS = 512
PIX = 128
F32 = jnp.float32
BF16 = jnp.bfloat16

NN = (((1,), (0,)), ((), ()))
NT = (((1,), (1,)), ((), ()))
TN = (((0,), (0,)), ((), ()))


def iota(shape, axis):
    return lax.broadcasted_iota(jnp.int32, shape, axis)


def mm(a, b, dims=NN):
    return lax.dot_general(a, b, dims, preferred_element_type=F32)


def split(x):
    high = x.astype(BF16)
    low = (x - high.astype(F32)).astype(BF16)
    return high, low


def mm_short(a, b):
    ah, al = split(a)
    bh, bl = split(b)
    return mm(jnp.concatenate([ah, al, ah], axis=0), jnp.concatenate([bh, bh, bl], axis=0), TN)


def project(proj, vectors):
    tall = jnp.concatenate([vectors, jnp.zeros((PIX // 2 - PARAMS, vectors.shape[1]), F32)], axis=0)
    ph, pl_ = split(proj)
    th, tl = split(tall)
    return mm(jnp.concatenate([ph, pl_, ph], axis=1), jnp.concatenate([th, th, tl], axis=0))


def total(x):
    return jnp.sum(jnp.sum(x, axis=1, keepdims=True), axis=0, keepdims=True)


def lanes(values, rows):
    lane = iota((rows, PIX), 1)
    out = jnp.zeros((rows, PIX), F32)
    for i, value in enumerate(values):
        out = jnp.where(lane == i, value, out)
    return out


def to_message(feats, select):
    stacked = jnp.concatenate(feats, axis=0)
    fields = [slice(i, i + FEAT) for i in range(0, stacked.shape[0], FEAT)]
    rows = stacked.shape[0]
    both = mm(jnp.concatenate(split(stacked), axis=0), select, NT)
    slots = both[:rows] + both[rows:]
    return jnp.concatenate([by_owner(slots[field]) for field in fields], axis=1)


def by_owner(slots):
    pieces = [slots[:, i * OWNERS : (i + 1) * OWNERS] for i in range(PIECES)]
    return jnp.concatenate(pieces, axis=0).T


def by_column(message, width):
    turned = message.T
    return jnp.concatenate([turned[i * width : (i + 1) * width] for i in range(PIECES)], axis=1)


def choose(order, dest):
    blocks = dest.shape[1]
    mine = iota((OWNERS, blocks), 0) == dest
    block = iota((OWNERS, blocks), 1).astype(F32)
    first = jnp.min(jnp.where(mine, block, float(blocks)), axis=1, keepdims=True)
    last = jnp.max(jnp.where(mine, block, -1.0), axis=1, keepdims=True)
    owns = [
        jnp.where(block == first, 1.0, 0.0),
        jnp.where((block == last) & (last > first), 1.0, 0.0),
    ]
    own_all = jnp.concatenate(owns, axis=0).astype(BF16)
    here = iota((blocks, GAUSS), 1) // ROWS == iota((blocks, GAUSS), 0)
    number = jnp.where(here, order + 1, 0)
    parts = jnp.concatenate(
        [(number >> 4).astype(F32), (number & 15).astype(F32)], axis=0
    ).astype(BF16)
    pick = jnp.where(iota((GAUSS, PIX), 0) % ROWS == iota((GAUSS, PIX), 1), 1.0, 0.0).astype(BF16)
    table = mm(parts, pick).astype(BF16)
    ids = mm(own_all, table[:blocks]) * 16.0 + mm(own_all, table[blocks:])
    return owns, ids


def chosen_rows(ids):
    columns = (iota((OWNERS, GAUSS), 1) + 1).astype(F32)
    rows = []
    for s in range(CAP):
        for r in range(ROWS):
            chosen = ids[s * OWNERS : (s + 1) * OWNERS, r : r + 1] == columns
            rows.append(jnp.where(chosen, 1.0, 0.0).astype(BF16))
    return jnp.concatenate(rows, axis=0)


def begin_kernel(
    point_hbm, right_hbm, damp_hbm, proj_hbm, basis_hbm, weight_hbm, order_hbm, dest_hbm, depth_hbm,
    message_ref, select_ref, aux_ref, proj_ref,
    point, right, damp, proj, basis, weight, order, dest, depth, sems,
):
    pairs = [
        (order_hbm, order), (dest_hbm, dest), (depth_hbm, depth), (proj_hbm, proj),
        (point_hbm, point), (right_hbm, right), (damp_hbm, damp), (basis_hbm, basis), (weight_hbm, weight),
    ]
    copies = [pltpu.make_async_copy(a, b, sems.at[i]) for i, (a, b) in enumerate(pairs)]
    for copy in copies:
        copy.start()
    for copy in copies[:3]:
        copy.wait()
    owns, ids = choose(order[...], dest[...])
    depth_f = depth[...].astype(F32) + 1.0
    marks = [jnp.sum(own * depth_f, axis=1, keepdims=True) for own in owns]
    for copy in copies[3:7]:
        copy.wait()
    right_now = right[...]
    padded = jnp.concatenate([proj[...], jnp.zeros((FEAT, PIX - PARAMS), F32)], axis=1)
    proj_ref[...] = padded
    feats = project(padded[:, : PIX // 2], jnp.concatenate([point[...], right_now], axis=1))
    select = chosen_rows(ids)
    select_ref[...] = select
    message = to_message([feats[:, :GAUSS], feats[:, GAUSS:]], select)
    squared = right_now * right_now
    tail = lanes(marks + [total(squared), total(damp[...] * squared)], OWNERS)
    message_ref[:, 0, :] = jnp.concatenate([message, tail], axis=1)
    for copy in copies[7:]:
        copy.wait()
    first = jnp.where(iota((4, PIX), 0) == 0, 1.0, 0.0)
    last = jnp.broadcast_to(weight[...], (8, PIX))
    aux_ref[...] = jnp.concatenate([first, basis[:, 0, :], last], axis=0)


def begin(*args):
    rows = PIECES * OWNERS
    return pl.pallas_call(
        begin_kernel,
        out_shape=[
            jax.ShapeDtypeStruct((OWNERS, 1, PIECES * 2 * FEAT + PIX), F32),
            jax.ShapeDtypeStruct((rows, GAUSS), BF16),
            jax.ShapeDtypeStruct((FEAT + 8, PIX), F32),
            jax.ShapeDtypeStruct((FEAT, PIX), F32),
        ],
        in_specs=[pl.BlockSpec(memory_space=pltpu.HBM)] * len(args),
        out_specs=[pl.BlockSpec(memory_space=pltpu.VMEM)] * 4,
        scratch_shapes=[pltpu.VMEM(x.shape, x.dtype) for x in args]
        + [pltpu.SemaphoreType.DMA((len(args),))],
        compiler_params=pltpu.CompilerParams(vmem_limit_bytes=40 * 1024 * 1024),
        name="begin",
    )(*[pltpu.with_memory_space_constraint(x, pltpu.HBM) for x in args])


def order_masks(marks):
    side = CAP * OWNERS
    by_row = jnp.broadcast_to(marks, (side, side))
    diagonal = iota((side, side), 0) == iota((side, side), 1)
    by_lane = jnp.sum(jnp.where(diagonal, by_row, 0.0), axis=0, keepdims=True)
    front = jnp.where((by_lane < by_row) & (by_lane > 0.0), 1.0, 0.0)
    behind = jnp.where((by_row < by_lane) & (by_row > 0.0), 1.0, 0.0)
    return front.astype(BF16), behind.astype(BF16)


def ordered_sum(mask, value):
    high, low = split(value)
    return mm(jnp.concatenate([mask, mask], axis=1), jnp.concatenate([high, low], axis=0))


def image_change(columns, both):
    high, low = split(columns)
    bh, bl = split(both)
    main = mm(jnp.concatenate([high, low], axis=0), bh)
    rest = mm(high, bl)
    change = (
        main[FEAT : 2 * FEAT, :PIX]
        + main[3 * FEAT :, :PIX]
        + rest[FEAT:, :PIX]
        + main[:FEAT, PIX:]
        + main[2 * FEAT : 3 * FEAT, PIX:]
        + rest[:FEAT, PIX:]
    )
    return colours_only(change)


def change_of(columns, values):
    high, low = split(columns)
    vh, vl = split(values)
    main = mm(jnp.concatenate([high, low], axis=0), vh)
    return main[:FEAT] + main[FEAT:] + mm(high, vl)


def colours_only(change):
    row = iota((FEAT, PIX), 0)
    return jnp.where((row >= 1) & (row < 4), change, 0.0)


def pull_back(prim_cols, basis, colour, alphas, clears, weights, blended, behind):
    shade = mm_short(prim_cols, colour)
    pulls = [weights[i] * shade[i * OWNERS : (i + 1) * OWNERS] for i in range(PIECES)]
    sums = sum(colour[1 + c : 2 + c] * blended[:, c * PIX : (c + 1) * PIX] for c in range(3))
    through = ordered_sum(behind, sums)
    logits = [None] * PIECES
    for s in range(CAP):
        acc = through[s * OWNERS : (s + 1) * OWNERS]
        for r in reversed(range(ROWS)):
            i = s * ROWS + r
            logits[i] = clears[i] * pulls[i] - alphas[i] * acc
            acc = acc + pulls[i]
    def over_pixels(first, second):
        high, low = split(second)
        fh, fl = split(first)
        main = mm(jnp.concatenate([fh, fl], axis=0), high, NT)
        return main[:FEAT] + main[FEAT:] + mm(fh, low, NT)

    early = over_pixels(colour, jnp.concatenate(weights, axis=0))
    return by_owner(early + over_pixels(basis, jnp.concatenate(logits, axis=0)))


def slope_terms(tangents, alphas, clears):
    slopes = []
    sums = []
    for s in range(CAP):
        acc = jnp.zeros((OWNERS, PIX), F32)
        for r in range(ROWS):
            i = s * ROWS + r
            slopes.append(clears[i] * tangents[i] + acc)
            acc = acc - alphas[i] * tangents[i]
        sums.append(acc)
    return slopes, jnp.concatenate(sums, axis=0)


def render_first(message, aux):
    width = PIECES * FEAT
    columns = jnp.concatenate(
        [by_column(message[:, :width], FEAT), by_column(message[:, width : 2 * width], FEAT)], axis=0
    )
    tail = message[:, 2 * width :]
    basis, pixel_weight = aux[:FEAT], aux[FEAT : FEAT + 1]
    both = jnp.zeros((FEAT, PIX), F32)
    wide = jnp.concatenate(
        [jnp.concatenate([basis, both], axis=1), jnp.concatenate([both, basis], axis=1)], axis=0
    )
    logits_tangents = mm_short(columns, wide)
    front, behind = order_masks(jnp.concatenate([tail[:, 0:1], tail[:, 1:2]], axis=0))
    alphas, clears, plain, tangents, lengths = [], [], [], [], []
    for s in range(CAP):
        open_now = None
        length = None
        for r in range(ROWS):
            i = s * ROWS + r
            block = logits_tangents[i * OWNERS : (i + 1) * OWNERS]
            z = block[:, :PIX] - OFFSET
            tangents.append(block[:, PIX:])
            small = jnp.exp(-jnp.abs(z))
            grown = 1.0 + small
            part = 1.0 / grown
            rest = small * part
            alpha = jnp.where(z >= 0.0, part, rest)
            clear = jnp.where(z >= 0.0, rest, part)
            log_clear = -(jnp.maximum(z, 0.0) + jnp.log(grown))
            alphas.append(alpha)
            clears.append(clear)
            plain.append(alpha if open_now is None else alpha * open_now)
            open_now = clear if open_now is None else open_now * clear
            length = log_clear if length is None else length + log_clear
        lengths.append(length)
    ahead = jnp.exp(ordered_sum(front, jnp.concatenate(lengths, axis=0)))
    weights = [
        plain[i] * ahead[(i // ROWS) * OWNERS : (i // ROWS + 1) * OWNERS] for i in range(PIECES)
    ]
    slopes, sums = slope_terms(tangents, alphas, clears)
    ahead_tangent = ordered_sum(front, sums)
    slopes = [
        weights[i]
        * (slopes[i] + ahead_tangent[(i // ROWS) * OWNERS : (i // ROWS + 1) * OWNERS])
        for i in range(PIECES)
    ]
    prim_cols = columns[:FEAT]
    row, lane = iota((FEAT, 3 * PIX), 0), iota((FEAT, 3 * PIX), 1)
    colours = mm(
        jnp.concatenate(split(prim_cols), axis=0),
        jnp.concatenate([jnp.where(row == lane // PIX + 1, 1.0, 0.0).astype(BF16)] * 2, axis=0),
        TN,
    )
    blended = []
    for c in range(3):
        shades = pieces_of(colours[:, c * PIX : (c + 1) * PIX])
        blended.append(
            jnp.concatenate(
                [
                    sum(weights[i] * shades[i] for i in range(s * ROWS, (s + 1) * ROWS))
                    for s in range(CAP)
                ],
                axis=0,
            )
        )
    blended = jnp.concatenate(blended, axis=1)
    change = image_change(
        columns,
        jnp.concatenate(
            [jnp.concatenate(weights, axis=0), jnp.concatenate(slopes, axis=0)], axis=1
        ),
    )
    colour = change * pixel_weight
    back = pull_back(prim_cols, basis, colour, alphas, clears, weights, blended, behind)
    return (
        back,
        jnp.concatenate(alphas, axis=0),
        jnp.concatenate(clears, axis=0),
        jnp.concatenate(weights, axis=0),
        prim_cols,
        blended,
        front,
        behind,
        jnp.sum(tail, axis=0, keepdims=True),
    )


def pieces_of(array):
    return [array[i * OWNERS : (i + 1) * OWNERS] for i in range(PIECES)]


def render_again(
    message, own_sums, aux, alphas, clears, weights, prim_cols, blended, front, behind
):
    columns = by_column(message, FEAT)
    basis, pixel_weight = aux[:FEAT], aux[FEAT : FEAT + 1]
    tangents = pieces_of(mm_short(columns, basis))
    alphas, clears, weight_list = pieces_of(alphas), pieces_of(clears), pieces_of(weights)
    slopes, sums = slope_terms(tangents, alphas, clears)
    ahead_tangent = ordered_sum(front, sums)
    slopes = [
        weight_list[i]
        * (slopes[i] + ahead_tangent[(i // ROWS) * OWNERS : (i // ROWS + 1) * OWNERS])
        for i in range(PIECES)
    ]
    change = colours_only(
        change_of(columns, weights) + change_of(prim_cols, jnp.concatenate(slopes, axis=0))
    )
    colour = change * pixel_weight
    back = pull_back(prim_cols, basis, colour, alphas, clears, weight_list, blended, behind)
    tail = jnp.where(iota((1, PIX), 1) == 0, total(colour * change), own_sums)
    return jnp.concatenate([back, jnp.broadcast_to(tail, (OWNERS, PIX))], axis=1)


def gathered_parts(message, select):
    columns = by_column(message[:, : PIECES * FEAT], FEAT)
    high, low = split(columns)
    wide = mm(jnp.concatenate([high, low], axis=0), select)
    gathered = wide[:FEAT] + wide[FEAT:]
    return [gathered[:, j : j + PIX] for j in range(0, GAUSS, PIX)]


def collect(views, message, select, proj):
    parts = gathered_parts(message, select)
    turned = jnp.concatenate([proj[:ROWS, : PIX // 2], proj[ROWS:, : PIX // 2]], axis=1)
    part = jnp.concatenate(parts + [turned], axis=0)
    return jnp.broadcast_to(part[None], (views,) + part.shape)


def collect_last(views, message, select):
    parts = gathered_parts(message, select)
    tail = jnp.sum(message[:, PIECES * FEAT :], axis=0, keepdims=True)
    part = jnp.concatenate(parts + [tail], axis=0)
    return jnp.broadcast_to(part[None], (views,) + part.shape)


def turned_pair(message):
    views = message.shape[0]
    last = message[:, GAUSS // PIX * FEAT :].reshape(views * ROWS, PIX)
    turned = jnp.concatenate([last[:, : PIX // 2], last[:, PIX // 2 :]], axis=0).T
    th, tl = split(turned)
    wide = jnp.concatenate(
        [
            jnp.concatenate([th, th], axis=1),
            jnp.concatenate([tl, jnp.zeros(tl.shape, BF16)], axis=1),
        ],
        axis=0,
    )
    return wide


def product_of(message, wide):
    views = message.shape[0]
    gathered = jnp.concatenate(
        [
            jnp.concatenate(
                [
                    message[:, j * FEAT + h : j * FEAT + h + ROWS].reshape(views * ROWS, PIX)
                    for j in range(GAUSS // PIX)
                ],
                axis=1,
            )
            for h in (0, ROWS)
        ],
        axis=0,
    )
    product = mm(wide, jnp.concatenate(split(gathered), axis=0))
    half = PIX // 2
    return (product[:half] + product[half:])[:PARAMS]


def first_guess(sums):
    square, damped = sums[:, 2:3], sums[:, 3:4]
    return jnp.where(damped > 0.0, square / damped, 1.0)


def step_first(message, right, damp, proj, select, start):
    wide = turned_pair(message)
    back = product_of(message, wide)
    product = back + damp * right
    near = right - first_guess(start) * product
    out = to_message([project(proj[:, : PIX // 2], near)], select)
    sums = [
        jnp.zeros((1, 1), F32),
        total(right * back),
        total(near * near),
        total(near * right),
        total(near * product),
        total(damp * near * near),
    ]
    return out, product, near, wide, lanes(sums, 1)


def finish_kernel(
    message_ref, right_ref, damp_ref, product_ref, near_ref, wide, start_ref,
    solution_hbm, final_hbm, solution, final, sems,
):
    message = message_ref[:, :, 0, :]
    product = product_of(message, wide[...])
    energy = jnp.sum(message[:, GAUSS // PIX * FEAT], axis=0, keepdims=True)[:, 0:1]
    start = start_ref[...]
    square, damped = start[:, 2:3], start[:, 3:4]
    sums = message[0, GAUSS // PIX * FEAT :]
    seen, nn, nb, ny, ndn = [sums[:, i : i + 1] for i in range(1, 6)]
    cross = seen + damped
    step, share, rest = square / cross, damped / cross, seen / cross
    square_now = share * share * nn + 2.0 * share * rest * nb + rest * rest * square
    ratio = square_now / square
    part = rest + ratio
    bent = share * share * (energy + ndn) + 2.0 * share * part * ny + part * part * cross
    step_now = square_now / bent
    right, before, near = right_ref[...], product_ref[...], near_ref[...]
    residual = share * near + rest * right
    solution[...] = step * right + step_now * (residual + ratio * right)
    first = pltpu.make_async_copy(solution, solution_hbm, sems.at[0])
    first.start()
    final[...] = residual - step_now * (
        share * (product + damp_ref[...] * near) + part * before
    )
    second = pltpu.make_async_copy(final, final_hbm, sems.at[1])
    second.start()
    first.wait()
    second.wait()


def finish(*args):
    shape = (PARAMS, GAUSS)
    return pl.pallas_call(
        finish_kernel,
        out_shape=[jax.ShapeDtypeStruct(shape, F32)] * 2,
        in_specs=[pl.BlockSpec(memory_space=pltpu.VMEM)] * len(args),
        out_specs=[pl.BlockSpec(memory_space=pltpu.HBM)] * 2,
        scratch_shapes=[pltpu.VMEM(shape, F32)] * 2 + [pltpu.SemaphoreType.DMA((2,))],
        compiler_params=pltpu.CompilerParams(vmem_limit_bytes=40 * 1024 * 1024),
        name="finish",
    )(*args)


def call(function, outs, *args):
    def kernel(*refs):
        results = function(*[ref[:, 0, :] if len(ref.shape) == 3 and ref.shape[1] == 1 else ref[...] for ref in refs[: len(args)]])
        if len(outs) == 1:
            results = (results,) if not isinstance(results, tuple) else results
        for ref, result in zip(refs[len(args) :], results):
            if result.ndim < len(ref.shape):
                ref[..., 0, :] = result
            else:
                ref[...] = result

    result = pl.pallas_call(
        kernel,
        out_shape=[jax.ShapeDtypeStruct(shape, dtype) for shape, dtype in outs],
        in_specs=[pl.BlockSpec(memory_space=pltpu.VMEM)] * len(args),
        out_specs=[pl.BlockSpec(memory_space=pltpu.VMEM)] * len(outs),
        compiler_params=pltpu.CompilerParams(vmem_limit_bytes=40 * 1024 * 1024),
        name=function.__name__,
    )(*args)
    return result


def body(
    linear_point,
    right_side,
    damping,
    projection,
    pixel_basis,
    pixel_weight,
    depth_order,
    tile_dest,
    block_depth,
):
    dest = tile_dest.reshape(1, -1)
    views = lax.axis_size("views")
    rows = PIECES * OWNERS
    slots = CAP * OWNERS

    def over_tiles(message):
        return lax.all_to_all(message, "tiles", split_axis=0, concat_axis=0, tiled=True)

    def over_views(part):
        return lax.all_to_all(part, "views", split_axis=0, concat_axis=0, tiled=True)

    message, select, aux, proj = begin(
        linear_point, right_side, damping, jnp.swapaxes(projection, 1, 2)[0],
        pixel_basis.reshape(FEAT - 4, 1, PIX), pixel_weight[0], depth_order[0], dest, block_depth,
    )
    width = PIECES * FEAT
    message, alphas, clears, weights, prim, blended, front, behind, start = call(
        render_first,
        [((OWNERS, 1, width), F32)]
        + [((rows, PIX), F32)] * 3
        + [((FEAT, rows), F32), ((slots, 3 * PIX), F32)]
        + [((slots, slots), BF16)] * 2
        + [((1, PIX), F32)],
        over_tiles(message), aux,
    )
    part_shape = ((views, GAUSS // PIX * FEAT + ROWS, PIX), F32)
    gather = functools.partial(collect, views)
    gather.__name__ = "collect"
    (part,) = call(gather, [part_shape], over_tiles(message), select, proj)
    message, product, near, wide, sums = call(
        step_first,
        [
            ((OWNERS, 1, width), F32),
            ((PARAMS, GAUSS), F32),
            ((PARAMS, GAUSS), F32),
            ((PIX, 2 * views * FEAT), BF16),
            ((1, PIX), F32),
        ],
        over_views(part), right_side, damping, proj, select, start,
    )
    (message,) = call(
        render_again,
        [((OWNERS, 1, width + PIX), F32)],
        over_tiles(message), sums, aux, alphas, clears, weights, prim, blended, front, behind,
    )
    gather = functools.partial(collect_last, views)
    gather.__name__ = "collect_last"
    last_shape = ((views, GAUSS // PIX * FEAT + 1, 1, PIX), F32)
    (part,) = call(gather, [last_shape], over_tiles(message), select)
    return tuple(
        finish(over_views(part), right_side, damping, product, near, wide, start)
    )


def solution(mesh):
    in_specs = (
        P(None, "tiles"),
        P(None, "tiles"),
        P(None, "tiles"),
        P("views", None, None),
        P("views", "tiles", None, None),
        P("views", "tiles", None),
        P("views", "tiles", None),
        P("views", "tiles", None),
        P("views", "tiles"),
    )
    out_specs = (P(None, "tiles"), P(None, "tiles"))
    return jax.shard_map(body, mesh=mesh, in_specs=in_specs, out_specs=out_specs, check_vma=False)
```

```python
import functools

import jax
import jax.numpy as jnp
from jax import lax
from jax.experimental import pallas as pl
from jax.experimental.pallas import tpu as pltpu
from jax.sharding import PartitionSpec as P

OFFSET = 6.0
PARAMS = 59
FEAT = 16
ROWS = 8
CAP = 2
PIECES = CAP * ROWS
OWNERS = 64
GAUSS = 512
PIX = 128
F32 = jnp.float32
BF16 = jnp.bfloat16

NN = (((1,), (0,)), ((), ()))
NT = (((1,), (1,)), ((), ()))
TN = (((0,), (0,)), ((), ()))


def iota(shape, axis):
    return lax.broadcasted_iota(jnp.int32, shape, axis)


def mm(a, b, dims=NN):
    return lax.dot_general(a, b, dims, preferred_element_type=F32)


def split(x):
    high = x.astype(BF16)
    low = (x - high.astype(F32)).astype(BF16)
    return high, low


def mm_short(a, b):
    ah, al = split(a)
    bh, bl = split(b)
    return mm(jnp.concatenate([ah, al, ah], axis=0), jnp.concatenate([bh, bh, bl], axis=0), TN)


def project(proj, vectors):
    tall = jnp.concatenate([vectors, jnp.zeros((PIX // 2 - PARAMS, vectors.shape[1]), F32)], axis=0)
    ph, pl_ = split(proj)
    th, tl = split(tall)
    return mm(jnp.concatenate([ph, pl_, ph], axis=1), jnp.concatenate([th, th, tl], axis=0))


def total(x):
    return jnp.sum(jnp.sum(x, axis=1, keepdims=True), axis=0, keepdims=True)


def lanes(values, rows):
    lane = iota((rows, PIX), 1)
    out = jnp.zeros((rows, PIX), F32)
    for i, value in enumerate(values):
        out = jnp.where(lane == i, value, out)
    return out


def to_message(feats, select):
    stacked = jnp.concatenate(feats, axis=0)
    fields = [slice(i, i + FEAT) for i in range(0, stacked.shape[0], FEAT)]
    rows = stacked.shape[0]
    both = mm(jnp.concatenate(split(stacked), axis=0), select, NT)
    slots = both[:rows] + both[rows:]
    return jnp.concatenate([by_owner(slots[field]) for field in fields], axis=1)


def by_owner(slots):
    pieces = [slots[:, i * OWNERS : (i + 1) * OWNERS] for i in range(PIECES)]
    return jnp.concatenate(pieces, axis=0).T


def by_column(message, width):
    turned = message.T
    return jnp.concatenate([turned[i * width : (i + 1) * width] for i in range(PIECES)], axis=1)


def choose(order, dest):
    blocks = dest.shape[1]
    mine = iota((OWNERS, blocks), 0) == dest
    block = iota((OWNERS, blocks), 1).astype(F32)
    first = jnp.min(jnp.where(mine, block, float(blocks)), axis=1, keepdims=True)
    last = jnp.max(jnp.where(mine, block, -1.0), axis=1, keepdims=True)
    owns = [
        jnp.where(block == first, 1.0, 0.0),
        jnp.where((block == last) & (last > first), 1.0, 0.0),
    ]
    own_all = jnp.concatenate(owns, axis=0).astype(BF16)
    here = iota((blocks, GAUSS), 1) // ROWS == iota((blocks, GAUSS), 0)
    number = jnp.where(here, order + 1, 0)
    parts = jnp.concatenate(
        [(number >> 4).astype(F32), (number & 15).astype(F32)], axis=0
    ).astype(BF16)
    pick = jnp.where(iota((GAUSS, PIX), 0) % ROWS == iota((GAUSS, PIX), 1), 1.0, 0.0).astype(BF16)
    table = mm(parts, pick).astype(BF16)
    ids = mm(own_all, table[:blocks]) * 16.0 + mm(own_all, table[blocks:])
    return owns, ids


def chosen_rows(ids):
    columns = (iota((OWNERS, GAUSS), 1) + 1).astype(F32)
    rows = []
    for s in range(CAP):
        for r in range(ROWS):
            chosen = ids[s * OWNERS : (s + 1) * OWNERS, r : r + 1] == columns
            rows.append(jnp.where(chosen, 1.0, 0.0).astype(BF16))
    return jnp.concatenate(rows, axis=0)


def begin_kernel(
    point_hbm, right_hbm, damp_hbm, proj_hbm, basis_hbm, weight_hbm, order_hbm, dest_hbm, depth_hbm,
    message_ref, select_ref, aux_ref, proj_ref,
    point, right, damp, proj, basis, weight, order, dest, depth, sems,
):
    pairs = [
        (order_hbm, order), (dest_hbm, dest), (depth_hbm, depth), (proj_hbm, proj),
        (point_hbm, point), (right_hbm, right), (damp_hbm, damp), (basis_hbm, basis), (weight_hbm, weight),
    ]
    copies = [pltpu.make_async_copy(a, b, sems.at[i]) for i, (a, b) in enumerate(pairs)]
    for copy in copies:
        copy.start()
    for copy in copies[:3]:
        copy.wait()
    owns, ids = choose(order[...], dest[...])
    depth_f = depth[...].astype(F32) + 1.0
    marks = [jnp.sum(own * depth_f, axis=1, keepdims=True) for own in owns]
    for copy in copies[3:7]:
        copy.wait()
    right_now = right[...]
    padded = jnp.concatenate([proj[...], jnp.zeros((FEAT, PIX - PARAMS), F32)], axis=1)
    proj_ref[...] = padded
    feats = project(padded[:, : PIX // 2], jnp.concatenate([point[...], right_now], axis=1))
    select = chosen_rows(ids)
    select_ref[...] = select
    message = to_message([feats[:, :GAUSS], feats[:, GAUSS:]], select)
    squared = right_now * right_now
    tail = lanes(marks + [total(squared), total(damp[...] * squared)], OWNERS)
    message_ref[:, 0, :] = jnp.concatenate([message, tail], axis=1)
    for copy in copies[7:]:
        copy.wait()
    first = jnp.where(iota((4, PIX), 0) == 0, 1.0, 0.0)
    last = jnp.broadcast_to(weight[...], (8, PIX))
    aux_ref[...] = jnp.concatenate([first, basis[:, 0, :], last], axis=0)


def begin(*args):
    rows = PIECES * OWNERS
    return pl.pallas_call(
        begin_kernel,
        out_shape=[
            jax.ShapeDtypeStruct((OWNERS, 1, PIECES * 2 * FEAT + PIX), F32),
            jax.ShapeDtypeStruct((rows, GAUSS), BF16),
            jax.ShapeDtypeStruct((FEAT + 8, PIX), F32),
            jax.ShapeDtypeStruct((FEAT, PIX), F32),
        ],
        in_specs=[pl.BlockSpec(memory_space=pltpu.HBM)] * len(args),
        out_specs=[pl.BlockSpec(memory_space=pltpu.VMEM)] * 4,
        scratch_shapes=[pltpu.VMEM(x.shape, x.dtype) for x in args]
        + [pltpu.SemaphoreType.DMA((len(args),))],
        compiler_params=pltpu.CompilerParams(vmem_limit_bytes=40 * 1024 * 1024),
        name="begin",
    )(*[pltpu.with_memory_space_constraint(x, pltpu.HBM) for x in args])


def order_masks(marks):
    side = CAP * OWNERS
    by_row = jnp.broadcast_to(marks, (side, side))
    diagonal = iota((side, side), 0) == iota((side, side), 1)
    by_lane = jnp.sum(jnp.where(diagonal, by_row, 0.0), axis=0, keepdims=True)
    front = jnp.where((by_lane < by_row) & (by_lane > 0.0), 1.0, 0.0)
    behind = jnp.where((by_row < by_lane) & (by_row > 0.0), 1.0, 0.0)
    return front.astype(BF16), behind.astype(BF16)


def ordered_sum(mask, value):
    high, low = split(value)
    return mm(jnp.concatenate([mask, mask], axis=1), jnp.concatenate([high, low], axis=0))


def image_change(columns, both):
    high, low = split(columns)
    bh, bl = split(both)
    main = mm(jnp.concatenate([high, low], axis=0), bh)
    rest = mm(high, bl)
    change = (
        main[FEAT : 2 * FEAT, :PIX]
        + main[3 * FEAT :, :PIX]
        + rest[FEAT:, :PIX]
        + main[:FEAT, PIX:]
        + main[2 * FEAT : 3 * FEAT, PIX:]
        + rest[:FEAT, PIX:]
    )
    return colours_only(change)


def change_of(columns, values):
    high, low = split(columns)
    vh, vl = split(values)
    main = mm(jnp.concatenate([high, low], axis=0), vh)
    return main[:FEAT] + main[FEAT:] + mm(high, vl)


def colours_only(change):
    row = iota((FEAT, PIX), 0)
    return jnp.where((row >= 1) & (row < 4), change, 0.0)


def pull_back(prim_cols, basis, colour, alphas, clears, weights, blended, behind):
    shade = mm_short(prim_cols, colour)
    pulls = [weights[i] * shade[i * OWNERS : (i + 1) * OWNERS] for i in range(PIECES)]
    sums = sum(colour[1 + c : 2 + c] * blended[:, c * PIX : (c + 1) * PIX] for c in range(3))
    through = ordered_sum(behind, sums)
    logits = [None] * PIECES
    for s in range(CAP):
        acc = through[s * OWNERS : (s + 1) * OWNERS]
        for r in reversed(range(ROWS)):
            i = s * ROWS + r
            logits[i] = clears[i] * pulls[i] - alphas[i] * acc
            acc = acc + pulls[i]
    def over_pixels(first, second):
        high, low = split(second)
        fh, fl = split(first)
        main = mm(jnp.concatenate([fh, fl], axis=0), high, NT)
        return main[:FEAT] + main[FEAT:] + mm(fh, low, NT)

    early = over_pixels(colour, jnp.concatenate(weights, axis=0))
    return by_owner(early + over_pixels(basis, jnp.concatenate(logits, axis=0)))


def slope_terms(tangents, alphas, clears):
    slopes = []
    sums = []
    for s in range(CAP):
        acc = jnp.zeros((OWNERS, PIX), F32)
        for r in range(ROWS):
            i = s * ROWS + r
            slopes.append(clears[i] * tangents[i] + acc)
            acc = acc - alphas[i] * tangents[i]
        sums.append(acc)
    return slopes, jnp.concatenate(sums, axis=0)


def render_first(message, aux):
    width = PIECES * FEAT
    columns = jnp.concatenate(
        [by_column(message[:, :width], FEAT), by_column(message[:, width : 2 * width], FEAT)], axis=0
    )
    tail = message[:, 2 * width :]
    basis, pixel_weight = aux[:FEAT], aux[FEAT : FEAT + 1]
    both = jnp.zeros((FEAT, PIX), F32)
    wide = jnp.concatenate(
        [jnp.concatenate([basis, both], axis=1), jnp.concatenate([both, basis], axis=1)], axis=0
    )
    logits_tangents = mm_short(columns, wide)
    front, behind = order_masks(jnp.concatenate([tail[:, 0:1], tail[:, 1:2]], axis=0))
    alphas, clears, plain, tangents, lengths = [], [], [], [], []
    for s in range(CAP):
        open_now = None
        length = None
        for r in range(ROWS):
            i = s * ROWS + r
            block = logits_tangents[i * OWNERS : (i + 1) * OWNERS]
            z = block[:, :PIX] - OFFSET
            tangents.append(block[:, PIX:])
            small = jnp.exp(-jnp.abs(z))
            grown = 1.0 + small
            part = 1.0 / grown
            rest = small * part
            alpha = jnp.where(z >= 0.0, part, rest)
            clear = jnp.where(z >= 0.0, rest, part)
            log_clear = -(jnp.maximum(z, 0.0) + jnp.log(grown))
            alphas.append(alpha)
            clears.append(clear)
            plain.append(alpha if open_now is None else alpha * open_now)
            open_now = clear if open_now is None else open_now * clear
            length = log_clear if length is None else length + log_clear
        lengths.append(length)
    ahead = jnp.exp(ordered_sum(front, jnp.concatenate(lengths, axis=0)))
    weights = [
        plain[i] * ahead[(i // ROWS) * OWNERS : (i // ROWS + 1) * OWNERS] for i in range(PIECES)
    ]
    slopes, sums = slope_terms(tangents, alphas, clears)
    ahead_tangent = ordered_sum(front, sums)
    slopes = [
        weights[i]
        * (slopes[i] + ahead_tangent[(i // ROWS) * OWNERS : (i // ROWS + 1) * OWNERS])
        for i in range(PIECES)
    ]
    prim_cols = columns[:FEAT]
    row, lane = iota((FEAT, 3 * PIX), 0), iota((FEAT, 3 * PIX), 1)
    colours = mm(
        jnp.concatenate(split(prim_cols), axis=0),
        jnp.concatenate([jnp.where(row == lane // PIX + 1, 1.0, 0.0).astype(BF16)] * 2, axis=0),
        TN,
    )
    blended = []
    for c in range(3):
        shades = pieces_of(colours[:, c * PIX : (c + 1) * PIX])
        blended.append(
            jnp.concatenate(
                [
                    sum(weights[i] * shades[i] for i in range(s * ROWS, (s + 1) * ROWS))
                    for s in range(CAP)
                ],
                axis=0,
            )
        )
    blended = jnp.concatenate(blended, axis=1)
    change = image_change(
        columns,
        jnp.concatenate(
            [jnp.concatenate(weights, axis=0), jnp.concatenate(slopes, axis=0)], axis=1
        ),
    )
    colour = change * pixel_weight
    back = pull_back(prim_cols, basis, colour, alphas, clears, weights, blended, behind)
    return (
        back,
        jnp.concatenate(alphas, axis=0),
        jnp.concatenate(clears, axis=0),
        jnp.concatenate(weights, axis=0),
        prim_cols,
        blended,
        front,
        behind,
        jnp.sum(tail, axis=0, keepdims=True),
    )


def pieces_of(array):
    return [array[i * OWNERS : (i + 1) * OWNERS] for i in range(PIECES)]


def render_again(
    message, own_sums, aux, alphas, clears, weights, prim_cols, blended, front, behind
):
    columns = by_column(message, FEAT)
    basis, pixel_weight = aux[:FEAT], aux[FEAT : FEAT + 1]
    tangents = pieces_of(mm_short(columns, basis))
    alphas, clears, weight_list = pieces_of(alphas), pieces_of(clears), pieces_of(weights)
    slopes, sums = slope_terms(tangents, alphas, clears)
    ahead_tangent = ordered_sum(front, sums)
    slopes = [
        weight_list[i]
        * (slopes[i] + ahead_tangent[(i // ROWS) * OWNERS : (i // ROWS + 1) * OWNERS])
        for i in range(PIECES)
    ]
    change = colours_only(
        change_of(columns, weights) + change_of(prim_cols, jnp.concatenate(slopes, axis=0))
    )
    colour = change * pixel_weight
    back = pull_back(prim_cols, basis, colour, alphas, clears, weight_list, blended, behind)
    tail = jnp.where(iota((1, PIX), 1) == 0, total(colour * change), own_sums)
    return jnp.concatenate([back, jnp.broadcast_to(tail, (OWNERS, PIX))], axis=1)


def gathered_parts(message, select):
    columns = by_column(message[:, : PIECES * FEAT], FEAT)
    high, low = split(columns)
    wide = mm(jnp.concatenate([high, low], axis=0), select)
    gathered = wide[:FEAT] + wide[FEAT:]
    return [gathered[:, j : j + PIX] for j in range(0, GAUSS, PIX)]


def collect(views, message, select, proj):
    parts = gathered_parts(message, select)
    turned = jnp.concatenate([proj[:ROWS, : PIX // 2], proj[ROWS:, : PIX // 2]], axis=1)
    part = jnp.concatenate(parts + [turned], axis=0)
    return jnp.broadcast_to(part[None], (views,) + part.shape)


def collect_last(message, select):
    parts = gathered_parts(message, select)
    tail = jnp.sum(message[:, PIECES * FEAT :], axis=0, keepdims=True)
    return jnp.concatenate(parts + [tail], axis=0)


def turned_pair(message):
    views = message.shape[0]
    last = message[:, GAUSS // PIX * FEAT :].reshape(views * ROWS, PIX)
    turned = jnp.concatenate([last[:, : PIX // 2], last[:, PIX // 2 :]], axis=0).T
    th, tl = split(turned)
    wide = jnp.concatenate(
        [
            jnp.concatenate([th, th], axis=1),
            jnp.concatenate([tl, jnp.zeros(tl.shape, BF16)], axis=1),
        ],
        axis=0,
    )
    return wide


def product_of(message, wide):
    views = message.shape[0]
    gathered = jnp.concatenate(
        [
            jnp.concatenate(
                [
                    message[:, j * FEAT + h : j * FEAT + h + ROWS].reshape(views * ROWS, PIX)
                    for j in range(GAUSS // PIX)
                ],
                axis=1,
            )
            for h in (0, ROWS)
        ],
        axis=0,
    )
    product = mm(wide, jnp.concatenate(split(gathered), axis=0))
    half = PIX // 2
    return (product[:half] + product[half:])[:PARAMS]


def first_guess(sums):
    square, damped = sums[:, 2:3], sums[:, 3:4]
    return jnp.where(damped > 0.0, square / damped, 1.0)


def step_first(message, right, damp, proj, select, start):
    wide = turned_pair(message)
    back = product_of(message, wide)
    product = back + damp * right
    near = right - first_guess(start) * product
    out = to_message([project(proj[:, : PIX // 2], near)], select)
    sums = [
        jnp.zeros((1, 1), F32),
        total(right * back),
        total(near * near),
        total(near * right),
        total(near * product),
        total(damp * near * near),
    ]
    return out, product, near, wide, lanes(sums, 1)


def finish_kernel(
    message_ref, right_ref, damp_ref, product_ref, near_ref, wide, start_ref,
    solution_hbm, final_hbm, solution, final, sems,
):
    message = message_ref[:, :, 0, :]
    product = product_of(message, wide[...])
    energy = jnp.sum(message[:, GAUSS // PIX * FEAT], axis=0, keepdims=True)[:, 0:1]
    start = start_ref[...]
    square, damped = start[:, 2:3], start[:, 3:4]
    sums = message[0, GAUSS // PIX * FEAT :]
    seen, nn, nb, ny, ndn = [sums[:, i : i + 1] for i in range(1, 6)]
    cross = seen + damped
    step, share, rest = square / cross, damped / cross, seen / cross
    square_now = share * share * nn + 2.0 * share * rest * nb + rest * rest * square
    ratio = square_now / square
    part = rest + ratio
    bent = share * share * (energy + ndn) + 2.0 * share * part * ny + part * part * cross
    step_now = square_now / bent
    right, before, near = right_ref[...], product_ref[...], near_ref[...]
    residual = share * near + rest * right
    solution[...] = step * right + step_now * (residual + ratio * right)
    first = pltpu.make_async_copy(solution, solution_hbm, sems.at[0])
    first.start()
    final[...] = residual - step_now * (
        share * (product + damp_ref[...] * near) + part * before
    )
    second = pltpu.make_async_copy(final, final_hbm, sems.at[1])
    second.start()
    first.wait()
    second.wait()


def finish(*args):
    shape = (PARAMS, GAUSS)
    return pl.pallas_call(
        finish_kernel,
        out_shape=[jax.ShapeDtypeStruct(shape, F32)] * 2,
        in_specs=[pl.BlockSpec(memory_space=pltpu.VMEM)] * len(args),
        out_specs=[pl.BlockSpec(memory_space=pltpu.HBM)] * 2,
        scratch_shapes=[pltpu.VMEM(shape, F32)] * 2 + [pltpu.SemaphoreType.DMA((2,))],
        compiler_params=pltpu.CompilerParams(vmem_limit_bytes=40 * 1024 * 1024),
        name="finish",
    )(*args)


def call(function, outs, *args):
    def kernel(*refs):
        results = function(*[ref[:, 0, :] if len(ref.shape) == 3 and ref.shape[1] == 1 else ref[...] for ref in refs[: len(args)]])
        if len(outs) == 1:
            results = (results,) if not isinstance(results, tuple) else results
        for ref, result in zip(refs[len(args) :], results):
            if result.ndim < len(ref.shape):
                ref[..., 0, :] = result
            else:
                ref[...] = result

    result = pl.pallas_call(
        kernel,
        out_shape=[jax.ShapeDtypeStruct(shape, dtype) for shape, dtype in outs],
        in_specs=[pl.BlockSpec(memory_space=pltpu.VMEM)] * len(args),
        out_specs=[pl.BlockSpec(memory_space=pltpu.VMEM)] * len(outs),
        compiler_params=pltpu.CompilerParams(vmem_limit_bytes=40 * 1024 * 1024),
        name=function.__name__,
    )(*args)
    return result


def body(
    linear_point,
    right_side,
    damping,
    projection,
    pixel_basis,
    pixel_weight,
    depth_order,
    tile_dest,
    block_depth,
):
    dest = tile_dest.reshape(1, -1)
    views = lax.axis_size("views")
    rows = PIECES * OWNERS
    slots = CAP * OWNERS

    def over_tiles(message):
        return lax.all_to_all(message, "tiles", split_axis=0, concat_axis=0, tiled=True)

    def over_views(part):
        return lax.all_to_all(part, "views", split_axis=0, concat_axis=0, tiled=True)

    message, select, aux, proj = begin(
        linear_point, right_side, damping, jnp.swapaxes(projection, 1, 2)[0],
        pixel_basis.reshape(FEAT - 4, 1, PIX), pixel_weight[0], depth_order[0], dest, block_depth,
    )
    width = PIECES * FEAT
    message, alphas, clears, weights, prim, blended, front, behind, start = call(
        render_first,
        [((OWNERS, 1, width), F32)]
        + [((rows, PIX), F32)] * 3
        + [((FEAT, rows), F32), ((slots, 3 * PIX), F32)]
        + [((slots, slots), BF16)] * 2
        + [((1, PIX), F32)],
        over_tiles(message), aux,
    )
    part_shape = ((views, GAUSS // PIX * FEAT + ROWS, PIX), F32)
    gather = functools.partial(collect, views)
    gather.__name__ = "collect"
    (part,) = call(gather, [part_shape], over_tiles(message), select, proj)
    message, product, near, wide, sums = call(
        step_first,
        [
            ((OWNERS, 1, width), F32),
            ((PARAMS, GAUSS), F32),
            ((PARAMS, GAUSS), F32),
            ((PIX, 2 * views * FEAT), BF16),
            ((1, PIX), F32),
        ],
        over_views(part), right_side, damping, proj, select, start,
    )
    (message,) = call(
        render_again,
        [((OWNERS, 1, width + PIX), F32)],
        over_tiles(message), sums, aux, alphas, clears, weights, prim, blended, front, behind,
    )
    last_shape = ((GAUSS // PIX * FEAT + 1, PIX), F32)
    (part,) = call(collect_last, [last_shape], over_tiles(message), select)
    part = jnp.broadcast_to(part[None, :, None], (views, part.shape[0], 1, PIX))
    return tuple(
        finish(over_views(part), right_side, damping, product, near, wide, start)
    )


def solution(mesh):
    in_specs = (
        P(None, "tiles"),
        P(None, "tiles"),
        P(None, "tiles"),
        P("views", None, None),
        P("views", "tiles", None, None),
        P("views", "tiles", None),
        P("views", "tiles", None),
        P("views", "tiles", None),
        P("views", "tiles"),
    )
    out_specs = (P(None, "tiles"), P(None, "tiles"))
    return jax.shard_map(body, mesh=mesh, in_specs=in_specs, out_specs=out_specs, check_vma=False)
```
